32 devices in a mesh: dp: 8 (over z, x), rep: 4 (over y, core).
Axes of the slice: x: 2, y: 2, z: 4, core: 2. Of those that a mesh axis runs over, the one named last changes fastest.
Arguments:
- tokens_in: bfloat16 [8192, 768], P(('dp', 'rep')), may hold values from -7 to 7
- boxes: int32 [2, 8192], P(None, ('dp', 'rep')), may hold values from 0 to 999
- page_lengths: int32 [32, 8], P(('dp', 'rep')), may hold values from 1 to 64, 256 in all within a row
- cotangent: bfloat16 [8192, 768], P(('dp', 'rep')), may hold values from -6 to 6
- w_qkv: bfloat16 [768, 2304], P(('dp', 'rep')), may hold values from -0.21875 to 0.21875
- w_out: bfloat16 [768, 768], P(('dp', 'rep')), may hold values from -0.875 to 0.875
- w_pos: bfloat16 [768, 768], P(('dp', 'rep')), may hold values from -0.21875 to 0.21875
- gain_attn: bfloat16 [768], P(('dp', 'rep')), may hold values from 0.5 to 1.5
- bias_attn: bfloat16 [768], P(('dp', 'rep')), may hold values from -1.1953125 to 1.1953125
- w_up: bfloat16 [768, 3072], P(('dp', 'rep')), may hold values from -0.21875 to 0.21875
- w_down: bfloat16 [3072, 768], P(('dp', 'rep')), may hold values from -0.109375 to 0.109375
- gain_ffn: bfloat16 [768], P(('dp', 'rep')), may hold values from 0.5 to 1.5
- bias_ffn: bfloat16 [768], P(('dp', 'rep')), may hold values from -1.1953125 to 1.1953125
Outputs:
- output: bfloat16 [8192, 768], P(('dp', 'rep'))
- grad_tokens: float32 [8192, 768], P(('dp', 'rep'))
- rms: float32 [3], replicated
- grad_w_qkv: float32 [768, 2304], P(('dp', 'rep'))
- grad_w_out: float32 [768, 768], P(('dp', 'rep'))
- grad_w_pos: float32 [768, 768], P(('dp', 'rep'))
- grad_gain_attn: float32 [768], P(('dp', 'rep'))
- grad_bias_attn: float32 [768], P(('dp', 'rep'))
- grad_w_up: float32 [768, 3072], P(('dp', 'rep'))
- grad_w_down: float32 [3072, 768], P(('dp', 'rep'))
- grad_gain_ffn: float32 [768], P(('dp', 'rep'))
- grad_bias_ffn: float32 [768], P(('dp', 'rep'))
The draws below stay inside these ranges and needn't reach their ends.
All inputs are finite; a program needn't handle non-finite values.
Results may differ from the reference program's by a relative error of at most 0.018.
Values may be sent and summed in bfloat16 or wider, within the bound.
No kernel may reach another device: no remote copies, remote signals or barrier semaphores. Data moves between devices by JAX's collectives and lax.ppermute only.
A program may use at most 192 MiB of HBM per device.

```python
import math
import jax
import jax.numpy as jnp
import numpy as np
from jax import lax

D = 768
HEADS = 12
FF = 3072
FREQS = 192
ROW_LEN = 256
PAGES = 8
HEAD_DIM = 64
MAX_PAGE = 64
ROWS = 32
TOKENS = 8192


def draw_tokens_in(key, part):
    key = jax.random.fold_in(key, 11)
    first = jax.random.fold_in(key, 0)
    rise = 1.0 + 0.75 * jnp.arange(TOKENS, dtype=jnp.float32)[:, None] / (TOKENS - 1)
    base = jnp.clip(jax.random.normal(first, (TOKENS, D), jnp.float32), -4.0, 4.0)
    return (base * rise).astype(jnp.bfloat16)


def touch_ends(result, stream_key, low, largest):
    extent = result.shape
    spot = [jax.random.randint(jax.random.fold_in(stream_key, axis), (), 0, extent[axis]) for axis in range(len(extent))]
    result = result.at[tuple(spot)].set(low)
    longest = extent.index(max(extent))
    spot[longest] = (spot[longest] + 1) % extent[longest]
    return result.at[tuple(spot)].set(largest)


def raised(values, key, source, target, shards_of, factor):
    def block_of(dim):
        return (jnp.arange(values.shape[dim]) // (values.shape[dim] // shards_of)).reshape((-1,) + (1,) * (values.ndim - 1 - dim))

    near = jax.random.permutation(key, shards_of)[block_of(target)]
    far = (block_of(target) + shards_of // 2) % shards_of
    return jnp.where((block_of(source) == near) | (block_of(source) == far), factor * values, values)


def levels(own_key, shape, pieces, low, top_value):
    level, own = 1.0, jax.random.fold_in(own_key, 6)
    for dim, shards_of in pieces:
        steps = jnp.exp(jax.random.uniform(jax.random.fold_in(own, dim), (shards_of,), jnp.float32, low / len(pieces), top_value / len(pieces)))
        level = level * jnp.repeat(steps, shape[dim] // shards_of).reshape([-1 if axis == dim else 1 for axis in range(len(shape))])
    return level


def profile(number_of, total, most, lean):
    portions = [(1 << 20) // math.isqrt(rank ** lean) + 1 for rank in range(2, number_of + 1)]
    surplus, given = total - most - (number_of - 1), [1] * (number_of - 1)
    while surplus > 0:
        candidates = [i for i in range(number_of - 1) if given[i] < most]
        whole, budget = sum([portions[i] for i in candidates]), surplus
        for i in candidates:
            more = min(most - given[i], max(1, budget * portions[i] // whole), surplus)
            given[i] = given[i] + more
            surplus = surplus - more
    return np.array([most] + given)


def uneven_parts(key, number_of, total, reach, slope):
    if number_of == 2:
        one = jax.random.randint(key, (), max(1, total - reach), min(reach, total - 1) + 1)
        return jnp.stack([one, total - one])
    tallies = jnp.asarray(profile(number_of, total, reach, slope), jnp.int32)
    couples = (number_of - 1) // 2
    source_of, taker = tallies[1:1 + 2 * couples:2], tallies[2:2 + 2 * couples:2]
    room = jnp.minimum(source_of - 1, reach - taker)
    passed = jax.random.randint(jax.random.fold_in(key, 1), (couples,), 0, 1 << 20) % (room + 1)
    tallies = tallies.at[1:1 + 2 * couples:2].set(source_of - passed).at[2:2 + 2 * couples:2].set(taker + passed)
    return tallies[jax.random.permutation(jax.random.fold_in(key, 2), number_of)]


def scatter_about(stream_key, shape, width, limit, pieces=(), held_as=jnp.bfloat16):
    level = levels(stream_key, shape, pieces, -0.22, 0.18) if pieces else 1.0
    entries = jax.random.normal(stream_key, shape, jnp.float32) * width * level
    return jnp.minimum(jnp.maximum(entries, -limit), limit).astype(held_as)


def gaussian_with(rng, extent, width, most, cuts, heavy, kind=jnp.bfloat16):
    drawn = width * jax.random.normal(rng, extent, jnp.float32)
    if cuts:
        drawn = drawn * levels(rng, extent, cuts, -0.22, 0.18)
    return jnp.clip(raised(drawn, jax.random.fold_in(rng, 3), *heavy), -most, most).astype(kind)


def setup_inputs(seed: int = 0) -> dict:
    splits = jax.random.split(jax.random.key(seed), 14)
    tokens_in = draw_tokens_in(jax.random.fold_in(splits[13], 71), 0)
    boxes = touch_ends(jax.random.randint(splits[1], (2, TOKENS), 0, 1000), jax.random.fold_in(splits[1], 1), 0, 999).astype(jnp.int32)
    page_lengths = jax.vmap(lambda own: uneven_parts(own, PAGES, ROW_LEN, MAX_PAGE, 2))(jax.random.split(splits[2], ROWS)).reshape((ROWS, PAGES)).astype(jnp.int32)
    cotangent = gaussian_with(splits[3], (TOKENS, D), 1.0, 6.0, ((0, 32),), (0, 1, 32, 2.75))
    w_qkv = scatter_about(splits[4], (D, 3 * D), D ** -0.5, 0.21875, ((0, 32),))
    w_out = scatter_about(splits[5], (D, D), (D // 16) ** -0.5, 0.875, ((0, 32),))
    w_pos = scatter_about(splits[6], (4 * FREQS, D), (4 * FREQS) ** -0.5, 0.21875, ((0, 32),))
    gain_attn = jnp.clip(1.0 + 0.1 * jax.random.normal(splits[7], (D,), jnp.float32), 0.5, 1.5).astype(jnp.bfloat16)
    bias_attn = scatter_about(splits[8], (D,), 0.3, 1.1953125, ((0, 32),))
    w_up = scatter_about(splits[9], (D, FF), D ** -0.5, 0.21875, ((0, 32),))
    w_down = scatter_about(splits[10], (FF, D), FF ** -0.5, 0.109375, ((0, 32),))
    gain_ffn = jnp.clip(1.0 + 0.1 * jax.random.normal(splits[11], (D,), jnp.float32), 0.5, 1.5).astype(jnp.bfloat16)
    bias_ffn = scatter_about(splits[12], (D,), 0.3, 1.1953125, ((0, 32),))
    return {"tokens_in": tokens_in, "boxes": boxes, "page_lengths": page_lengths, "cotangent": cotangent, "w_qkv": w_qkv, "w_out": w_out, "w_pos": w_pos, "gain_attn": gain_attn, "bias_attn": bias_attn, "w_up": w_up, "w_down": w_down, "gain_ffn": gain_ffn, "bias_ffn": bias_ffn}


@jax.custom_vjp
def low(v):
    return lax.optimization_barrier(v.astype(jnp.bfloat16)).astype(jnp.float32)

@jax.custom_vjp
def low_back(v):
    return v

def low_keep(v):
    return (low(v), None)

def low_pass(kept, grad):
    return (grad,)

def back_keep(v):
    return (v, None)

def back_low(kept, grad):
    return (low(grad),)
low.defvjp(low_keep, low_pass)
low_back.defvjp(back_keep, back_low)
epsilon = 1e-05

def sinusoid_parts(boxes, freq_count):
    steps_f = jnp.arange(freq_count, dtype=jnp.float32)
    rates = jnp.exp(steps_f * (-math.log(10000.0) / freq_count))
    angles = boxes.astype(jnp.float32)[:, :, None] * rates[None, None, :]
    return (jnp.sin(angles), jnp.cos(angles))

def token_features(sines, cosines):
    stacked = jnp.stack([sines, cosines], axis=1)
    tok_count = sines.shape[1]
    return jnp.transpose(stacked, (2, 0, 1, 3)).reshape(tok_count, -1)

def rotate(coeff, sin_tok, cos_tok):
    tok_count, head_count, pos_width = coeff.shape
    parts = coeff.reshape(tok_count, head_count, 2, 2, pos_width // 4)
    along_sin = parts[:, :, :, 0, :]
    along_cos = parts[:, :, :, 1, :]
    first = along_cos * sin_tok - along_sin * cos_tok
    second = along_sin * sin_tok + along_cos * cos_tok
    return jnp.stack([first, second], axis=3).reshape(tok_count, head_count, pos_width)

def segment_ids(page_lengths, row_len):
    ends = jnp.cumsum(page_lengths, axis=1)
    places = jnp.arange(row_len, dtype=jnp.int32)
    return lax.optimization_barrier(jnp.sum((places[None, :, None] >= ends[:, None, :]).astype(jnp.int32), axis=2))

def layer_norm(values, gain, bias):
    centered = values - lax.optimization_barrier(jnp.mean(values, axis=-1, keepdims=True))
    variance = lax.optimization_barrier(jnp.mean(centered * centered, axis=-1, keepdims=True))
    return centered * lax.rsqrt(variance + epsilon) * gain + bias

def row_forward(row_tokens, row_boxes, row_lengths, weights):
    w_qkv, w_out, w_pos, gain_attn, bias_attn, w_up, w_down, gain_ffn, bias_ffn = weights
    highest = lax.Precision.HIGHEST
    head_dim = D // HEADS
    sines, cosines = sinusoid_parts(row_boxes, FREQS)
    sin_tok = jnp.transpose(sines, (1, 0, 2))[:, None]
    cos_tok = jnp.transpose(cosines, (1, 0, 2))[:, None]
    feats = low(token_features(sines, cosines))
    segment = segment_ids(row_lengths[None], ROW_LEN)[0]
    qkv = low(low_back(jnp.dot(row_tokens, w_qkv, precision=highest)))
    qkv = qkv.reshape(ROW_LEN, 3, HEADS, head_dim)
    query = qkv[:, 0]
    key = qkv[:, 1]
    value = qkv[:, 2]
    pos_weights = w_pos.reshape(4 * FREQS, HEADS, head_dim)
    query_coeff = low_back(jnp.einsum('thd,phd->thp', query, pos_weights, precision=highest))
    key_coeff = low_back(jnp.einsum('thd,phd->thp', key, pos_weights, precision=highest))
    query_pos = low(rotate(query_coeff, sin_tok, cos_tok))
    key_pos = low(rotate(key_coeff, sin_tok, cos_tok))
    plain = jnp.einsum('ihd,jhd->hij', query, key, precision=highest)
    to_pos = jnp.einsum('ihp,jp->hij', query_pos, feats, precision=highest)
    from_pos = jnp.einsum('ip,jhp->hij', feats, key_pos, precision=highest)
    raw = low_back((plain + to_pos + from_pos) * HEAD_DIM ** (-0.5))
    same = segment[:, None] == segment[None, :]
    scores = jnp.where(same[None], raw, -1e+30)
    top = lax.optimization_barrier(jnp.max(scores, axis=-1, keepdims=True))
    expo = jnp.exp(scores - top)
    probs = low(expo / lax.optimization_barrier(jnp.sum(expo, axis=-1, keepdims=True)))
    mixed = jnp.einsum('hij,jhd->ihd', probs, value, precision=highest)
    context = low(low_back(mixed.reshape(ROW_LEN, D)))
    attn_out = low_back(jnp.dot(context, w_out, precision=highest))
    resid_sum = row_tokens + attn_out
    normed_one = layer_norm(resid_sum, gain_attn, bias_attn)
    pre_act = low_back(jnp.dot(low(normed_one), w_up, precision=highest))
    act = low(jax.nn.gelu(pre_act, approximate=False))
    ffn_out = low_back(jnp.dot(act, w_down, precision=highest))
    output = layer_norm(normed_one + ffn_out, gain_ffn, bias_ffn)
    sums = jnp.stack([jnp.sum(row_tokens * row_tokens), jnp.sum(attn_out * attn_out), jnp.sum(resid_sum * resid_sum)])
    return (output, sums)

def reference(tokens_in, boxes, page_lengths, cotangent, w_qkv, w_out, w_pos, gain_attn, bias_attn, w_up, w_down, gain_ffn, bias_ffn):
    box_rows = jnp.transpose(boxes.reshape(2, ROWS, ROW_LEN), (1, 0, 2))
    weights_f = tuple((item.astype(jnp.float32) for item in (w_qkv, w_out, w_pos, gain_attn, bias_attn, w_up, w_down, gain_ffn, bias_ffn)))

    def forward(tokens_f, *weights):

        def one_row(items):
            return row_forward(items[0], items[1], items[2], weights)
        outputs, sums = lax.map(jax.checkpoint(one_row), (tokens_f.reshape(ROWS, ROW_LEN, D), box_rows, page_lengths))
        rms_values = jnp.sqrt(lax.optimization_barrier(jnp.sum(sums, axis=0)) / (TOKENS * D))
        return (outputs.reshape(TOKENS, D), rms_values)
    output, pullback, rms_values = jax.vjp(forward, tokens_in.astype(jnp.float32), *weights_f, has_aux=True)
    grads = pullback(cotangent.astype(jnp.float32))
    return (output.astype(jnp.bfloat16), grads[0], rms_values, grads[1], grads[2], grads[3], grads[4], grads[5], grads[6], grads[7], grads[8], grads[9])
```

```python
from functools import partial
import math

import jax
import jax.numpy as jnp
from jax import lax
from jax.sharding import PartitionSpec as P

HEADS = 12
FREQS = 192


epsilon = 1e-05
masked_value = -1e30


def sinusoid_parts(boxes, freq_count):
    steps_f = jnp.arange(freq_count, dtype=jnp.float32)
    rates = jnp.exp(steps_f * (-math.log(10000.0) / freq_count))
    angles = boxes.astype(jnp.float32)[:, :, None] * rates[None, None, :]
    return (jnp.sin(angles), jnp.cos(angles))


def token_features(sines, cosines):
    stacked = jnp.stack([sines, cosines], axis=1)
    tok_count = sines.shape[1]
    return jnp.transpose(stacked, (2, 0, 1, 3)).reshape(tok_count, -1)


def rotate(coeff, sin_tok, cos_tok):
    tok_count, head_count, pos_width = coeff.shape
    parts = coeff.reshape(tok_count, head_count, 2, 2, pos_width // 4)
    along_sin = parts[:, :, :, 0, :]
    along_cos = parts[:, :, :, 1, :]
    first = along_cos * sin_tok - along_sin * cos_tok
    second = along_sin * sin_tok + along_cos * cos_tok
    return jnp.stack([first, second], axis=3).reshape(tok_count, head_count, pos_width)


def rotate_back(grads, sin_tok, cos_tok):
    tok_count, head_count, pos_width = grads.shape
    parts = grads.reshape(tok_count, head_count, 2, 2, pos_width // 4)
    first = parts[:, :, :, 0, :]
    second = parts[:, :, :, 1, :]
    grad_sin = second * sin_tok - first * cos_tok
    grad_cos = first * sin_tok + second * cos_tok
    return jnp.stack([grad_sin, grad_cos], axis=3).reshape(tok_count, head_count, pos_width)


def segment_ids(page_lengths, row_len):
    ends = jnp.cumsum(page_lengths, axis=1)
    places = jnp.arange(row_len, dtype=jnp.int32)
    return jnp.sum((places[None, :, None] >= ends[:, None, :]).astype(jnp.int32), axis=2)


def norm_forward(values, gain, bias):
    centered = values - jnp.mean(values, axis=-1, keepdims=True)
    inv_std = lax.rsqrt(jnp.mean(centered * centered, axis=-1, keepdims=True) + epsilon)
    normed_vals = centered * inv_std
    return (normed_vals * gain + bias, normed_vals, inv_std)


def norm_backward(grad, normed_vals, inv_std, gain):
    grad_normed = grad * gain
    centered_grad = grad_normed - jnp.mean(grad_normed, axis=-1, keepdims=True)
    grad_values = inv_std * (
        centered_grad - normed_vals * jnp.mean(grad_normed * normed_vals, axis=-1, keepdims=True)
    )
    return (grad_values, jnp.sum(grad * normed_vals, axis=0), jnp.sum(grad, axis=0))


def gelu_exact(values):
    return jax.nn.gelu(values, approximate=False)


def fetch_weights(w_qkv, w_out, w_pos, w_up, w_down, gain_attn, bias_attn, gain_ffn, bias_ffn):
    axes = ("dp", "rep")
    width = w_out.shape[1]
    first = jnp.concatenate([w_qkv, w_pos, w_out], axis=1)
    first = lax.all_gather(first, axes, axis=0, tiled=True)
    wide = lax.all_gather(w_up, axes, axis=0, tiled=True)
    deep = lax.all_gather(w_down, axes, axis=0, tiled=True)
    small = jnp.stack([gain_attn, bias_attn, gain_ffn, bias_ffn], axis=1)
    small = lax.all_gather(small, axes, axis=0, tiled=True)
    return (
        first[:, : 3 * width],
        first[:, 4 * width :],
        first[:, 3 * width : 4 * width],
        wide,
        deep,
        small[:, 0],
        small[:, 1],
        small[:, 2],
        small[:, 3],
    )


def row_scores(query, key, query_pos, key_pos, feats, segment, scale):
    plain = jnp.einsum("ihd,jhd->hij", query, key, preferred_element_type=jnp.float32)
    to_pos = jnp.einsum("ihp,jp->hij", query_pos, feats, preferred_element_type=jnp.float32)
    from_pos = jnp.einsum("ip,jhp->hij", feats, key_pos, preferred_element_type=jnp.float32)
    raw = (plain + to_pos + from_pos) * scale
    same = segment[:, None] == segment[None, :]
    return jnp.where(same[None], raw, masked_value)


def attend_forward(items, scale):
    query, key, value, query_pos, key_pos, feats, segment = items
    scores = row_scores(query, key, query_pos, key_pos, feats, segment, scale)
    top = jnp.max(scores, axis=-1, keepdims=True)
    expo = jnp.exp(scores - top)
    total = jnp.sum(expo, axis=-1, keepdims=True)
    probs = (expo / total).astype(jnp.bfloat16)
    mixed = jnp.einsum("hij,jhd->ihd", probs, value, preferred_element_type=jnp.float32)
    return (mixed, (top + jnp.log(total))[:, :, 0])


def attend_backward(items, scale):
    query, key, value, query_pos, key_pos, feats, segment, log_total, grad_mixed = items
    scores = row_scores(query, key, query_pos, key_pos, feats, segment, scale)
    probs = jnp.exp(scores - log_total[:, :, None])
    grad_value = jnp.einsum(
        "hij,ihd->jhd", probs.astype(jnp.bfloat16), grad_mixed, preferred_element_type=jnp.float32
    )
    grad_probs = jnp.einsum("ihd,jhd->hij", grad_mixed, value, preferred_element_type=jnp.float32)
    row_inner = jnp.sum(probs * grad_probs, axis=-1, keepdims=True)
    grad_scores = (probs * (grad_probs - row_inner)).astype(jnp.bfloat16)
    grad_query = (
        jnp.einsum("hij,jhd->ihd", grad_scores, key, preferred_element_type=jnp.float32) * scale
    )
    grad_key = (
        jnp.einsum("hij,ihd->jhd", grad_scores, query, preferred_element_type=jnp.float32) * scale
    )
    grad_query_pos = (
        jnp.einsum("hij,jp->ihp", grad_scores, feats, preferred_element_type=jnp.float32) * scale
    )
    grad_key_pos = (
        jnp.einsum("hij,ip->jhp", grad_scores, feats, preferred_element_type=jnp.float32) * scale
    )
    return (grad_query, grad_key, grad_value, grad_query_pos, grad_key_pos)


def body(
    tokens_in,
    boxes,
    page_lengths,
    cotangent,
    w_qkv,
    w_out,
    w_pos,
    gain_attn,
    bias_attn,
    w_up,
    w_down,
    gain_ffn,
    bias_ffn,
):
    tok_count, width = tokens_in.shape
    row_count = page_lengths.shape[0]
    row_len = tok_count // row_count
    head_dim = width // HEADS
    pos_width = 4 * FREQS
    scale = head_dim ** (-0.5)

    def by_rows(values):
        return values.reshape((row_count, row_len) + values.shape[1:])

    (
        full_qkv,
        full_out,
        full_pos,
        full_up,
        full_down,
        full_gain_attn,
        full_bias_attn,
        full_gain_ffn,
        full_bias_ffn,
    ) = fetch_weights(w_qkv, w_out, w_pos, w_up, w_down, gain_attn, bias_attn, gain_ffn, bias_ffn)
    sines, cosines = sinusoid_parts(boxes, FREQS)
    sin_tok = jnp.transpose(sines, (1, 0, 2))[:, None]
    cos_tok = jnp.transpose(cosines, (1, 0, 2))[:, None]
    feats = token_features(sines, cosines).astype(jnp.bfloat16)
    segments = segment_ids(page_lengths, row_len)
    qkv = jnp.dot(tokens_in, full_qkv, preferred_element_type=jnp.float32).astype(jnp.bfloat16)
    qkv = qkv.reshape(tok_count, 3, HEADS, head_dim)
    query = qkv[:, 0]
    key = qkv[:, 1]
    value = qkv[:, 2]
    pos_weights = full_pos.reshape(pos_width, HEADS, head_dim)
    query_coeff = jnp.einsum("thd,phd->thp", query, pos_weights, preferred_element_type=jnp.float32)
    key_coeff = jnp.einsum("thd,phd->thp", key, pos_weights, preferred_element_type=jnp.float32)
    query_pos = rotate(query_coeff, sin_tok, cos_tok).astype(jnp.bfloat16)
    key_pos = rotate(key_coeff, sin_tok, cos_tok).astype(jnp.bfloat16)
    row_items = (
        by_rows(query),
        by_rows(key),
        by_rows(value),
        by_rows(query_pos),
        by_rows(key_pos),
        by_rows(feats),
        segments,
    )
    mixed, log_total = lax.map(partial(attend_forward, scale=scale), row_items)
    context = mixed.reshape(tok_count, width).astype(jnp.bfloat16)
    attn_out = jnp.dot(context, full_out, preferred_element_type=jnp.float32)
    tokens_f = tokens_in.astype(jnp.float32)
    resid_sum = tokens_f + attn_out
    normed_one, normed_vals_one, inv_std_one = norm_forward(
        resid_sum, full_gain_attn.astype(jnp.float32), full_bias_attn.astype(jnp.float32)
    )
    normed_low = normed_one.astype(jnp.bfloat16)
    pre_act = jnp.dot(normed_low, full_up, preferred_element_type=jnp.float32)
    act_low = gelu_exact(pre_act).astype(jnp.bfloat16)
    ffn_out = jnp.dot(act_low, full_down, preferred_element_type=jnp.float32)
    output, normed_vals_two, inv_std_two = norm_forward(
        normed_one + ffn_out, full_gain_ffn.astype(jnp.float32), full_bias_ffn.astype(jnp.float32)
    )
    sum_tokens, sum_attn, sum_resid = lax.psum(
        (
            jnp.sum(tokens_f * tokens_f),
            jnp.sum(attn_out * attn_out),
            jnp.sum(resid_sum * resid_sum),
        ),
        ("dp", "rep"),
    )
    entry_count = tok_count * width * lax.axis_size("dp") * lax.axis_size("rep")
    rms_values = jnp.sqrt(jnp.stack([sum_tokens, sum_attn, sum_resid]) / entry_count)
    back_qkv, back_out, back_pos, back_up, back_down = full_qkv, full_out, full_pos, full_up, full_down
    back_gain_attn, back_gain_ffn = full_gain_attn, full_gain_ffn
    back_pos_heads = back_pos.reshape(pos_width, HEADS, head_dim)
    grad_resid_two, grad_gain_ffn, grad_bias_ffn = norm_backward(
        cotangent.astype(jnp.float32),
        normed_vals_two,
        inv_std_two,
        back_gain_ffn.astype(jnp.float32),
    )
    grad_ffn_low = grad_resid_two.astype(jnp.bfloat16)
    grad_w_down = jnp.einsum("tf,td->fd", act_low, grad_ffn_low, preferred_element_type=jnp.float32)
    grad_act = jnp.einsum("td,fd->tf", grad_ffn_low, back_down, preferred_element_type=jnp.float32)
    unused_value, gelu_pull = jax.vjp(gelu_exact, pre_act)
    grad_pre = gelu_pull(grad_act)[0].astype(jnp.bfloat16)
    grad_w_up = jnp.einsum("td,tf->df", normed_low, grad_pre, preferred_element_type=jnp.float32)
    grad_normed = grad_resid_two + jnp.einsum(
        "tf,df->td", grad_pre, back_up, preferred_element_type=jnp.float32
    )
    grad_resid_one, grad_gain_attn, grad_bias_attn = norm_backward(
        grad_normed, normed_vals_one, inv_std_one, back_gain_attn.astype(jnp.float32)
    )
    grad_attn_low = grad_resid_one.astype(jnp.bfloat16)
    grad_w_out = jnp.einsum("tc,td->cd", context, grad_attn_low, preferred_element_type=jnp.float32)
    grad_context = jnp.einsum(
        "td,cd->tc", grad_attn_low, back_out, preferred_element_type=jnp.float32
    ).astype(jnp.bfloat16)
    back_items = row_items + (log_total, by_rows(grad_context.reshape(tok_count, HEADS, head_dim)))
    grad_query, grad_key, grad_value, grad_query_pos, grad_key_pos = lax.map(
        partial(attend_backward, scale=scale), back_items
    )
    grad_query_coeff = rotate_back(
        grad_query_pos.reshape(tok_count, HEADS, pos_width), sin_tok, cos_tok
    ).astype(jnp.bfloat16)
    grad_key_coeff = rotate_back(
        grad_key_pos.reshape(tok_count, HEADS, pos_width), sin_tok, cos_tok
    ).astype(jnp.bfloat16)
    grad_w_pos = jnp.einsum(
        "thp,thd->phd", grad_query_coeff, query, preferred_element_type=jnp.float32
    )
    grad_w_pos = (
        grad_w_pos
        + jnp.einsum("thp,thd->phd", grad_key_coeff, key, preferred_element_type=jnp.float32)
    ).reshape(pos_width, width)
    grad_query = grad_query.reshape(tok_count, HEADS, head_dim) + jnp.einsum(
        "thp,phd->thd", grad_query_coeff, back_pos_heads, preferred_element_type=jnp.float32
    )
    grad_key = grad_key.reshape(tok_count, HEADS, head_dim) + jnp.einsum(
        "thp,phd->thd", grad_key_coeff, back_pos_heads, preferred_element_type=jnp.float32
    )
    grad_value = grad_value.reshape(tok_count, HEADS, head_dim)
    grad_qkv = (
        jnp.stack([grad_query, grad_key, grad_value], axis=1)
        .reshape(tok_count, 3 * width)
        .astype(jnp.bfloat16)
    )
    grad_w_qkv = jnp.einsum("td,te->de", tokens_in, grad_qkv, preferred_element_type=jnp.float32)
    grad_tokens = grad_resid_one + jnp.einsum(
        "te,de->td", grad_qkv, back_qkv, preferred_element_type=jnp.float32
    )
    axes = ("dp", "rep")

    def scatter_sum(values):
        return lax.psum_scatter(values, axes, scatter_dimension=0, tiled=True).astype(jnp.float32)

    low = jnp.bfloat16
    sum_down = scatter_sum(grad_w_down.astype(low))
    sum_up = scatter_sum(grad_w_up.astype(low))
    sum_first = scatter_sum(
        jnp.concatenate([grad_w_qkv.astype(low), grad_w_pos.astype(low), grad_w_out.astype(low)], axis=1)
    )
    sum_qkv = sum_first[:, : 3 * width]
    sum_pos = sum_first[:, 3 * width : 4 * width]
    sum_out = sum_first[:, 4 * width :]
    sum_small = lax.psum_scatter(
        jnp.stack([grad_gain_attn, grad_bias_attn, grad_gain_ffn, grad_bias_ffn], axis=1),
        axes,
        scatter_dimension=0,
        tiled=True,
    )
    sum_gain_attn, sum_bias_attn, sum_gain_ffn, sum_bias_ffn = [sum_small[:, i] for i in range(4)]
    return (
        output.astype(jnp.bfloat16),
        grad_tokens,
        rms_values,
        sum_qkv,
        sum_out,
        sum_pos,
        sum_gain_attn,
        sum_bias_attn,
        sum_up,
        sum_down,
        sum_gain_ffn,
        sum_bias_ffn,
    )


def solution(mesh):
    in_specs = (
        P(("dp", "rep"), None),
        P(None, ("dp", "rep")),
        P(("dp", "rep"), None),
        P(("dp", "rep"), None),
        P(("dp", "rep"), None),
        P(("dp", "rep"), None),
        P(("dp", "rep"), None),
        P(("dp", "rep")),
        P(("dp", "rep")),
        P(("dp", "rep"), None),
        P(("dp", "rep"), None),
        P(("dp", "rep")),
        P(("dp", "rep")),
    )
    out_specs = (
        P(("dp", "rep"), None),
        P(("dp", "rep"), None),
        P(),
        P(("dp", "rep"), None),
        P(("dp", "rep"), None),
        P(("dp", "rep"), None),
        P(("dp", "rep")),
        P(("dp", "rep")),
        P(("dp", "rep"), None),
        P(("dp", "rep"), None),
        P(("dp", "rep")),
        P(("dp", "rep")),
    )
    return jax.shard_map(body, mesh=mesh, in_specs=in_specs, out_specs=out_specs, check_vma=False)
```

```python
from functools import partial
import math

import jax
import jax.numpy as jnp
import numpy as np
from jax import lax
from jax.experimental import pallas as pl
from jax.experimental.pallas import tpu as pltpu
from jax.sharding import PartitionSpec as P

HEADS = 12
FREQS = 192
BLOCKS = 16
LANES = 128
UP_CHUNK = 1024

epsilon = 1e-05
masked_value = -1e30
f32 = jnp.float32
bf16 = jnp.bfloat16
VMEM_LIMIT = 48 * 1024 * 1024


def swap(values, axis, mask):
    size = lax.axis_size(axis)
    return lax.ppermute(values, axis, [(i, i ^ mask) for i in range(size)])


def swap_core(values):
    return swap(values, "rep", 1)


def tree_stages():
    dp, rep = lax.axis_size("dp"), lax.axis_size("rep")
    half = rep // 2
    y = [[("rep", 2 * k, k) for k in range(1, half)]] if half > 1 else []
    x = [[("dp", 1, half)]]
    z = []
    bit = 2
    while bit < dp:
        if 2 * bit < dp:
            z.append([("dp", k * bit, k * bit * half) for k in (1, 2, 3)])
            bit *= 4
        else:
            z.append([("dp", bit, bit * half)])
            bit *= 2
    return x, y, z


def slot_chips(stages):
    rels = [0]
    for stage in stages:
        rels = rels + [rel ^ chip for _, _, chip in stage for rel in rels]
    return rels


def after(value, *others):
    return lax.optimization_barrier((value,) + others)[0] if others else value


class Gather:
    def __init__(self, block, stages):
        self.stack, self.stages = [block], list(stages)

    def step(self, *others):
        for _ in range(max(1, len(self.stages) - 2)):
            whole = self.stack[0] if len(self.stack) == 1 else jnp.concatenate(self.stack, axis=0)
            whole = after(whole, *others)
            self.stack = [whole] + [swap(whole, axis, mask) for axis, mask, _ in self.stages.pop(0)]


def add_up(terms):
    total = terms[0].astype(f32)
    for term in terms[1:]:
        total = total + term.astype(f32)
    return total


class Scatter:
    def __init__(self, chunks, stages):
        self.chunks, self.stages = chunks, list(stages[::-1])
        self.sends = []

    def load(self, *others):
        self.sends = [after(add_up(chunk).astype(bf16), *others) for chunk in self.chunks[1:]]
        return self.sends

    def step(self, *others):
        stage = self.stages.pop(0)
        if not self.sends:
            self.load(*others)
        terms = list(self.chunks[0])
        terms += [swap(send, axis, mask) for (axis, mask, _), send in zip(stage, self.sends)]
        self.sends = []
        if not self.stages:
            self.total = add_up(terms)
            return
        parts = len(self.stages[0]) + 1
        rows = terms[0].shape[0] // parts
        self.chunks = [[term[i * rows : (i + 1) * rows] for term in terms] for i in range(parts)]

    def finish(self):
        while self.stages:
            self.step()
        return self.total


def natural_pieces(stack, rels, chip, fast):
    if fast:
        per = len(rels) // len(stack)
        return stack, [rels[i * per : (i + 1) * per] for i in range(len(stack))]
    whole = jnp.concatenate(stack, axis=0)
    count = len(rels)
    where = np.zeros(count, np.int32)
    for slot, rel in enumerate(rels):
        where[rel] = slot
    order = jnp.asarray(where)[chip ^ jnp.arange(count, dtype=jnp.int32)]
    whole = whole.reshape(count, whole.shape[0] // count, whole.shape[1])
    whole = jnp.take(whole, order, axis=0).reshape(-1, whole.shape[2])
    return [whole], [list(range(BLOCKS))]


def tree_chunks(pieces, rels, parts, chip, fast):
    if fast:
        return pieces
    whole = jnp.concatenate(pieces, axis=0)
    count = len(rels)
    whole = whole.reshape(count, whole.shape[0] // count, whole.shape[1])
    order = jnp.asarray(np.array(rels, np.int32)) ^ chip
    whole = jnp.take(whole, order, axis=0).reshape(-1, whole.shape[2])
    rows = whole.shape[0] // parts
    return [whole[i * rows : (i + 1) * rows] for i in range(parts)]


def by_core(core, mine, other, axis):
    return jnp.where(
        core == 0,
        jnp.concatenate([mine, other], axis=axis),
        jnp.concatenate([other, mine], axis=axis),
    )


def pair_block(core, halves):
    mine = jnp.where(core == 0, halves[0], halves[1])
    send = jnp.where(core == 0, halves[1], halves[0])
    return by_core(core, mine, swap_core(send), 0)


def dot(left, right):
    return lax.dot_general(left, right, (((1,), (0,)), ((), ())), preferred_element_type=f32)


def dot_nt(left, right):
    return lax.dot_general(left, right, (((1,), (1,)), ((), ())), preferred_element_type=f32)


def run_copies(copies, sems):
    started = []
    for at, (source, target) in enumerate(copies):
        copy = pltpu.make_async_copy(source, target, sems.at[at])
        copy.start()
        started.append(copy)
    return started


def wait_all(started):
    for copy in started:
        copy.wait()


def slots_of(pieces, rels):
    return [(piece, at, rel) for piece, table in zip(pieces, rels) for at, rel in enumerate(table)]


def block_rows(index, size):
    return pl.ds(pl.multiple_of(index * size, size), size)


def pos_block(index):
    quarter, within = index // (BLOCKS // 4), index % (BLOCKS // 4)
    return ((quarter % 2) * 2 + quarter // 2) * (BLOCKS // 4) + within


def core_lanes(core, width):
    return pl.ds(pl.multiple_of(core * width, LANES), width)


def head_mask(shape, dim, which, head_dim, kind):
    place = lax.broadcasted_iota(jnp.int32, shape, dim)
    return ((place // head_dim) == which).astype(f32).astype(kind)


def attend_forward_kernel(rels_one, rels_two, scale, head_dim, meta, x2, sin, cos, sin_t, cos_t, feats, feats_t, bias, *refs):
    count_one, count_two = len(rels_one), len(rels_two)
    pieces_one, refs = refs[:count_one], refs[count_one:]
    pieces_two, refs = refs[:count_two], refs[count_two:]
    w_qk, w_v, w_pos, query, key, value, probs, ctx_own, ctx_par, lhs, rhs, sems = refs
    chip = meta[0]
    width = x2.shape[1]
    part = w_v.shape[1]
    row_len = bias.shape[1]
    rows = width // BLOCKS
    copies = []
    for piece, at, rel in slots_of(pieces_one, rels_one):
        copies.append((piece.at[pl.ds(at * rows, rows), :], w_qk.at[block_rows(chip ^ rel, rows), :]))
    for piece, at, rel in slots_of(pieces_two, rels_two):
        source = piece.at[pl.ds(at * rows, rows), :]
        copies.append((source.at[:, pl.ds(0, part)], w_v.at[block_rows(chip ^ rel, rows), :]))
        copies.append((source.at[:, pl.ds(part, part)], w_pos.at[block_rows(pos_block(chip ^ rel), rows), :]))
    started = run_copies(copies, sems)
    lhs[:, width : 2 * width] = feats[...]
    rhs[0:width, :] = feats_t[...]
    wait_all(started)
    query[...] = dot(x2[...], w_qk[:, 0:part]).astype(bf16)
    key[...] = dot(x2[...], w_qk[:, part:]).astype(bf16)
    value[...] = dot(x2[...], w_v[...]).astype(bf16)
    half = width // 2

    def one_pair(pair, carry):
        lanes = pl.ds(pl.multiple_of(pair * LANES, LANES), LANES)
        q_pair, k_pair, v_pair, w_pair = query[:, lanes], key[:, lanes], value[:, lanes], w_pos[:, lanes]
        rhs[2 * width : 2 * width + LANES, :] = k_pair.T
        mixed = [None, None]
        for which in (0, 1):
            lane_mask = head_mask((1, LANES), 1, which, head_dim, bf16)
            q_head = q_pair * lane_mask
            k_head = k_pair * lane_mask
            lhs[:, 2 * width :] = q_head
            for row in (0, 1):
                span = slice(row * row_len, (row + 1) * row_len)
                coeff = dot_nt(q_head[span], w_pair)
                along_sin, along_cos = coeff[:, :half], coeff[:, half:]
                sin_row, cos_row = sin[span, :], cos[span, :]
                lhs[span, 0:half] = (along_cos * sin_row - along_sin * cos_row).astype(bf16)
                lhs[span, half:width] = (along_sin * sin_row + along_cos * cos_row).astype(bf16)
                coeff = dot_nt(w_pair, k_head[span])
                along_sin, along_cos = coeff[:half], coeff[half:]
                sin_row, cos_row = sin_t[:, span], cos_t[:, span]
                rhs[width : width + half, span] = (along_cos * sin_row - along_sin * cos_row).astype(bf16)
                rhs[width + half : 2 * width, span] = (along_sin * sin_row + along_cos * cos_row).astype(bf16)
            for row in (0, 1):
                span = slice(row * row_len, (row + 1) * row_len)
                scores = dot(lhs[span, :], rhs[:, span]) * scale + bias[row]
                top = jnp.max(scores, axis=-1, keepdims=True)
                expo = jnp.exp(scores - top)
                prob = expo / jnp.sum(expo, axis=-1, keepdims=True)
                probs[pair, which * 2 + row] = prob
                piece = dot(prob.astype(bf16), v_pair[span] * lane_mask)
                mixed[row] = piece if mixed[row] is None else mixed[row] + piece
        ctx_own[:, lanes] = mixed[0].astype(bf16)
        ctx_par[:, lanes] = mixed[1].astype(bf16)
        return carry

    lax.fori_loop(0, part // LANES, one_pair, 0)


def vmem_spec():
    return pl.BlockSpec(memory_space=pltpu.VMEM)


def any_spec():
    return pl.BlockSpec(memory_space=pl.ANY)


def smem_spec():
    return pl.BlockSpec(memory_space=pltpu.SMEM)


def params():
    return pltpu.CompilerParams(vmem_limit_bytes=VMEM_LIMIT)


def shape(dims, kind):
    return jax.ShapeDtypeStruct(dims, kind)


def cost(flops, moved):
    return pl.CostEstimate(flops=int(flops), bytes_accessed=int(moved), transcendentals=0)


def attend_forward(meta, x2, tables, bias, stack_one, rels_one, stack_two, rels_two, scale, head_dim):
    tokens, width = x2.shape
    part = width // 2
    row_len = tokens // 2
    pairs = part // LANES
    copies = sum(map(len, rels_one)) + 2 * sum(map(len, rels_two))
    return pl.pallas_call(
        partial(attend_forward_kernel, rels_one, rels_two, scale, head_dim),
        out_shape=[
            shape((width, 2 * part), bf16),
            shape((width, part), bf16),
            shape((width, part), bf16),
            shape((tokens, part), bf16),
            shape((tokens, part), bf16),
            shape((tokens, part), bf16),
            shape((pairs, 4, row_len, row_len), f32),
            shape((row_len, part), bf16),
            shape((row_len, part), bf16),
        ],
        in_specs=[smem_spec()] + [vmem_spec()] * 8 + [any_spec()] * (len(stack_one) + len(stack_two)),
        out_specs=[vmem_spec()] * 9,
        scratch_shapes=[
            pltpu.VMEM((tokens, 2 * width + LANES), bf16),
            pltpu.VMEM((2 * width + LANES, tokens), bf16),
            pltpu.SemaphoreType.DMA((copies,)),
        ],
        compiler_params=params(),
        cost_estimate=cost(2 * 2.0e9, 15e6),
        name="attend_forward",
    )(meta, x2, *tables, bias, *stack_one, *stack_two)


def norm_values(values):
    centered = values - jnp.mean(values, axis=-1, keepdims=True)
    inv_std = lax.rsqrt(jnp.mean(centered * centered, axis=-1, keepdims=True) + epsilon)
    return centered * inv_std, inv_std


def norm_backward(grad, normed_vals, inv_std, gain):
    grad_normed = grad * gain
    centered_grad = grad_normed - jnp.mean(grad_normed, axis=-1, keepdims=True)
    return inv_std * (
        centered_grad - normed_vals * jnp.mean(grad_normed * normed_vals, axis=-1, keepdims=True)
    )


def column_copies(pieces, rels, chip, rows, start, size, target, lanes):
    place = pl.ds(pl.multiple_of(lanes, LANES), size)
    return [
        (piece.at[pl.ds(at * rows, rows), pl.ds(start, size)], target.at[block_rows(chip ^ rel, rows), place])
        for piece, at, rel in slots_of(pieces, rels)
    ]


def out_proj_kernel(rels, start, meta, ctx_mine, ctx_recv, tokens, *refs):
    count = len(rels)
    mine, other, refs = refs[:count], refs[count : 2 * count], refs[2 * count :]
    w_out, gains, normed_one, normed_vals, inv_std, normed_low, sums, gain_buf, sems = refs
    chip, core = meta[0], meta[1]
    width = tokens.shape[1]
    half = width // 2
    rows = width // BLOCKS
    copies = []
    for pieces, side in ((mine, core), (other, 1 - core)):
        copies += column_copies(pieces, rels, chip, rows, start, half, w_out, side * half)
        copies += column_copies(pieces, rels, chip, rows, start + half, LANES, gain_buf, side * LANES)
    started = run_copies(copies, sems)
    wait_all(started)
    attn_out = dot(ctx_mine[...], w_out[block_rows(core, half), :])
    attn_out = attn_out + dot(ctx_recv[...], w_out[block_rows(1 - core, half), :])
    gain_t = [gain_buf[:, i * LANES : (i + 1) * LANES].astype(f32).T for i in (0, 1)]
    for i in (0, 1):
        gains[2 * i : 2 * i + 2, :] = gain_t[i][0:2, :]
    gains[4:8, :] = jnp.zeros((4, width), f32)
    tokens_f = tokens[...].astype(f32)
    resid = tokens_f + attn_out
    vals, inv = norm_values(resid)
    one = vals * gain_t[0][0:1, :] + gain_t[0][1:2, :]
    normed_one[...] = one
    normed_vals[...] = vals
    inv_std[...] = inv
    normed_low[...] = one.astype(bf16)
    sums[0:1, :] = jnp.sum(tokens_f * tokens_f, axis=0, keepdims=True)
    sums[1:2, :] = jnp.sum(attn_out * attn_out, axis=0, keepdims=True)
    sums[2:3, :] = jnp.sum(resid * resid, axis=0, keepdims=True)
    sums[3:8, :] = jnp.zeros((5, width), f32)


def out_proj(meta, ctx_mine, ctx_recv, tokens, mine, other, rels, start):
    count, width = tokens.shape
    return pl.pallas_call(
        partial(out_proj_kernel, rels, start),
        out_shape=[
            shape((width, width), bf16),
            shape((8, width), f32),
            shape((count, width), f32),
            shape((count, width), f32),
            shape((count, 1), f32),
            shape((count, width), bf16),
            shape((8, width), f32),
        ],
        in_specs=[smem_spec()] + [vmem_spec()] * 3 + [any_spec()] * (len(mine) + len(other)),
        out_specs=[vmem_spec()] * 7,
        scratch_shapes=[
            pltpu.VMEM((width, 2 * LANES), bf16),
            pltpu.SemaphoreType.DMA((4 * sum(map(len, rels)),)),
        ],
        compiler_params=params(),
        cost_estimate=cost(2 * 0.15e9, 5e6),
        name="out_proj",
    )(meta, ctx_mine, ctx_recv, tokens, *mine, *other)


def up_copies(pieces, rels, chip, core, w_up):
    width, ff = w_up.shape
    rows = width // BLOCKS
    split = UP_CHUNK
    copies = []
    for side, chunks in ((core, pieces[:2]), (1 - core, pieces[2:])):
        start = side * (ff // 2)
        copies += column_copies(chunks[0], rels[0], chip, rows, 0, split, w_up, start)
        copies += column_copies(chunks[1], rels[1], chip, rows, 0, ff // 2 - split, w_up, start + split)
    return copies


def take_lists(refs, sizes):
    taken = []
    for size in sizes:
        taken.append(refs[:size])
        refs = refs[size:]
    return taken, refs


def ffn_up_kernel(rels, tile, meta, normed_low, *refs):
    pieces, refs = take_lists(refs, [len(rels[0]), len(rels[1])] * 2)
    act, act_grad, w_up, sems = refs
    ff = w_up.shape[1]
    wait_all(run_copies(up_copies(pieces, rels, meta[0], meta[1], w_up), sems))

    def one_tile(at, carry):
        lanes = pl.ds(pl.multiple_of(at * tile, tile), tile)
        pre = dot(normed_low[...], w_up[:, lanes])
        bell = 0.5 * (1.0 + lax.erf(pre * (0.5**0.5)))
        act[:, lanes] = (pre * bell).astype(bf16)
        act_grad[:, lanes] = bell + pre * jnp.exp(pre * pre * -0.5) * (0.5 / math.pi) ** 0.5
        return carry

    lax.fori_loop(0, ff // tile, one_tile, 0)


def up_copy_count(rels):
    return 2 * sum(map(len, rels[0])) + 2 * sum(map(len, rels[1]))


def ffn_up(meta, normed_low, pieces, rels, ff):
    count, width = normed_low.shape
    flat = [array for chunk in pieces for array in chunk]
    return pl.pallas_call(
        partial(ffn_up_kernel, rels, 512),
        out_shape=[shape((count, ff), bf16), shape((count, ff), f32)],
        in_specs=[smem_spec(), vmem_spec()] + [any_spec()] * len(flat),
        out_specs=[vmem_spec()] * 2,
        scratch_shapes=[
            pltpu.VMEM((width, ff), bf16),
            pltpu.SemaphoreType.DMA((up_copy_count(rels),)),
        ],
        compiler_params=params(),
        cost_estimate=cost(2 * 0.6e9, 10e6),
        name="ffn_up",
    )(meta, normed_low, *flat)


def ffn_down_kernel(rels, out_rels, tile, meta, act, act_grad, normed_one, gains, cotangent, *refs):
    pieces, refs = take_lists(refs, [len(rels[0]), len(rels[1])] * 2)
    output, grad_resid, grad_gains, grad_pre = refs[:4]
    outs, refs = refs[4:12], refs[12:]
    w_down, act_t, ordered, low, sems = refs
    chip, core = meta[0], meta[1]
    ff, width = w_down.shape
    half = width // 2
    rows = ff // BLOCKS // 2
    copies = []
    for side, chunks in ((core, pieces[:2]), (1 - core, pieces[2:])):
        for i in (0, 1):
            for piece, at, rel in slots_of(chunks[i], rels[i]):
                copies.append(
                    (
                        piece.at[pl.ds(at * rows, rows), :],
                        w_down.at[block_rows((chip ^ rel) * 2 + side, rows), pl.ds(i * half, half)],
                    )
                )
    started = run_copies(copies, sems)

    def turn(at, carry):
        lanes = pl.ds(pl.multiple_of(at * tile, tile), tile)
        act_t[lanes, :] = act[:, lanes].T
        return carry

    lax.fori_loop(0, ff // tile, turn, 0)
    wait_all(started)
    vals, inv = norm_values(normed_one[...] + dot(act[...], w_down[...]))
    gain, shift = gains[2:3, :], gains[3:4, :]
    output[...] = (vals * gain + shift).astype(bf16)
    grad = cotangent[...].astype(f32)
    grad_gains[0:1, :] = jnp.sum(grad * vals, axis=0, keepdims=True)
    grad_gains[1:2, :] = jnp.sum(grad, axis=0, keepdims=True)
    grad_gains[2:8, :] = jnp.zeros((6, width), f32)
    resid = norm_backward(grad, vals, inv, gain)
    grad_resid[...] = resid
    low[...] = resid.astype(bf16)
    for i in (0, 1):
        for side, place in ((0, core), (1, 1 - core)):
            for slot, rel in enumerate(out_rels[i]):
                ordered[slot * rows : (slot + 1) * rows, :] = act_t[block_rows((chip ^ rel) * 2 + place, rows), :]
            keep, send = outs[4 * side + 2 * i : 4 * side + 2 * i + 2]
            piece = dot(ordered[...], low[:, i * half : (i + 1) * half]).astype(bf16)
            keep[...] = piece[: ff // 4]
            send[...] = piece[ff // 4 :]

    def one_tile(at, carry):
        lanes = pl.ds(pl.multiple_of(at * tile, tile), tile)
        grad_pre[:, lanes] = (dot_nt(low[...], w_down[lanes, :]) * act_grad[:, lanes]).astype(bf16)
        return carry

    lax.fori_loop(0, ff // tile, one_tile, 0)


def ffn_down(meta, act, act_grad, normed_one, gains, cotangent, pieces, rels, out_rels):
    count, ff = act.shape
    width = normed_one.shape[1]
    flat = [array for chunk in pieces for array in chunk]
    return pl.pallas_call(
        partial(ffn_down_kernel, rels, out_rels, 512),
        out_shape=[
            shape((count, width), bf16),
            shape((count, width), f32),
            shape((8, width), f32),
            shape((count, ff), bf16),
        ]
        + [shape((ff // 4, width // 2), bf16)] * 8,
        in_specs=[smem_spec()] + [vmem_spec()] * 5 + [any_spec()] * len(flat),
        out_specs=[vmem_spec()] * 12,
        scratch_shapes=[
            pltpu.VMEM((ff, width), bf16),
            pltpu.VMEM((ff, count), bf16),
            pltpu.VMEM((ff // 2, count), bf16),
            pltpu.VMEM((count, width), bf16),
            pltpu.SemaphoreType.DMA((up_copy_count(rels),)),
        ],
        compiler_params=params(),
        cost_estimate=cost(2 * 1.8e9, 22e6),
        name="ffn_down",
    )(meta, act, act_grad, normed_one, gains, cotangent, *flat)


def permute_rows(source, target, chip, out_rels):
    rows = source.shape[0] // BLOCKS
    for slot, rel in enumerate(out_rels):
        target[slot * rows : (slot + 1) * rows, :] = source[block_rows(chip ^ rel, rows), :]


def ffn_back_kernel(
    rels, out_rels, tile, meta, grad_pre, normed_low, w_out, grad_resid_two, normed_vals, inv_std, gains,
    grad_gains, ctx_mine, ctx_recv, *refs
):
    pieces, refs = take_lists(refs, [len(rels[0]), len(rels[1])] * 2)
    grad_resid, grad_ctx_mine, grad_ctx_send = refs[:3]
    outs, refs = refs[3:11], refs[11:]
    w_up, turned, ordered_one, ordered_two, low, gain_buf, sems = refs
    chip, core = meta[0], meta[1]
    width, ff = w_up.shape
    half, ff_half = width // 2, ff // 2
    rows = width // BLOCKS
    started = run_copies(up_copies(pieces, rels, chip, core, w_up), sems)
    turned[...] = normed_low[...].T
    permute_rows(turned, ordered_one, chip, out_rels[0])
    permute_rows(turned, ordered_two, chip, out_rels[1])

    def chunk_of(side, i):
        return outs[4 * side + 2 * i : 4 * side + 2 * i + 2]

    def put(targets, place, piece):
        targets[0][:, place] = piece[:half]
        targets[1][:, place] = piece[half:]

    for side, place in ((0, core), (1, 1 - core)):

        def one_tile(at, carry, side=side, place=place):
            lanes = pl.ds(pl.multiple_of(place * ff_half + at * tile, tile), tile)
            piece = dot(ordered_one[...], grad_pre[:, lanes]).astype(bf16)
            put(chunk_of(side, 0), pl.ds(pl.multiple_of(at * tile, tile), tile), piece)
            return carry

        lax.fori_loop(0, UP_CHUNK // tile, one_tile, 0)
        rest = ff_half - UP_CHUNK
        lanes = pl.ds(pl.multiple_of(place * ff_half + UP_CHUNK, LANES), rest)
        put(chunk_of(side, 1), pl.ds(0, rest), dot(ordered_two[...], grad_pre[:, lanes]).astype(bf16))
    wait_all(started)
    grad = grad_resid_two[...] + dot_nt(grad_pre[...], w_up[...])
    vals = normed_vals[...]
    resid = norm_backward(grad, vals, inv_std[...], gains[0:1, :])
    grad_resid[...] = resid
    low[...] = resid.astype(bf16)
    grad_ctx_mine[...] = dot_nt(low[...], w_out[block_rows(core, half), :]).astype(bf16)
    grad_ctx_send[...] = dot_nt(low[...], w_out[block_rows(1 - core, half), :]).astype(bf16)
    turned[block_rows(core, half), :] = ctx_mine[...].T
    turned[block_rows(1 - core, half), :] = ctx_recv[...].T
    permute_rows(turned, ordered_two, chip, out_rels[1])
    first = jnp.concatenate(
        [jnp.sum(grad * vals, axis=0, keepdims=True), jnp.sum(grad, axis=0, keepdims=True)], axis=0
    )
    second = grad_gains[0:2, :]
    at_first = (core == 0).astype(f32)
    pair = (first * at_first + second * (1.0 - at_first), first * (1.0 - at_first) + second * at_first)
    start = ff_half - UP_CHUNK
    slots = BLOCKS // 2
    for side, place in ((0, core), (1, 1 - core)):
        targets = chunk_of(side, 1)
        piece = dot(ordered_two[...], low[:, core_lanes(place, half)]).astype(bf16)
        put(targets, pl.ds(start, half), piece)
        padded = jnp.concatenate([pair[side], jnp.zeros((LANES - 2, width), f32)], axis=0)
        gain_buf[...] = padded.T.astype(bf16)
        for slot, rel in enumerate(out_rels[1]):
            at = slot % slots
            targets[slot // slots][at * rows : (at + 1) * rows, pl.ds(start + half, LANES)] = gain_buf[
                block_rows(chip ^ rel, rows), :
            ]


def ffn_back(meta, grad_pre, normed_low, w_out, grad_resid_two, normed_vals, inv_std, gains, grad_gains, ctx_mine,
             ctx_recv, pieces, rels, out_rels):
    count, ff = grad_pre.shape
    width = normed_low.shape[1]
    half = width // 2
    flat = [array for chunk in pieces for array in chunk]
    one = shape((half, UP_CHUNK), bf16)
    two = shape((half, ff // 2 - UP_CHUNK + half + LANES), bf16)
    return pl.pallas_call(
        partial(ffn_back_kernel, rels, out_rels, 512),
        out_shape=[
            shape((count, width), f32),
            shape((count, half), bf16),
            shape((count, half), bf16),
        ]
        + [one, one, two, two] * 2,
        in_specs=[smem_spec()] + [vmem_spec()] * 10 + [any_spec()] * len(flat),
        out_specs=[vmem_spec()] * 11,
        scratch_shapes=[
            pltpu.VMEM((width, ff), bf16),
            pltpu.VMEM((width, count), bf16),
            pltpu.VMEM((width, count), bf16),
            pltpu.VMEM((width, count), bf16),
            pltpu.VMEM((count, width), bf16),
            pltpu.VMEM((width, LANES), bf16),
            pltpu.SemaphoreType.DMA((up_copy_count(rels),)),
        ],
        compiler_params=params(),
        cost_estimate=cost(2 * 1.6e9, 20e6),
        name="ffn_back",
    )(meta, grad_pre, normed_low, w_out, grad_resid_two, normed_vals, inv_std, gains, grad_gains, ctx_mine, ctx_recv,
      *flat)


def attend_backward_kernel(
    out_rels, scale, head_dim, meta, x2_t, sin, cos, sin_t, cos_t, feats, feats_t, query, key, value, w_pos, probs,
    grad_own, grad_par, grad_qkv, keep, send, grad_ctx, coeff_q, coeff_k, x2_rel, pos_buf
):
    chip = meta[0]
    tokens, width = feats.shape
    row_len = tokens // 2
    half = width // 2
    grad_ctx[0:row_len, :] = grad_own[...]
    grad_ctx[row_len:, :] = grad_par[...]
    permute_rows(x2_t, x2_rel, chip, out_rels)
    q_pair, k_pair, v_pair, w_pair, g_pair = query[...], key[...], value[...], w_pos[...], grad_ctx[...]
    q_t, v_t, g_t, w_t = q_pair.T, v_pair.T, g_pair.T, w_pair.T
    grad_q = [None, None]
    grad_k = [None, None]
    grad_v = [None, None]

    def plus(total, term):
        return term if total is None else total + term

    grad_q_coeff = None
    grad_k_coeff = None
    pos_q = None
    pos_k = None
    for which in (0, 1):
        lane_mask = head_mask((1, LANES), 1, which, head_dim, bf16)
        row_mask = head_mask((LANES, 1), 0, which, head_dim, bf16)
        k_head, g_head, w_head = k_pair * lane_mask, g_pair * lane_mask, w_pair * lane_mask
        q_t_head, g_t_head, w_t_head = q_t * row_mask, g_t * row_mask, w_t * row_mask
        for row in (0, 1):
            span = slice(row * row_len, (row + 1) * row_len)
            prob = probs[0, which * 2 + row]
            grad_probs = dot(g_head[span], v_t[:, span])
            inner = jnp.sum(prob * grad_probs, axis=-1, keepdims=True)
            grad_scores = (prob * (grad_probs - inner) * scale).astype(bf16)
            grad_v[row] = plus(grad_v[row], dot(g_t_head[:, span], prob.astype(bf16)))
            grad_k[row] = plus(grad_k[row], dot(q_t_head[:, span], grad_scores))
            grad_q[row] = plus(grad_q[row], dot(grad_scores, k_head[span]))
            pos = dot(grad_scores, feats[span, :])
            first, second = pos[:, :half], pos[:, half:]
            sin_row, cos_row = sin[span, :], cos[span, :]
            coeff_q[span, 0:half] = (second * sin_row - first * cos_row).astype(bf16)
            coeff_q[span, half:] = (first * sin_row + second * cos_row).astype(bf16)
            pos = dot(feats_t[:, span], grad_scores)
            first, second = pos[:half], pos[half:]
            sin_row, cos_row = sin_t[:, span], cos_t[:, span]
            coeff_k[0:half, span] = (second * sin_row - first * cos_row).astype(bf16)
            coeff_k[half:, span] = (first * sin_row + second * cos_row).astype(bf16)
        grad_q_coeff = plus(grad_q_coeff, dot(coeff_q[...], w_head))
        grad_k_coeff = plus(grad_k_coeff, dot(w_t_head, coeff_k[...]))
        pos_q = plus(pos_q, dot(q_t_head, coeff_q[...]))
        pos_k = plus(pos_k, dot(coeff_k[...], k_head))
    d_q = (jnp.concatenate(grad_q, axis=0) + grad_q_coeff).astype(bf16)
    d_k = (jnp.concatenate(grad_k, axis=1) + grad_k_coeff).astype(bf16).T
    d_v = jnp.concatenate(grad_v, axis=1).astype(bf16).T
    grad_qkv[:, 0:LANES] = d_q
    grad_qkv[:, LANES : 2 * LANES] = d_k
    grad_qkv[:, 2 * LANES :] = d_v
    weights = dot(x2_rel[...], grad_qkv[...]).astype(bf16)
    rows_half = width // 2
    keep[:, 0 : 3 * LANES] = weights[:rows_half]
    send[:, 0 : 3 * LANES] = weights[rows_half:]
    pos_buf[...] = (pos_k + pos_q.T).astype(bf16)
    rows = width // BLOCKS
    slots = BLOCKS // 2
    for slot, rel in enumerate(out_rels):
        target = keep if slot < slots else send
        at = slot % slots
        target[at * rows : (at + 1) * rows, 3 * LANES :] = pos_buf[block_rows(pos_block(chip ^ rel), rows), :]


def attend_backward(meta, pair, x2_t, tables, query, key, value, w_pos, probs, grad_own, grad_par, out_rels, scale, head_dim):
    width, tokens = x2_t.shape
    row_len = tokens // 2

    def whole(array):
        return pl.BlockSpec(array.shape, lambda i: (0,) * array.ndim)

    def columns(rows):
        return pl.BlockSpec((rows, LANES), lambda i: (0, pair))

    piece = shape((width // 2, 4 * LANES), bf16)
    return pl.pallas_call(
        partial(attend_backward_kernel, out_rels, scale, head_dim),
        grid=(1,),
        out_shape=[shape((tokens, 3 * LANES), bf16), piece, piece],
        in_specs=[smem_spec(), whole(x2_t)]
        + [whole(table) for table in tables]
        + [columns(tokens)] * 3
        + [columns(width), pl.BlockSpec((1, 4, row_len, row_len), lambda i: (pair, 0, 0, 0))]
        + [columns(row_len)] * 2,
        out_specs=[
            pl.BlockSpec((tokens, 3 * LANES), lambda i: (0, 0)),
            pl.BlockSpec(piece.shape, lambda i: (0, 0)),
            pl.BlockSpec(piece.shape, lambda i: (0, 0)),
        ],
        scratch_shapes=[
            pltpu.VMEM((tokens, LANES), bf16),
            pltpu.VMEM((tokens, width), bf16),
            pltpu.VMEM((width, tokens), bf16),
            pltpu.VMEM((width, tokens), bf16),
            pltpu.VMEM((width, LANES), bf16),
        ],
        compiler_params=params(),
        cost_estimate=cost(2 * 1.3e9, 10e6),
        name="attend_backward",
    )(meta, x2_t, *tables, query, key, value, w_pos, probs, grad_own, grad_par)


def row_tables(boxes):
    rates = jnp.exp(jnp.arange(FREQS, dtype=f32) * (-math.log(10000.0) / FREQS))
    angles = boxes.astype(f32)[:, :, None] * rates[None, None, :]
    angles = jnp.transpose(angles, (1, 0, 2)).reshape(boxes.shape[1], 2 * FREQS)
    sin, cos = jnp.sin(angles), jnp.cos(angles)
    feats = jnp.concatenate([sin, cos], axis=1).astype(bf16)
    return sin, cos, sin.T, cos.T, feats, feats.T


def body(
    tokens_in, boxes, page_lengths, cotangent, w_qkv, w_out, w_pos, gain_attn, bias_attn, w_up, w_down, gain_ffn, bias_ffn
):
    row_len, width = tokens_in.shape
    ff = w_up.shape[1]
    half, ff_half = width // 2, ff // 2
    head_dim = width // HEADS
    scale = head_dim ** (-0.5)
    dp, rep = lax.axis_size("dp"), lax.axis_size("rep")
    chips = dp * rep // 2
    core = lax.axis_index("rep") % 2
    chip = lax.axis_index("dp") * (rep // 2) + lax.axis_index("rep") // 2
    fast = chips == BLOCKS
    meta = jnp.stack([chip if fast else 0 * chip, core]).astype(jnp.int32)
    x, y, z = tree_stages()
    order_one, order_two = z + x + y, z + y + x
    rels_one, rels_two = slot_chips(order_one), slot_chips(order_two)

    def heads_half(weight, at, side):
        return weight[:, at * width + side * half : at * width + (side + 1) * half]

    qk = pair_block(
        core, [jnp.concatenate([heads_half(w_qkv, 0, s), heads_half(w_qkv, 1, s)], axis=1) for s in (0, 1)]
    )
    vp = pair_block(core, [jnp.concatenate([heads_half(w_qkv, 2, s), heads_half(w_pos, 0, s)], axis=1) for s in (0, 1)])
    g_qk, g_vp = Gather(qk, order_one), Gather(vp, order_two)
    g_qk.step()
    g_vp.step()
    x2 = jnp.concatenate([tokens_in, swap_core(tokens_in)], axis=0)
    ends = jnp.cumsum(page_lengths, axis=1)
    places = jnp.arange(row_len, dtype=jnp.int32)
    segment = jnp.sum((places[None, :, None] >= ends[:, None, :]).astype(jnp.int32), axis=2)
    marks = jnp.concatenate([boxes, segment], axis=0)
    marks_other = swap_core(marks)
    segments = jnp.stack([marks[2], marks_other[2]])
    bias = jnp.where(segments[:, :, None] == segments[:, None, :], 0.0, masked_value).astype(f32)
    tables = row_tables(jnp.concatenate([marks[:2], marks_other[:2]], axis=1))

    gain_sets = ((gain_attn, bias_attn), (gain_ffn, bias_ffn))
    pad = jnp.zeros((w_up.shape[0], LANES - 2), bf16)

    def up_part(side, start, stop):
        return w_up[:, side * ff_half + start : side * ff_half + stop]

    wide_one = pair_block(core, [up_part(s, 0, UP_CHUNK) for s in (0, 1)])
    wide_two = pair_block(
        core,
        [
            jnp.concatenate(
                [
                    up_part(s, UP_CHUNK, ff_half),
                    w_out[:, s * half : (s + 1) * half],
                    jnp.stack(gain_sets[s], axis=1),
                    pad,
                ],
                axis=1,
            )
            for s in (0, 1)
        ],
    )
    g_wide = [Gather(wide_one, order_one), Gather(wide_two, order_two)]
    g_deep = [Gather(w_down[:, :half], order_one), Gather(w_down[:, half:], order_two)]
    first = g_qk.stack + g_vp.stack
    for gather in g_wide:
        gather.step(*first)
    wide_first = g_wide[0].stack + g_wide[1].stack
    g_qk.step()
    g_vp.step()
    second = g_qk.stack + g_vp.stack
    for gather in g_deep:
        gather.step(*wide_first)
    deep_first = g_deep[0].stack + g_deep[1].stack
    g_qk.step()
    g_vp.step()
    for gather in g_wide:
        gather.step(*second)
    wide_second = g_wide[0].stack + g_wide[1].stack
    for gather in g_deep:
        gather.step(*wide_second)
    for gather in g_wide:
        gather.step()
    for gather in g_deep:
        gather.step()

    def with_other(gathers):
        mine = [gather.stack for gather in gathers]
        return mine + [[swap_core(piece) for piece in stack] for stack in mine]

    def tabled(stacks):
        done = [natural_pieces(stack, rels, chip, fast) for stack, rels in zip(stacks, (rels_one, rels_two) * 2)]
        return [pieces for pieces, _ in done], [table for _, table in done[:2]]

    wide, table_wide = tabled(with_other(g_wide))
    deep_stacks = with_other(g_deep)
    if fast:
        deep, table_deep = tabled(deep_stacks)
    else:
        plain, table_deep = tabled(deep_stacks)
        deep = [None] * 4
        for i in (0, 1):
            mine, other = [stack[0].reshape(chips, 1, -1, half) for stack in (plain[i], plain[2 + i])]
            cut = by_core(core, mine, other, 1).reshape(BLOCKS, 2, -1, half)
            deep[i] = [jnp.where(core == 0, cut[:, 0], cut[:, 1]).reshape(-1, half)]
            deep[2 + i] = [jnp.where(core == 0, cut[:, 1], cut[:, 0]).reshape(-1, half)]
    stack_qk, table_qk = natural_pieces(g_qk.stack, rels_one, chip, fast)
    stack_vp, table_vp = natural_pieces(g_vp.stack, rels_two, chip, fast)

    w_qk, w_v, w_pos_half, query, key, value, probs, ctx_mine, ctx_send = attend_forward(
        meta, after(x2, *wide_second, *deep_first), tables, bias, stack_qk, table_qk, stack_vp, table_vp, scale, head_dim
    )
    ctx_recv = swap_core(ctx_send)
    w_out_whole, gains, normed_one, normed_vals, inv_std, normed_low, sums = out_proj(
        meta, ctx_mine, ctx_recv, tokens_in, wide[1], wide[3], table_wide[1], ff_half - UP_CHUNK
    )
    act, act_grad = ffn_up(meta, normed_low, wide, table_wide, ff)
    natural = list(range(BLOCKS))
    out_rels = (rels_one, rels_two) if fast else (natural, natural)
    orders = (order_one, order_two)
    all_rels = (rels_one, rels_two)
    output, grad_resid_two, grad_gains, grad_pre, *deep_grads = ffn_down(
        meta, act, act_grad, normed_one, gains, cotangent, deep, table_deep, out_rels
    )
    if not fast:
        fixed = [None] * 8
        for i in (0, 1):
            mine, other = [
                jnp.concatenate(deep_grads[4 * s + 2 * i : 4 * s + 2 * i + 2], axis=0).reshape(BLOCKS, 1, -1, half)
                for s in (0, 1)
            ]
            cut = by_core(core, mine, other, 1).reshape(chips, 2, -1, half)
            for s, picked in ((0, jnp.where(core == 0, cut[:, 0], cut[:, 1])), (1, jnp.where(core == 0, cut[:, 1], cut[:, 0]))):
                picked = picked.reshape(-1, half)
                rows = picked.shape[0] // 2
                fixed[4 * s + 2 * i], fixed[4 * s + 2 * i + 1] = picked[:rows], picked[rows:]
        deep_grads = fixed

    def start_scatter(grads, which):
        stages, rels = orders[which], all_rels[which]
        parts = len(stages[-1]) + 1
        mine = tree_chunks(grads[:2], rels, parts, chip, fast)
        if len(grads) == 2:
            return Scatter([[piece] for piece in mine], stages)
        other = [swap_core(piece) for piece in tree_chunks(grads[2:], rels, parts, chip, fast)]
        return Scatter([[a, b] for a, b in zip(mine, other)], stages)

    def start_both(grads):
        return [start_scatter(grads[2 * i : 2 * i + 2] + grads[4 + 2 * i : 6 + 2 * i], i) for i in (0, 1)]

    s_deep = start_both(deep_grads)
    deep_loads = [send for scatter in s_deep for send in scatter.load()]
    grad_resid_one, grad_ctx_mine, grad_ctx_send, *wide_grads = ffn_back(
        meta, after(grad_pre, *deep_loads), normed_low, w_out_whole, grad_resid_two, normed_vals, inv_std, gains,
        grad_gains, ctx_mine, ctx_recv, wide, table_wide, out_rels
    )
    for scatter in s_deep:
        scatter.step()
    s_wide = start_both(wide_grads)
    wide_loads = [send for scatter in s_wide for send in scatter.load()]
    grad_ctx_recv = swap_core(grad_ctx_send)
    x2_t = x2.T

    def back_pair(pair, *others):
        grad_qkv, keep, send = attend_backward(
            meta, pair, x2_t, tables, query, key, value, w_pos_half, probs, after(grad_ctx_mine, *others), grad_ctx_recv,
            out_rels[pair % 2], scale, head_dim
        )
        return grad_qkv, start_scatter([keep, send], pair % 2)

    pairs = [back_pair(0, *wide_loads)]
    for scatter in s_wide:
        scatter.step()
    pairs.append(back_pair(1, pairs[0][0]))
    deep_loads = [send for scatter in s_deep for send in scatter.load(pairs[0][0])]
    for scatter in s_deep:
        scatter.step()
    pairs.append(back_pair(2, pairs[1][0], *deep_loads))
    deep_sum = [scatter.finish() for scatter in s_deep]
    wide_sum = [scatter.finish() for scatter in s_wide]
    pair_grads = [grads for grads, _ in pairs]
    pair_sums = [scatter.finish() for _, scatter in pairs]
    grad_q, grad_k, grad_v = [
        jnp.concatenate([grads[:, i * LANES : (i + 1) * LANES] for grads in pair_grads], axis=1) for i in range(3)
    ]
    grad_x2 = dot_nt(jnp.concatenate([grad_q, grad_k], axis=1), w_qk) + dot_nt(grad_v, w_v)
    grad_tokens = grad_resid_one + grad_x2[:row_len] + swap_core(grad_x2[row_len:])

    def own_rows(values):
        rows = values.shape[0] // 2
        mine = jnp.where(core == 0, values[:rows], values[rows:])
        send = jnp.where(core == 0, values[rows:], values[:rows])
        return mine, swap_core(send)

    def sides(pieces, start, size):
        return by_core(core, pieces[0][:, start : start + size], pieces[1][:, start : start + size], 1)

    wide_rows = own_rows(jnp.concatenate(wide_sum, axis=1))
    pair_rows = own_rows(jnp.concatenate(pair_sums, axis=1))

    def pair_columns(which):
        picked = [
            jnp.concatenate(
                [rows[:, (4 * i + which) * LANES : (4 * i + which + 1) * LANES] for i in range(half // LANES)], axis=1
            )
            for rows in pair_rows
        ]
        return by_core(core, picked[0], picked[1], 1)

    gain_rows = sides(wide_rows, ff_half + half, LANES)
    total = jnp.sum(sums[:3], axis=1)
    for axis, size in (("rep", rep), ("dp", dp)):
        for bit in range(size.bit_length() - 1):
            total = total + swap(total, axis, 1 << bit)
    rms = jnp.sqrt(total / (row_len * width * dp * rep))
    return (
        output,
        grad_tokens,
        rms,
        jnp.concatenate([pair_columns(0), pair_columns(1), pair_columns(2)], axis=1),
        sides(wide_rows, ff_half, half),
        pair_columns(3),
        gain_rows[:, 0],
        gain_rows[:, 1],
        sides(wide_rows, 0, ff_half),
        jnp.concatenate(deep_sum, axis=1),
        gain_rows[:, LANES],
        gain_rows[:, LANES + 1],
    )


def solution(mesh):
    rows = P(("dp", "rep"), None)
    line = P(("dp", "rep"))
    in_specs = (rows, P(None, ("dp", "rep")), rows, rows, rows, rows, rows, line, line, rows, rows, line, line)
    out_specs = (rows, rows, P(), rows, rows, rows, line, line, rows, rows, line, line)
    return jax.shard_map(body, mesh=mesh, in_specs=in_specs, out_specs=out_specs, check_vma=False)
```

```python
from functools import partial
import math

import jax
import jax.numpy as jnp
import numpy as np
from jax import lax
from jax.experimental import pallas as pl
from jax.experimental.pallas import tpu as pltpu
from jax.sharding import PartitionSpec as P

HEADS = 12
FREQS = 192
BLOCKS = 16
LANES = 128
UP_CHUNK = 1024
COST_SCALE = 100.0

epsilon = 1e-05
masked_value = -1e30
f32 = jnp.float32
bf16 = jnp.bfloat16
VMEM_LIMIT = 48 * 1024 * 1024


def swap(values, axis, mask):
    size = lax.axis_size(axis)
    return lax.ppermute(values, axis, [(i, i ^ mask) for i in range(size)])


def swap_core(values):
    return swap(values, "rep", 1)


def tree_stages():
    dp, rep = lax.axis_size("dp"), lax.axis_size("rep")
    half = rep // 2
    y = [[("rep", 2 * k, k) for k in range(1, half)]] if half > 1 else []
    x = [[("dp", 1, half)]]
    z_wide, z_thin = [], []
    bit = 2
    while bit < dp:
        z_thin.insert(0, [("dp", bit, bit * half)])
        bit *= 2
    bit = 2
    while bit < dp:
        if 2 * bit < dp:
            z_wide.append([("dp", k * bit, k * bit * half) for k in (1, 2, 3)])
            bit *= 4
        else:
            z_wide.append([("dp", bit, bit * half)])
            bit *= 2
    return x, y, z_wide, z_thin


def slot_chips(stages):
    rels = [0]
    for stage in stages:
        rels = rels + [rel ^ chip for _, _, chip in stage for rel in rels]
    return rels


def after(value, *others):
    return lax.optimization_barrier((value,) + others)[0] if others else value


def gather_first(block, stages, *others):
    stack = [after(block, *others)]
    for at, stage in enumerate(stages):
        whole = stack[0] if len(stack) == 1 else jnp.concatenate(stack, axis=0)
        stack = [whole] + [swap(whole, axis, mask) for axis, mask, _ in stage]
    return stack


def columns_of(stack, start, stop):
    return jnp.concatenate([piece[:, start:stop] for piece in stack], axis=0)


def gather_rest(stack, stages):
    for stage in stages:
        whole = stack[0] if len(stack) == 1 else jnp.concatenate(stack, axis=0)
        stack = [whole] + [swap(whole, axis, mask) for axis, mask, _ in stage]
    return stack


def add_up(terms):
    total = terms[0].astype(f32)
    for term in terms[1:]:
        total = total + term.astype(f32)
    return total


def split_rows(terms, parts):
    rows = terms[0].shape[0] // parts
    return [[term[i * rows : (i + 1) * rows] for term in terms] for i in range(parts)]


class Scatter:
    def __init__(self, arrays, orders, z):
        self.arrays = arrays
        self.stages = [order[len(z) :][::-1] for order in orders]
        self.z = z[::-1]
        self.joined = False

    def load(self, *others):
        if not self.joined and not self.stages[0]:
            self.arrays = [[jnp.concatenate([add_up(terms) for terms in self.arrays], axis=1)]]
            self.stages = [self.z]
            self.joined = True
        self.now = [stages.pop(0) for stages in self.stages]
        self.chunks = [split_rows(terms, len(stage) + 1) for terms, stage in zip(self.arrays, self.now)]
        self.sends = [[after(add_up(chunk).astype(bf16), *others) for chunk in chunks[1:]] for chunks in self.chunks]
        return [send for sends in self.sends for send in sends]

    def move(self):
        self.arrays = [
            chunks[0] + [swap(send, axis, mask) for (axis, mask, _), send in zip(stage, sends)]
            for chunks, stage, sends in zip(self.chunks, self.now, self.sends)
        ]

    def step(self, *others):
        sends = self.load(*others)
        self.move()
        return sends

    def finish(self, *others):
        while not self.joined or self.stages[0]:
            self.step(*others)
        return add_up(self.arrays[0])


def natural_pieces(stack, rels, chip, fast):
    if fast:
        per = len(rels) // len(stack)
        return stack, [rels[i * per : (i + 1) * per] for i in range(len(stack))]
    whole = jnp.concatenate(stack, axis=0)
    count = len(rels)
    where = np.zeros(count, np.int32)
    for slot, rel in enumerate(rels):
        where[rel] = slot
    order = jnp.asarray(where)[chip ^ jnp.arange(count, dtype=jnp.int32)]
    whole = whole.reshape(count, whole.shape[0] // count, whole.shape[1])
    whole = jnp.take(whole, order, axis=0).reshape(-1, whole.shape[2])
    return [whole], [list(range(BLOCKS))]


def in_slots(whole, rels, chip, fast):
    if fast:
        return whole
    count = len(rels)
    whole = whole.reshape(count, whole.shape[0] // count, whole.shape[1])
    order = jnp.asarray(np.array(rels, np.int32)) ^ chip
    return jnp.take(whole, order, axis=0).reshape(-1, whole.shape[2])


def by_core(core, mine, other, axis):
    return jnp.where(
        core == 0,
        jnp.concatenate([mine, other], axis=axis),
        jnp.concatenate([other, mine], axis=axis),
    )


def pair_block(core, halves):
    mine = jnp.where(core == 0, halves[0], halves[1])
    send = jnp.where(core == 0, halves[1], halves[0])
    return by_core(core, mine, swap_core(send), 0)


def dot(left, right):
    return lax.dot_general(left, right, (((1,), (0,)), ((), ())), preferred_element_type=f32)


def dot_nt(left, right):
    return lax.dot_general(left, right, (((1,), (1,)), ((), ())), preferred_element_type=f32)


def run_copies(copies, sems):
    started = []
    for at, (source, target) in enumerate(copies):
        copy = pltpu.make_async_copy(source, target, sems.at[at])
        copy.start()
        started.append(copy)
    return started


def wait_all(started):
    for copy in started:
        copy.wait()


def slots_of(pieces, rels):
    return [(piece, at, rel) for piece, table in zip(pieces, rels) for at, rel in enumerate(table)]


def block_rows(index, size):
    return pl.ds(pl.multiple_of(index * size, size), size)


def pos_block(index):
    quarter, within = index // (BLOCKS // 4), index % (BLOCKS // 4)
    return ((quarter % 2) * 2 + quarter // 2) * (BLOCKS // 4) + within


def core_lanes(core, width):
    return pl.ds(pl.multiple_of(core * width, LANES), width)


def head_mask(shape, dim, which, head_dim, kind):
    place = lax.broadcasted_iota(jnp.int32, shape, dim)
    return ((place // head_dim) == which).astype(f32).astype(kind)


def attend_forward_kernel(rels_one, rels_two, scale, head_dim, meta, x2, sin, cos, sin_t, cos_t, feats, feats_t, bias, *refs):
    count_one, count_two = len(rels_one), len(rels_two)
    pieces_one, refs = refs[:count_one], refs[count_one:]
    pieces_two, refs = refs[:count_two], refs[count_two:]
    w_qk, w_v, w_pos, query, key, value, probs, ctx_own, ctx_par, lhs, rhs, sems = refs
    chip = meta[0]
    width = x2.shape[1]
    part = w_v.shape[1]
    row_len = bias.shape[1]
    rows = width // BLOCKS
    copies = []
    for piece, at, rel in slots_of(pieces_one, rels_one):
        copies.append((piece.at[pl.ds(at * rows, rows), :], w_qk.at[block_rows(chip ^ rel, rows), :]))
    for piece, at, rel in slots_of(pieces_two, rels_two):
        source = piece.at[pl.ds(at * rows, rows), :]
        copies.append((source.at[:, pl.ds(0, part)], w_v.at[block_rows(chip ^ rel, rows), :]))
        copies.append((source.at[:, pl.ds(part, part)], w_pos.at[block_rows(pos_block(chip ^ rel), rows), :]))
    started = run_copies(copies, sems)
    lhs[:, width : 2 * width] = feats[...]
    rhs[0:width, :] = feats_t[...]
    wait_all(started)
    query[...] = dot(x2[...], w_qk[:, 0:part]).astype(bf16)
    key[...] = dot(x2[...], w_qk[:, part:]).astype(bf16)
    value[...] = dot(x2[...], w_v[...]).astype(bf16)
    half = width // 2

    def one_pair(pair, carry):
        lanes = pl.ds(pl.multiple_of(pair * LANES, LANES), LANES)
        q_pair, k_pair, v_pair, w_pair = query[:, lanes], key[:, lanes], value[:, lanes], w_pos[:, lanes]
        rhs[2 * width : 2 * width + LANES, :] = k_pair.T
        mixed = [None, None]
        for which in (0, 1):
            lane_mask = head_mask((1, LANES), 1, which, head_dim, bf16)
            q_head = q_pair * lane_mask
            k_head = k_pair * lane_mask
            lhs[:, 2 * width :] = q_head
            for row in (0, 1):
                span = slice(row * row_len, (row + 1) * row_len)
                coeff = dot_nt(q_head[span], w_pair)
                along_sin, along_cos = coeff[:, :half], coeff[:, half:]
                sin_row, cos_row = sin[span, :], cos[span, :]
                lhs[span, 0:half] = (along_cos * sin_row - along_sin * cos_row).astype(bf16)
                lhs[span, half:width] = (along_sin * sin_row + along_cos * cos_row).astype(bf16)
                coeff = dot_nt(w_pair, k_head[span])
                along_sin, along_cos = coeff[:half], coeff[half:]
                sin_row, cos_row = sin_t[:, span], cos_t[:, span]
                rhs[width : width + half, span] = (along_cos * sin_row - along_sin * cos_row).astype(bf16)
                rhs[width + half : 2 * width, span] = (along_sin * sin_row + along_cos * cos_row).astype(bf16)
            for row in (0, 1):
                span = slice(row * row_len, (row + 1) * row_len)
                scores = dot(lhs[span, :], rhs[:, span]) * scale + bias[row]
                top = jnp.max(scores, axis=-1, keepdims=True)
                expo = jnp.exp(scores - top)
                prob = expo / jnp.sum(expo, axis=-1, keepdims=True)
                probs[pair, which * 2 + row] = prob
                piece = dot(prob.astype(bf16), v_pair[span] * lane_mask)
                mixed[row] = piece if mixed[row] is None else mixed[row] + piece
        ctx_own[:, lanes] = mixed[0].astype(bf16)
        ctx_par[:, lanes] = mixed[1].astype(bf16)
        return carry

    lax.fori_loop(0, part // LANES, one_pair, 0)


def vmem_spec():
    return pl.BlockSpec(memory_space=pltpu.VMEM)


def any_spec():
    return pl.BlockSpec(memory_space=pl.ANY)


def smem_spec():
    return pl.BlockSpec(memory_space=pltpu.SMEM)


def params():
    return pltpu.CompilerParams(vmem_limit_bytes=VMEM_LIMIT)


def shape(dims, kind):
    return jax.ShapeDtypeStruct(dims, kind)


def cost(flops, moved):
    return pl.CostEstimate(flops=int(flops * COST_SCALE), bytes_accessed=int(moved * COST_SCALE), transcendentals=0)


def attend_forward(meta, x2, tables, bias, stack_one, rels_one, stack_two, rels_two, scale, head_dim):
    tokens, width = x2.shape
    part = width // 2
    row_len = tokens // 2
    pairs = part // LANES
    copies = sum(map(len, rels_one)) + 2 * sum(map(len, rels_two))
    return pl.pallas_call(
        partial(attend_forward_kernel, rels_one, rels_two, scale, head_dim),
        out_shape=[
            shape((width, 2 * part), bf16),
            shape((width, part), bf16),
            shape((width, part), bf16),
            shape((tokens, part), bf16),
            shape((tokens, part), bf16),
            shape((tokens, part), bf16),
            shape((pairs, 4, row_len, row_len), f32),
            shape((row_len, part), bf16),
            shape((row_len, part), bf16),
        ],
        in_specs=[smem_spec()] + [vmem_spec()] * 8 + [any_spec()] * (len(stack_one) + len(stack_two)),
        out_specs=[vmem_spec()] * 9,
        scratch_shapes=[
            pltpu.VMEM((tokens, 2 * width + LANES), bf16),
            pltpu.VMEM((2 * width + LANES, tokens), bf16),
            pltpu.SemaphoreType.DMA((copies,)),
        ],
        compiler_params=params(),
        cost_estimate=cost(2 * 2.0e9, 15e6),
        name="attend_forward",
    )(meta, x2, *tables, bias, *stack_one, *stack_two)


def norm_values(values):
    centered = values - jnp.mean(values, axis=-1, keepdims=True)
    inv_std = lax.rsqrt(jnp.mean(centered * centered, axis=-1, keepdims=True) + epsilon)
    return centered * inv_std, inv_std


def norm_backward(grad, normed_vals, inv_std, gain):
    grad_normed = grad * gain
    centered_grad = grad_normed - jnp.mean(grad_normed, axis=-1, keepdims=True)
    return inv_std * (
        centered_grad - normed_vals * jnp.mean(grad_normed * normed_vals, axis=-1, keepdims=True)
    )


def out_proj_kernel(ff, meta, ctx_mine, ctx_recv, tokens, wide, w_out, gains, normed_one, normed_vals, inv_std, normed_low,
                    sums, gain_buf, sems):
    core = meta[1]
    width = tokens.shape[1]
    half = width // 2
    wait_all(
        run_copies(
            [(wide.at[:, pl.ds(ff, width)], w_out), (wide.at[:, pl.ds(ff + width, LANES)], gain_buf)], sems
        )
    )
    attn_out = dot(ctx_mine[...], w_out[block_rows(core, half), :])
    attn_out = attn_out + dot(ctx_recv[...], w_out[block_rows(1 - core, half), :])
    gain_t = gain_buf[...].astype(f32).T
    gains[...] = gain_t[0:8, :]
    tokens_f = tokens[...].astype(f32)
    resid = tokens_f + attn_out
    vals, inv = norm_values(resid)
    one = vals * gain_t[0:1, :] + gain_t[1:2, :]
    normed_one[...] = one
    normed_vals[...] = vals
    inv_std[...] = inv
    normed_low[...] = one.astype(bf16)
    sums[0:1, :] = jnp.sum(tokens_f * tokens_f, axis=0, keepdims=True)
    sums[1:2, :] = jnp.sum(attn_out * attn_out, axis=0, keepdims=True)
    sums[2:3, :] = jnp.sum(resid * resid, axis=0, keepdims=True)
    sums[3:8, :] = jnp.zeros((5, width), f32)


def out_proj(meta, ctx_mine, ctx_recv, tokens, wide, ff):
    count, width = tokens.shape
    return pl.pallas_call(
        partial(out_proj_kernel, ff),
        out_shape=[
            shape((width, width), bf16),
            shape((8, width), f32),
            shape((count, width), f32),
            shape((count, width), f32),
            shape((count, 1), f32),
            shape((count, width), bf16),
            shape((8, width), f32),
        ],
        in_specs=[smem_spec()] + [vmem_spec()] * 3 + [any_spec()],
        out_specs=[vmem_spec()] * 7,
        scratch_shapes=[pltpu.VMEM((width, LANES), bf16), pltpu.SemaphoreType.DMA((2,))],
        compiler_params=params(),
        cost_estimate=cost(2 * 0.15e9, 5e6),
        name="out_proj",
    )(meta, ctx_mine, ctx_recv, tokens, wide)


def tile_copies(wide, w_up, tile):
    return [(wide.at[:, pl.ds(at, tile)], w_up.at[:, pl.ds(at, tile)]) for at in range(0, w_up.shape[1], tile)]


def ffn_up_kernel(tile, meta, normed_low, wide, act, act_grad, w_up, sems):
    started = run_copies(tile_copies(wide, w_up, tile), sems)
    for at, copy in enumerate(started):
        copy.wait()
        lanes = pl.ds(at * tile, tile)
        pre = dot(normed_low[...], w_up[:, lanes])
        bell = 0.5 * (1.0 + lax.erf(pre * (0.5**0.5)))
        act[:, lanes] = (pre * bell).astype(bf16)
        act_grad[:, lanes] = bell + pre * jnp.exp(pre * pre * -0.5) * (0.5 / math.pi) ** 0.5


def ffn_up(meta, normed_low, wide, ff):
    count, width = normed_low.shape
    tile = 512
    return pl.pallas_call(
        partial(ffn_up_kernel, tile),
        out_shape=[shape((count, ff), bf16), shape((count, ff), f32)],
        in_specs=[smem_spec(), vmem_spec(), any_spec()],
        out_specs=[vmem_spec()] * 2,
        scratch_shapes=[pltpu.VMEM((width, ff), bf16), pltpu.SemaphoreType.DMA((ff // tile,))],
        compiler_params=params(),
        cost_estimate=cost(2 * 0.6e9, 10e6),
        name="ffn_up",
    )(meta, normed_low, wide)


def take_lists(refs, sizes):
    taken = []
    for size in sizes:
        taken.append(refs[:size])
        refs = refs[size:]
    return taken, refs


def ffn_down_kernel(rels, out_rels, tile, meta, act, act_grad, normed_one, gains, cotangent, *refs):
    pieces, refs = take_lists(refs, [len(rels[0]), len(rels[1])] * 2)
    output, grad_resid, grad_gains, grad_pre, grad_mine, grad_other, w_down, act_t, ordered, low, sems = refs
    chip, core = meta[0], meta[1]
    ff, width = w_down.shape
    half = width // 2
    rows = ff // BLOCKS // 2
    copies = []
    for side, chunks in ((core, pieces[:2]), (1 - core, pieces[2:])):
        for i in (0, 1):
            for piece, at, rel in slots_of(chunks[i], rels[i]):
                copies.append(
                    (
                        piece.at[pl.ds(at * rows, rows), :],
                        w_down.at[block_rows((chip ^ rel) * 2 + side, rows), pl.ds(i * half, half)],
                    )
                )
    started = run_copies(copies, sems)

    def turn(at, carry):
        lanes = pl.ds(pl.multiple_of(at * tile, tile), tile)
        act_t[lanes, :] = act[:, lanes].T
        return carry

    lax.fori_loop(0, ff // tile, turn, 0)
    wait_all(started)
    vals, inv = norm_values(normed_one[...] + dot(act[...], w_down[...]))
    gain, shift = gains[2:3, :], gains[3:4, :]
    output[...] = (vals * gain + shift).astype(bf16)
    grad = cotangent[...].astype(f32)
    grad_gains[0:1, :] = jnp.sum(grad * vals, axis=0, keepdims=True)
    grad_gains[1:2, :] = jnp.sum(grad, axis=0, keepdims=True)
    grad_gains[2:8, :] = jnp.zeros((6, width), f32)
    resid = norm_backward(grad, vals, inv, gain)
    grad_resid[...] = resid
    low[...] = resid.astype(bf16)
    for i in (0, 1):
        for target, place in ((grad_mine, core), (grad_other, 1 - core)):
            for slot, rel in enumerate(out_rels[i]):
                ordered[slot * rows : (slot + 1) * rows, :] = act_t[block_rows((chip ^ rel) * 2 + place, rows), :]
            target[:, i * half : (i + 1) * half] = dot(ordered[...], low[:, i * half : (i + 1) * half]).astype(bf16)

    def one_tile(at, carry):
        lanes = pl.ds(pl.multiple_of(at * tile, tile), tile)
        grad_pre[:, lanes] = (dot_nt(low[...], w_down[lanes, :]) * act_grad[:, lanes]).astype(bf16)
        return carry

    lax.fori_loop(0, ff // tile, one_tile, 0)


def ffn_down(meta, act, act_grad, normed_one, gains, cotangent, pieces, rels, out_rels):
    count, ff = act.shape
    width = normed_one.shape[1]
    flat = [array for chunk in pieces for array in chunk]
    return pl.pallas_call(
        partial(ffn_down_kernel, rels, out_rels, 512),
        out_shape=[
            shape((count, width), bf16),
            shape((count, width), f32),
            shape((8, width), f32),
            shape((count, ff), bf16),
        ]
        + [shape((ff // 2, width), bf16)] * 2,
        in_specs=[smem_spec()] + [vmem_spec()] * 5 + [any_spec()] * len(flat),
        out_specs=[vmem_spec()] * 6,
        scratch_shapes=[
            pltpu.VMEM((ff, width), bf16),
            pltpu.VMEM((ff, count), bf16),
            pltpu.VMEM((ff // 2, count), bf16),
            pltpu.VMEM((count, width), bf16),
            pltpu.SemaphoreType.DMA((2 * sum(map(len, rels[0] + rels[1])),)),
        ],
        compiler_params=params(),
        cost_estimate=cost(2 * 1.8e9, 22e6),
        name="ffn_down",
    )(meta, act, act_grad, normed_one, gains, cotangent, *flat)


def permute_rows(source, target, chip, out_rels):
    rows = source.shape[0] // BLOCKS
    for slot, rel in enumerate(out_rels):
        target[slot * rows : (slot + 1) * rows, :] = source[block_rows(chip ^ rel, rows), :]


def ffn_back_kernel(
    tile, meta, grad_pre, w_out, grad_resid_two, normed_vals, inv_std, gains, grad_gains, wide, grad_resid, low,
    grad_ctx_mine, grad_ctx_send, all_gains, w_up, sems
):
    core = meta[1]
    width = w_up.shape[0]
    half = width // 2
    started = run_copies(tile_copies(wide, w_up, tile), sems)
    grad = grad_resid_two[...]
    for at, copy in enumerate(started):
        copy.wait()
        lanes = pl.ds(at * tile, tile)
        grad = grad + dot_nt(grad_pre[:, lanes], w_up[:, lanes])
    vals = normed_vals[...]
    resid = norm_backward(grad, vals, inv_std[...], gains[0:1, :])
    grad_resid[...] = resid
    low[...] = resid.astype(bf16)
    grad_ctx_mine[...] = dot_nt(low[...], w_out[block_rows(core, half), :]).astype(bf16)
    grad_ctx_send[...] = dot_nt(low[...], w_out[block_rows(1 - core, half), :]).astype(bf16)
    all_gains[0:1, :] = jnp.sum(grad * vals, axis=0, keepdims=True)
    all_gains[1:2, :] = jnp.sum(grad, axis=0, keepdims=True)
    all_gains[2:4, :] = grad_gains[0:2, :]
    all_gains[4:8, :] = jnp.zeros((4, width), f32)


def ffn_back(meta, grad_pre, w_out, grad_resid_two, normed_vals, inv_std, gains, grad_gains, wide):
    count, ff = grad_pre.shape
    width = w_out.shape[0]
    half = width // 2
    tile = 1024
    return pl.pallas_call(
        partial(ffn_back_kernel, tile),
        out_shape=[
            shape((count, width), f32),
            shape((count, width), bf16),
            shape((count, half), bf16),
            shape((count, half), bf16),
            shape((8, width), f32),
        ],
        in_specs=[smem_spec()] + [vmem_spec()] * 7 + [any_spec()],
        out_specs=[vmem_spec()] * 5,
        scratch_shapes=[pltpu.VMEM((width, ff), bf16), pltpu.SemaphoreType.DMA((ff // tile,))],
        compiler_params=params(),
        cost_estimate=cost(2 * 0.8e9, 10e6),
        name="ffn_back",
    )(meta, grad_pre, w_out, grad_resid_two, normed_vals, inv_std, gains, grad_gains, wide)


def weight_grads_kernel(out_rels, tile, meta, grad_pre, normed_low, low, all_gains, ctx_mine, ctx_recv, *refs):
    grads, (turned, ordered_one, ordered_two, gain_buf) = refs[:2], refs[2:]
    chip, core = meta[0], meta[1]
    width, ff = turned.shape[0], grad_pre.shape[1]
    half, ff_half = width // 2, ff // 2
    rows = width // BLOCKS
    turned[...] = normed_low[...].T
    permute_rows(turned, ordered_one, chip, out_rels[0])
    permute_rows(turned, ordered_two, chip, out_rels[1])
    rest = ff_half - UP_CHUNK
    for grad, place in ((grads[0], core), (grads[1], 1 - core)):

        def one_tile(at, carry, grad=grad, place=place):
            lanes = pl.ds(pl.multiple_of(place * ff_half + at * tile, tile), tile)
            target = pl.ds(pl.multiple_of(at * tile, tile), tile)
            grad[:, target] = dot(ordered_one[...], grad_pre[:, lanes]).astype(bf16)
            return carry

        lax.fori_loop(0, UP_CHUNK // tile, one_tile, 0)
        lanes = pl.ds(pl.multiple_of(place * ff_half + UP_CHUNK, LANES), rest)
        grad[:, UP_CHUNK:ff_half] = dot(ordered_two[...], grad_pre[:, lanes]).astype(bf16)
    turned[block_rows(core, half), :] = ctx_mine[...].T
    turned[block_rows(1 - core, half), :] = ctx_recv[...].T
    permute_rows(turned, ordered_two, chip, out_rels[1])
    first, second = all_gains[0:2, :], all_gains[2:4, :]
    at_first = (core == 0).astype(f32)
    pair = (first * at_first + second * (1.0 - at_first), first * (1.0 - at_first) + second * at_first)
    for side, place in ((0, core), (1, 1 - core)):
        grad = grads[side]
        grad[:, ff_half : ff_half + half] = dot(ordered_two[...], low[:, core_lanes(place, half)]).astype(bf16)
        padded = jnp.concatenate([pair[side], jnp.zeros((LANES - 2, width), f32)], axis=0)
        gain_buf[...] = padded.T.astype(bf16)
        for slot, rel in enumerate(out_rels[1]):
            grad[slot * rows : (slot + 1) * rows, ff_half + half :] = gain_buf[block_rows(chip ^ rel, rows), :]


def weight_grads(meta, grad_pre, normed_low, low, all_gains, ctx_mine, ctx_recv, out_rels):
    count, ff = grad_pre.shape
    width = normed_low.shape[1]
    return pl.pallas_call(
        partial(weight_grads_kernel, out_rels, 512),
        out_shape=[shape((width, ff // 2 + width // 2 + LANES), bf16)] * 2,
        in_specs=[smem_spec()] + [vmem_spec()] * 6,
        out_specs=[vmem_spec()] * 2,
        scratch_shapes=[pltpu.VMEM((width, count), bf16)] * 3 + [pltpu.VMEM((width, LANES), bf16)],
        compiler_params=params(),
        cost_estimate=cost(2 * 0.8e9, 10e6),
        name="weight_grads",
    )(meta, grad_pre, normed_low, low, all_gains, ctx_mine, ctx_recv)


def attend_backward_kernel(
    out_rels, split, scale, head_dim, meta, x2_t, sin, cos, sin_t, cos_t, feats, feats_t, query, key, value, w_pos, probs,
    grad_own, grad_par, grad_qkv, *refs
):
    outs, refs = (refs[:2], refs[2:]) if split else (refs[:1], refs[1:])
    grad_ctx, coeff_q, coeff_k, x2_rel, pos_buf = refs
    chip = meta[0]
    tokens, width = feats.shape
    row_len = tokens // 2
    half = width // 2
    grad_ctx[0:row_len, :] = grad_own[...]
    grad_ctx[row_len:, :] = grad_par[...]
    q_pair, k_pair, v_pair, w_pair, g_pair = query[...], key[...], value[...], w_pos[...], grad_ctx[...]
    q_t, v_t, g_t, w_t = q_pair.T, v_pair.T, g_pair.T, w_pair.T
    grad_q = [None, None]
    grad_k = [None, None]
    grad_v = [None, None]

    def plus(total, term):
        return term if total is None else total + term

    grad_q_coeff = None
    grad_k_coeff = None
    pos_q = None
    pos_k = None
    for which in (0, 1):
        lane_mask = head_mask((1, LANES), 1, which, head_dim, bf16)
        row_mask = head_mask((LANES, 1), 0, which, head_dim, bf16)
        k_head, g_head, w_head = k_pair * lane_mask, g_pair * lane_mask, w_pair * lane_mask
        q_t_head, g_t_head, w_t_head = q_t * row_mask, g_t * row_mask, w_t * row_mask
        for row in (0, 1):
            span = slice(row * row_len, (row + 1) * row_len)
            prob = probs[0, which * 2 + row]
            grad_probs = dot(g_head[span], v_t[:, span])
            inner = jnp.sum(prob * grad_probs, axis=-1, keepdims=True)
            grad_scores = (prob * (grad_probs - inner) * scale).astype(bf16)
            grad_v[row] = plus(grad_v[row], dot(g_t_head[:, span], prob.astype(bf16)))
            grad_k[row] = plus(grad_k[row], dot(q_t_head[:, span], grad_scores))
            grad_q[row] = plus(grad_q[row], dot(grad_scores, k_head[span]))
            pos = dot(grad_scores, feats[span, :])
            first, second = pos[:, :half], pos[:, half:]
            sin_row, cos_row = sin[span, :], cos[span, :]
            coeff_q[span, 0:half] = (second * sin_row - first * cos_row).astype(bf16)
            coeff_q[span, half:] = (first * sin_row + second * cos_row).astype(bf16)
            pos = dot(feats_t[:, span], grad_scores)
            first, second = pos[:half], pos[half:]
            sin_row, cos_row = sin_t[:, span], cos_t[:, span]
            coeff_k[0:half, span] = (second * sin_row - first * cos_row).astype(bf16)
            coeff_k[half:, span] = (first * sin_row + second * cos_row).astype(bf16)
        grad_q_coeff = plus(grad_q_coeff, dot(coeff_q[...], w_head))
        grad_k_coeff = plus(grad_k_coeff, dot(w_t_head, coeff_k[...]))
        pos_q = plus(pos_q, dot(q_t_head, coeff_q[...]))
        pos_k = plus(pos_k, dot(coeff_k[...], k_head))
    d_q = (jnp.concatenate(grad_q, axis=0) + grad_q_coeff).astype(bf16)
    d_k = (jnp.concatenate(grad_k, axis=1) + grad_k_coeff).astype(bf16).T
    d_v = jnp.concatenate(grad_v, axis=1).astype(bf16).T
    grad_qkv[:, 0:LANES] = d_q
    grad_qkv[:, LANES : 2 * LANES] = d_k
    grad_qkv[:, 2 * LANES :] = d_v
    pos_buf[...] = (pos_k + pos_q.T).astype(bf16)
    rows = width // BLOCKS
    cuts = (0, 2 * LANES, 3 * LANES) if split else (0, 3 * LANES)
    for at, out in enumerate(outs):
        size = cuts[at + 1] - cuts[at]
        permute_rows(x2_t, x2_rel, chip, out_rels[at])
        out[:, 0:size] = dot(x2_rel[...], grad_qkv[:, cuts[at] : cuts[at + 1]]).astype(bf16)
    for slot, rel in enumerate(out_rels[-1]):
        outs[-1][slot * rows : (slot + 1) * rows, size:] = pos_buf[block_rows(pos_block(chip ^ rel), rows), :]


def attend_backward(meta, pair, x2_t, tables, query, key, value, w_pos, probs, grad_own, grad_par, out_rels, scale, head_dim):
    width, tokens = x2_t.shape
    row_len = tokens // 2

    def whole(array):
        return pl.BlockSpec(array.shape, lambda i: (0,) * array.ndim)

    def columns(rows):
        return pl.BlockSpec((rows, LANES), lambda i: (0, pair))

    split = len(out_rels) > 1
    pieces = [shape((width, (2 if split else 4) * LANES), bf16)] * (2 if split else 1)
    return pl.pallas_call(
        partial(attend_backward_kernel, out_rels, split, scale, head_dim),
        grid=(1,),
        out_shape=[shape((tokens, 3 * LANES), bf16)] + pieces,
        in_specs=[smem_spec(), whole(x2_t)]
        + [whole(table) for table in tables]
        + [columns(tokens)] * 3
        + [columns(width), pl.BlockSpec((1, 4, row_len, row_len), lambda i: (pair, 0, 0, 0))]
        + [columns(row_len)] * 2,
        out_specs=[pl.BlockSpec((tokens, 3 * LANES), lambda i: (0, 0))]
        + [pl.BlockSpec(piece.shape, lambda i: (0, 0)) for piece in pieces],
        scratch_shapes=[
            pltpu.VMEM((tokens, LANES), bf16),
            pltpu.VMEM((tokens, width), bf16),
            pltpu.VMEM((width, tokens), bf16),
            pltpu.VMEM((width, tokens), bf16),
            pltpu.VMEM((width, LANES), bf16),
        ],
        compiler_params=params(),
        cost_estimate=cost(2 * 1.3e9, 10e6),
        name="attend_backward",
    )(meta, x2_t, *tables, query, key, value, w_pos, probs, grad_own, grad_par)


def row_tables(boxes):
    rates = jnp.exp(jnp.arange(FREQS, dtype=f32) * (-math.log(10000.0) / FREQS))
    angles = boxes.astype(f32)[:, :, None] * rates[None, None, :]
    angles = jnp.transpose(angles, (1, 0, 2)).reshape(boxes.shape[1], 2 * FREQS)
    sin, cos = jnp.sin(angles), jnp.cos(angles)
    feats = jnp.concatenate([sin, cos], axis=1).astype(bf16)
    return sin, cos, sin.T, cos.T, feats, feats.T


def body(
    tokens_in, boxes, page_lengths, cotangent, w_qkv, w_out, w_pos, gain_attn, bias_attn, w_up, w_down, gain_ffn, bias_ffn
):
    row_len, width = tokens_in.shape
    ff = w_up.shape[1]
    half, ff_half = width // 2, ff // 2
    head_dim = width // HEADS
    scale = head_dim ** (-0.5)
    dp, rep = lax.axis_size("dp"), lax.axis_size("rep")
    chips = dp * rep // 2
    core = lax.axis_index("rep") % 2
    chip = lax.axis_index("dp") * (rep // 2) + lax.axis_index("rep") // 2
    fast = chips == BLOCKS
    meta = jnp.stack([chip if fast else 0 * chip, core]).astype(jnp.int32)
    gains_in = jnp.stack([gain_attn, bias_attn, gain_ffn, bias_ffn], axis=1)
    pad = jnp.zeros((w_up.shape[0], LANES - 4), bf16)
    wide = lax.all_gather(jnp.concatenate([w_up, w_out, gains_in, pad], axis=1), ("dp", "rep"), axis=0, tiled=True)

    x, y, z_wide, z = tree_stages()
    heads_orders = (z_wide + x + y, z_wide + y + x)
    orders = (z + x + y, z + y + x)
    heads_rels = [slot_chips(order) for order in heads_orders]
    all_rels = [slot_chips(order) for order in orders]

    def split_columns(stack, cut, *others):
        parts = (columns_of(stack, 0, cut), columns_of(stack, cut, stack[0].shape[1]))
        return [[after(part, *others)] for part in parts]

    def move(stacks, stages, *others):
        moved = []
        for stack, stage in zip(stacks, stages):
            whole = after(stack[0] if len(stack) == 1 else jnp.concatenate(stack, axis=0), *others)
            moved.append([whole] + [swap(whole, axis, mask) for axis, mask, _ in stage])
        return moved

    def sent(stacks):
        return [stack[0] for stack in stacks]

    def heads_half(side):
        parts = [w_qkv[:, at * width + side * half : at * width + (side + 1) * half] for at in range(3)]
        return jnp.concatenate(parts + [w_pos[:, side * half : (side + 1) * half]], axis=1)

    heads_block = pair_block(core, [heads_half(s) for s in (0, 1)])
    heads_z = gather_first(heads_block, z_wide)
    x2 = jnp.concatenate([tokens_in, swap_core(after(tokens_in, heads_block))], axis=0)
    ends = jnp.cumsum(page_lengths, axis=1)
    places = jnp.arange(row_len, dtype=jnp.int32)
    segment = jnp.sum((places[None, :, None] >= ends[:, None, :]).astype(jnp.int32), axis=2)
    marks = after(jnp.concatenate([boxes, segment], axis=0), heads_block)
    marks_other = swap_core(marks)
    segments = jnp.stack([marks[2], marks_other[2]])
    bias = jnp.where(segments[:, :, None] == segments[:, None, :], 0.0, masked_value).astype(f32)
    tables = row_tables(jnp.concatenate([marks[:2], marks_other[:2]], axis=1))

    heads = move(split_columns(heads_z, width), (x[0], y[0]))
    deep_z = gather_first(w_down, z[:-1], *sent(heads))
    heads = move(heads, (y[0], x[0]))
    deep_z = gather_first(jnp.concatenate(deep_z, axis=0), z[-1:], *sent(heads))
    deep = move(split_columns(deep_z, half), (x[0], y[0]))
    deep = move(deep, (y[0], x[0]))
    deep_sent = sent(deep)

    def tabled(stacks, rels):
        done = [natural_pieces(stack, table, chip, fast) for stack, table in zip(stacks, rels * 2)]
        return [pieces for pieces, _ in done], [table for _, table in done[:2]]

    (stack_qk, stack_vp), (table_qk, table_vp) = tabled(heads, heads_rels)
    deep, table_deep = tabled(deep + [[swap_core(piece) for piece in stack] for stack in deep], all_rels)
    if not fast:
        plain, deep = deep, [None] * 4
        for i in (0, 1):
            mine, other = [stack[0].reshape(chips, 1, -1, half) for stack in (plain[i], plain[2 + i])]
            cut = by_core(core, mine, other, 1).reshape(BLOCKS, 2, -1, half)
            deep[i] = [jnp.where(core == 0, cut[:, 0], cut[:, 1]).reshape(-1, half)]
            deep[2 + i] = [jnp.where(core == 0, cut[:, 1], cut[:, 0]).reshape(-1, half)]

    w_qk, w_v, w_pos_half, query, key, value, probs, ctx_mine, ctx_send = attend_forward(
        meta, after(x2, *deep_sent), tables, bias, stack_qk, table_qk, stack_vp, table_vp, scale, head_dim
    )
    ctx_recv = swap_core(ctx_send)
    w_out_whole, gains, normed_one, normed_vals, inv_std, normed_low, sums = out_proj(
        meta, ctx_mine, ctx_recv, tokens_in, wide, ff
    )
    totals = jnp.sum(sums[:3], axis=1)
    act, act_grad = ffn_up(meta, normed_low, wide, ff)
    natural = list(range(BLOCKS))
    out_rels = tuple(all_rels) if fast else (natural, natural)
    output, grad_resid_two, grad_gains, grad_pre, deep_mine, deep_other = ffn_down(
        meta, act, act_grad, normed_one, gains, cotangent, deep, table_deep, out_rels
    )
    if not fast:
        mine, other = [grads.reshape(BLOCKS, 1, -1, width) for grads in (deep_mine, deep_other)]
        cut = by_core(core, mine, other, 1).reshape(chips, 2, -1, width)
        deep_mine = jnp.where(core == 0, cut[:, 0], cut[:, 1]).reshape(-1, width)
        deep_other = jnp.where(core == 0, cut[:, 1], cut[:, 0]).reshape(-1, width)

    def two_arrays(terms, cut):
        parts = [[term[:, :cut] for term in terms], [term[:, cut:] for term in terms]]
        parts = [[in_slots(term, rels, chip, fast) for term in part] for part, rels in zip(parts, all_rels)]
        return Scatter(parts, orders, z)

    s_deep = two_arrays([deep_mine, swap_core(deep_other)], half)
    grad_resid_one, grad_low, grad_ctx_mine, grad_ctx_send, all_gains = ffn_back(
        meta, grad_pre, w_out_whole, grad_resid_two, normed_vals, inv_std, gains, grad_gains, wide
    )
    grad_ctx_recv = swap_core(grad_ctx_send)
    token = s_deep.step(grad_low)
    hops = [(axis, 1 << bit) for axis, size in (("rep", rep), ("dp", dp)) for bit in range(size.bit_length() - 1)]

    def hop(total, *others):
        if not hops:
            return total
        axis, mask = hops.pop(0)
        total = after(total, *others)
        return total + swap(total, axis, mask)

    wide_mine, wide_other = weight_grads(
        meta, after(grad_pre, *token), normed_low, grad_low, all_gains, ctx_mine, ctx_recv, out_rels
    )
    s_wide = two_arrays([wide_mine, swap_core(wide_other)], UP_CHUNK)
    x2_t = x2.T

    def back_pair(pair, rels, *others):
        return attend_backward(
            meta, pair, x2_t, tables, query, key, value, w_pos_half, probs, after(grad_ctx_mine, *others), grad_ctx_recv,
            rels, scale, head_dim
        )

    pair_grads = [None] * 3
    pair_grads[0], pair_zero = back_pair(0, out_rels[:1], wide_mine)
    totals = hop(totals, pair_zero)
    token = s_wide.step(pair_zero)
    pair_grads[1], pair_one, pair_two = back_pair(1, out_rels, *token)
    totals = hop(totals, pair_one)
    token = s_deep.step(pair_one)
    pair_grads[2], pair_three = back_pair(2, out_rels[1:], *token)
    s_pair = Scatter(
        [
            [in_slots(jnp.concatenate(pieces, axis=1), rels, chip, fast)]
            for pieces, rels in zip(((pair_zero, pair_one), (pair_two, pair_three)), all_rels)
        ],
        orders,
        z,
    )
    totals = hop(totals, pair_three)
    token = s_wide.step(pair_three)
    grad_q, grad_k, grad_v = [
        jnp.concatenate([grads[:, i * LANES : (i + 1) * LANES] for grads in pair_grads], axis=1) for i in range(3)
    ]
    grad_x2 = dot_nt(after(jnp.concatenate([grad_q, grad_k], axis=1), *token), w_qk) + dot_nt(grad_v, w_v)
    grad_tokens = grad_resid_one + grad_x2[:row_len] + swap_core(grad_x2[row_len:])
    token = s_deep.step(*token)
    token = s_pair.step(*token)
    totals = hop(totals, *token)
    deep_sum = s_deep.finish(*token)
    token = s_wide.step(*token)
    token = s_pair.step(*token)
    totals = hop(totals, *token)
    while hops:
        totals = hop(totals)
    rms = jnp.sqrt(totals / (row_len * width * dp * rep))
    wide_sum = s_wide.finish(*token)
    pair_sum = s_pair.finish()

    def own_rows(values):
        rows = values.shape[0] // 2
        mine = jnp.where(core == 0, values[:rows], values[rows:])
        send = jnp.where(core == 0, values[rows:], values[:rows])
        return mine, swap_core(send)

    def sides(pieces, start, size):
        return by_core(core, pieces[0][:, start : start + size], pieces[1][:, start : start + size], 1)

    wide_rows = own_rows(wide_sum)
    pair_rows = own_rows(pair_sum)

    starts = [[0, 1, 2, 3], [4, 5, 6, 7], [8, 9, 10, 11]]

    def pair_columns(which):
        picked = [
            jnp.concatenate([rows[:, at[which] * LANES : (at[which] + 1) * LANES] for at in starts], axis=1)
            for rows in pair_rows
        ]
        return by_core(core, picked[0], picked[1], 1)

    gain_rows = sides(wide_rows, ff_half + half, LANES)
    return (
        output,
        grad_tokens,
        rms,
        jnp.concatenate([pair_columns(0), pair_columns(1), pair_columns(2)], axis=1),
        sides(wide_rows, ff_half, half),
        pair_columns(3),
        gain_rows[:, 0],
        gain_rows[:, 1],
        sides(wide_rows, 0, ff_half),
        deep_sum,
        gain_rows[:, LANES],
        gain_rows[:, LANES + 1],
    )


def solution(mesh):
    rows = P(("dp", "rep"), None)
    line = P(("dp", "rep"))
    in_specs = (rows, P(None, ("dp", "rep")), rows, rows, rows, rows, rows, line, line, rows, rows, line, line)
    out_specs = (rows, rows, P(), rows, rows, rows, line, line, rows, rows, line, line)
    return jax.shard_map(body, mesh=mesh, in_specs=in_specs, out_specs=out_specs, check_vma=False)
```

```python
from functools import partial
import math

import jax
import jax.numpy as jnp
import numpy as np
from jax import lax
from jax.experimental import pallas as pl
from jax.experimental.pallas import tpu as pltpu
from jax.sharding import PartitionSpec as P

HEADS = 12
FREQS = 192
BLOCKS = 16
LANES = 128
UP_CHUNK = 1024
COST_SCALE = 100.0

epsilon = 1e-05
masked_value = -1e30
f32 = jnp.float32
bf16 = jnp.bfloat16
VMEM_LIMIT = 48 * 1024 * 1024


def swap(values, axis, mask):
    size = lax.axis_size(axis)
    return lax.ppermute(values, axis, [(i, i ^ mask) for i in range(size)])


def swap_core(values):
    return swap(values, "rep", 1)


def tree_stages():
    dp, rep = lax.axis_size("dp"), lax.axis_size("rep")
    half = rep // 2
    y = [[("rep", 2 * k, k) for k in range(1, half)]] if half > 1 else []
    x = [[("dp", 1, half)]]
    z_wide, z_thin = [], []
    bit = 2
    while bit < dp:
        z_thin.insert(0, [("dp", bit, bit * half)])
        bit *= 2
    bit = 2
    while bit < dp:
        if 2 * bit < dp:
            z_wide.append([("dp", k * bit, k * bit * half) for k in (1, 2, 3)])
            bit *= 4
        else:
            z_wide.append([("dp", bit, bit * half)])
            bit *= 2
    return x, y, z_wide, z_thin


def slot_chips(stages):
    rels = [0]
    for stage in stages:
        rels = rels + [rel ^ chip for _, _, chip in stage for rel in rels]
    return rels


def after(value, *others):
    return lax.optimization_barrier((value,) + others)[0] if others else value


def hold(values, others):
    return list(lax.optimization_barrier(tuple(values) + tuple(others))[: len(values)]) if others else list(values)


def gather_first(block, stages, *others):
    stack = [after(block, *others)]
    for at, stage in enumerate(stages):
        whole = stack[0] if len(stack) == 1 else jnp.concatenate(stack, axis=0)
        stack = [whole] + [swap(whole, axis, mask) for axis, mask, _ in stage]
    return stack


def columns_of(stack, start, stop):
    return jnp.concatenate([piece[:, start:stop] for piece in stack], axis=0)


def gather_rest(stack, stages):
    for stage in stages:
        whole = stack[0] if len(stack) == 1 else jnp.concatenate(stack, axis=0)
        stack = [whole] + [swap(whole, axis, mask) for axis, mask, _ in stage]
    return stack


def add_up(terms):
    total = terms[0].astype(f32)
    for term in terms[1:]:
        total = total + term.astype(f32)
    return total


def split_rows(terms, parts):
    rows = terms[0].shape[0] // parts
    return [[term[i * rows : (i + 1) * rows] for term in terms] for i in range(parts)]


class Scatter:
    def __init__(self, arrays, orders, z):
        self.arrays = arrays
        self.fresh = [[] for _ in arrays]
        self.stages = [order[len(z) :][::-1] for order in orders]
        self.z = z[::-1]
        self.joined = False

    def load(self, *others):
        self.arrays = [kept + hold(fresh, others if fresh else ()) for kept, fresh in zip(self.arrays, self.fresh)]
        if not self.joined and not self.stages[0]:
            self.arrays = [[jnp.concatenate([add_up(terms) for terms in self.arrays], axis=1)]]
            self.stages = [self.z]
            self.joined = True
        self.now = [stages.pop(0) for stages in self.stages]
        self.chunks = [split_rows(terms, len(stage) + 1) for terms, stage in zip(self.arrays, self.now)]
        self.sends = [[add_up(chunk).astype(bf16) for chunk in chunks[1:]] for chunks in self.chunks]
        return [send for sends in self.sends for send in sends]

    def move(self):
        self.arrays = [chunks[0] for chunks in self.chunks]
        self.fresh = [
            [swap(send, axis, mask) for (axis, mask, _), send in zip(stage, sends)]
            for stage, sends in zip(self.now, self.sends)
        ]

    def received(self):
        return [array for fresh in self.fresh for array in fresh]

    def step(self, *others):
        sends = self.load(*others)
        self.move()
        return sends

    def finish(self, *others):
        while not self.joined or self.stages[0]:
            self.step(*others)
        return add_up(self.arrays[0] + self.fresh[0])


def natural_pieces(stack, rels, chip, fast):
    if fast:
        per = len(rels) // len(stack)
        return stack, [rels[i * per : (i + 1) * per] for i in range(len(stack))]
    whole = jnp.concatenate(stack, axis=0)
    count = len(rels)
    where = np.zeros(count, np.int32)
    for slot, rel in enumerate(rels):
        where[rel] = slot
    order = jnp.asarray(where)[chip ^ jnp.arange(count, dtype=jnp.int32)]
    whole = whole.reshape(count, whole.shape[0] // count, whole.shape[1])
    whole = jnp.take(whole, order, axis=0).reshape(-1, whole.shape[2])
    return [whole], [list(range(BLOCKS))]


def in_slots(whole, rels, chip, fast):
    if fast:
        return whole
    count = len(rels)
    whole = whole.reshape(count, whole.shape[0] // count, whole.shape[1])
    order = jnp.asarray(np.array(rels, np.int32)) ^ chip
    return jnp.take(whole, order, axis=0).reshape(-1, whole.shape[2])


def by_core(core, mine, other, axis):
    return jnp.where(
        core == 0,
        jnp.concatenate([mine, other], axis=axis),
        jnp.concatenate([other, mine], axis=axis),
    )


def pair_block(core, halves):
    mine = jnp.where(core == 0, halves[0], halves[1])
    send = jnp.where(core == 0, halves[1], halves[0])
    return by_core(core, mine, swap_core(send), 0)


def dot(left, right):
    return lax.dot_general(left, right, (((1,), (0,)), ((), ())), preferred_element_type=f32)


def dot_nt(left, right):
    return lax.dot_general(left, right, (((1,), (1,)), ((), ())), preferred_element_type=f32)


def run_copies(copies, sems):
    started = []
    for at, (source, target) in enumerate(copies):
        copy = pltpu.make_async_copy(source, target, sems.at[at])
        copy.start()
        started.append(copy)
    return started


def wait_all(started):
    for copy in started:
        copy.wait()


def slots_of(pieces, rels):
    return [(piece, at, rel) for piece, table in zip(pieces, rels) for at, rel in enumerate(table)]


def block_rows(index, size):
    return pl.ds(pl.multiple_of(index * size, size), size)


def pos_block(index):
    quarter, within = index // (BLOCKS // 4), index % (BLOCKS // 4)
    return ((quarter % 2) * 2 + quarter // 2) * (BLOCKS // 4) + within


def core_lanes(core, width):
    return pl.ds(pl.multiple_of(core * width, LANES), width)


def head_mask(shape, dim, which, head_dim, kind):
    place = lax.broadcasted_iota(jnp.int32, shape, dim)
    return ((place // head_dim) == which).astype(f32).astype(kind)


def attend_pairs(pairs, scale, head_dim, tables, bias, query, key, value, w_pos, probs, ctx_own, ctx_par, lhs, rhs):
    sin, cos, sin_t, cos_t, feats, feats_t = tables
    width = feats.shape[1]
    half = width // 2
    row_len = bias.shape[1]
    lhs[:, width : 2 * width] = feats[...]
    rhs[0:width, :] = feats_t[...]

    def one_pair(pair, carry):
        lanes = pl.ds(pl.multiple_of(pair * LANES, LANES), LANES)
        q_pair, k_pair, v_pair, w_pair = query[:, lanes], key[:, lanes], value[:, lanes], w_pos[:, lanes]
        rhs[2 * width : 2 * width + LANES, :] = k_pair.T
        mixed = [None, None]
        for which in (0, 1):
            lane_mask = head_mask((1, LANES), 1, which, head_dim, bf16)
            q_head = q_pair * lane_mask
            k_head = k_pair * lane_mask
            lhs[:, 2 * width :] = q_head
            for row in (0, 1):
                span = slice(row * row_len, (row + 1) * row_len)
                coeff = dot_nt(q_head[span], w_pair)
                along_sin, along_cos = coeff[:, :half], coeff[:, half:]
                sin_row, cos_row = sin[span, :], cos[span, :]
                lhs[span, 0:half] = (along_cos * sin_row - along_sin * cos_row).astype(bf16)
                lhs[span, half:width] = (along_sin * sin_row + along_cos * cos_row).astype(bf16)
                coeff = dot_nt(w_pair, k_head[span])
                along_sin, along_cos = coeff[:half], coeff[half:]
                sin_row, cos_row = sin_t[:, span], cos_t[:, span]
                rhs[width : width + half, span] = (along_cos * sin_row - along_sin * cos_row).astype(bf16)
                rhs[width + half : 2 * width, span] = (along_sin * sin_row + along_cos * cos_row).astype(bf16)
            for row in (0, 1):
                span = slice(row * row_len, (row + 1) * row_len)
                scores = dot(lhs[span, :], rhs[:, span]) * scale + bias[row]
                top = jnp.max(scores, axis=-1, keepdims=True)
                expo = jnp.exp(scores - top)
                prob = expo / jnp.sum(expo, axis=-1, keepdims=True)
                probs[pair - pairs[0], which * 2 + row] = prob
                piece = dot(prob.astype(bf16), v_pair[span] * lane_mask)
                mixed[row] = piece if mixed[row] is None else mixed[row] + piece
        ctx_own[:, lanes] = mixed[0].astype(bf16)
        ctx_par[:, lanes] = mixed[1].astype(bf16)
        return carry

    if pairs[1] - pairs[0] == 1:
        one_pair(pairs[0], 0)
    else:
        lax.fori_loop(pairs[0], pairs[1], one_pair, 0)


def attend_first_kernel(rels_one, rels_two, pairs, scale, head_dim, meta, x2, *refs):
    tables, bias, refs = refs[:6], refs[6], refs[7:]
    (pieces_one, pieces_two), refs = take_lists(refs, [len(rels_one), len(rels_two)])
    w_qk, w_v, w_pos, query, key, value, probs, ctx_own, ctx_par, lhs, rhs, sems = refs
    chip = meta[0]
    width = x2.shape[1]
    part = w_v.shape[1]
    rows = width // BLOCKS
    copies = []
    for piece, at, rel in slots_of(pieces_one, rels_one):
        copies.append((piece.at[pl.ds(at * rows, rows), :], w_qk.at[block_rows(chip ^ rel, rows), :]))
    for piece, at, rel in slots_of(pieces_two, rels_two):
        source = piece.at[pl.ds(at * rows, rows), :]
        copies.append((source.at[:, pl.ds(0, part)], w_v.at[block_rows(chip ^ rel, rows), :]))
        copies.append((source.at[:, pl.ds(part, part)], w_pos.at[block_rows(pos_block(chip ^ rel), rows), :]))
    wait_all(run_copies(copies, sems))
    query[...] = dot(x2[...], w_qk[:, 0:part]).astype(bf16)
    key[...] = dot(x2[...], w_qk[:, part:]).astype(bf16)
    value[...] = dot(x2[...], w_v[...]).astype(bf16)
    attend_pairs(pairs, scale, head_dim, tables, bias, query, key, value, w_pos, probs, ctx_own, ctx_par, lhs, rhs)


def attend_second_kernel(pairs, scale, head_dim, *refs):
    tables, bias, refs = refs[:6], refs[6], refs[7:]
    query, key, value, w_pos, own_before, par_before, probs, ctx_own, ctx_par, lhs, rhs = refs
    before = pairs[0] * LANES
    ctx_own[:, 0:before] = own_before[:, 0:before]
    ctx_par[:, 0:before] = par_before[:, 0:before]
    attend_pairs(pairs, scale, head_dim, tables, bias, query, key, value, w_pos, probs, ctx_own, ctx_par, lhs, rhs)


def take_lists(refs, sizes):
    taken = []
    for size in sizes:
        taken.append(refs[:size])
        refs = refs[size:]
    return taken, refs


def vmem_spec():
    return pl.BlockSpec(memory_space=pltpu.VMEM)


def any_spec():
    return pl.BlockSpec(memory_space=pl.ANY)


def smem_spec():
    return pl.BlockSpec(memory_space=pltpu.SMEM)


def params():
    return pltpu.CompilerParams(vmem_limit_bytes=VMEM_LIMIT)


def shape(dims, kind):
    return jax.ShapeDtypeStruct(dims, kind)


def cost(flops, moved):
    return pl.CostEstimate(flops=int(flops * COST_SCALE), bytes_accessed=int(moved * COST_SCALE), transcendentals=0)


def attend_first(meta, x2, tables, bias, stack_one, rels_one, stack_two, rels_two, pairs, scale, head_dim):
    tokens, width = x2.shape
    part = width // 2
    row_len = tokens // 2
    copies = sum(map(len, rels_one)) + 2 * sum(map(len, rels_two))
    return pl.pallas_call(
        partial(attend_first_kernel, rels_one, rels_two, pairs, scale, head_dim),
        out_shape=[
            shape((width, 2 * part), bf16),
            shape((width, part), bf16),
            shape((width, part), bf16),
            shape((tokens, part), bf16),
            shape((tokens, part), bf16),
            shape((tokens, part), bf16),
            shape((pairs[1] - pairs[0], 4, row_len, row_len), f32),
            shape((row_len, part), bf16),
            shape((row_len, part), bf16),
        ],
        in_specs=[smem_spec()] + [vmem_spec()] * 8 + [any_spec()] * (len(stack_one) + len(stack_two)),
        out_specs=[vmem_spec()] * 9,
        scratch_shapes=[
            pltpu.VMEM((tokens, 2 * width + LANES), bf16),
            pltpu.VMEM((2 * width + LANES, tokens), bf16),
            pltpu.SemaphoreType.DMA((copies,)),
        ],
        compiler_params=params(),
        cost_estimate=cost(2 * 1.0e9, 12e6),
        name="attend_first",
    )(meta, x2, *tables, bias, *stack_one, *stack_two)


def attend_second(tables, bias, query, key, value, w_pos, own_before, par_before, pairs, scale, head_dim):
    tokens, part = query.shape
    width = 2 * part
    row_len = tokens // 2
    return pl.pallas_call(
        partial(attend_second_kernel, pairs, scale, head_dim),
        out_shape=[
            shape((pairs[1] - pairs[0], 4, row_len, row_len), f32),
            shape((row_len, part), bf16),
            shape((row_len, part), bf16),
        ],
        in_specs=[vmem_spec()] * 13,
        out_specs=[vmem_spec()] * 3,
        scratch_shapes=[
            pltpu.VMEM((tokens, 2 * width + LANES), bf16),
            pltpu.VMEM((2 * width + LANES, tokens), bf16),
        ],
        compiler_params=params(),
        cost_estimate=cost(2 * 1.0e9, 12e6),
        name="attend_second",
    )(*tables, bias, query, key, value, w_pos, own_before, par_before)


def norm_values(values):
    centered = values - jnp.mean(values, axis=-1, keepdims=True)
    inv_std = lax.rsqrt(jnp.mean(centered * centered, axis=-1, keepdims=True) + epsilon)
    return centered * inv_std, inv_std


def norm_backward(grad, normed_vals, inv_std, gain):
    grad_normed = grad * gain
    centered_grad = grad_normed - jnp.mean(grad_normed, axis=-1, keepdims=True)
    return inv_std * (
        centered_grad - normed_vals * jnp.mean(grad_normed * normed_vals, axis=-1, keepdims=True)
    )


def out_proj_kernel(ff, meta, ctx_mine, ctx_recv, tokens, wide, w_out, gains, normed_one, normed_vals, inv_std, normed_low,
                    sums, gain_buf, sems):
    core = meta[1]
    width = tokens.shape[1]
    half = width // 2
    wait_all(
        run_copies(
            [(wide.at[:, pl.ds(ff, width)], w_out), (wide.at[:, pl.ds(ff + width, LANES)], gain_buf)], sems
        )
    )
    attn_out = dot(ctx_mine[...], w_out[block_rows(core, half), :])
    attn_out = attn_out + dot(ctx_recv[...], w_out[block_rows(1 - core, half), :])
    gain_t = gain_buf[...].astype(f32).T
    gains[...] = gain_t[0:8, :]
    tokens_f = tokens[...].astype(f32)
    resid = tokens_f + attn_out
    vals, inv = norm_values(resid)
    one = vals * gain_t[0:1, :] + gain_t[1:2, :]
    normed_one[...] = one
    normed_vals[...] = vals
    inv_std[...] = inv
    normed_low[...] = one.astype(bf16)
    sums[0:1, :] = jnp.sum(tokens_f * tokens_f, axis=0, keepdims=True)
    sums[1:2, :] = jnp.sum(attn_out * attn_out, axis=0, keepdims=True)
    sums[2:3, :] = jnp.sum(resid * resid, axis=0, keepdims=True)
    sums[3:8, :] = jnp.zeros((5, width), f32)


def out_proj(meta, ctx_mine, ctx_recv, tokens, wide, ff):
    count, width = tokens.shape
    return pl.pallas_call(
        partial(out_proj_kernel, ff),
        out_shape=[
            shape((width, width), bf16),
            shape((8, width), f32),
            shape((count, width), f32),
            shape((count, width), f32),
            shape((count, 1), f32),
            shape((count, width), bf16),
            shape((8, width), f32),
        ],
        in_specs=[smem_spec()] + [vmem_spec()] * 3 + [any_spec()],
        out_specs=[vmem_spec()] * 7,
        scratch_shapes=[pltpu.VMEM((width, LANES), bf16), pltpu.SemaphoreType.DMA((2,))],
        compiler_params=params(),
        cost_estimate=cost(2 * 0.15e9, 5e6),
        name="out_proj",
    )(meta, ctx_mine, ctx_recv, tokens, wide)


def tile_copies(wide, w_up, tile):
    return [(wide.at[:, pl.ds(at, tile)], w_up.at[:, pl.ds(at, tile)]) for at in range(0, w_up.shape[1], tile)]


def ffn_kernel(rels, out_rels, tile, meta, normed_low, normed_one, gains, cotangent, wide, *refs):
    pieces, refs = take_lists(refs, [len(rels[0]), len(rels[1])] * 2)
    output, grad_resid, grad_gains, grad_pre, grad_mine, grad_other = refs[:6]
    w_up, w_down, act, act_grad, act_t, ordered, low, grad_buf, up_sems, down_sems, out_sems = refs[6:]
    chip, core = meta[0], meta[1]
    ff, width = w_down.shape
    half = width // 2
    rows = ff // BLOCKS // 2
    started_up = run_copies(tile_copies(wide, w_up, tile), up_sems)
    copies = []
    for side, chunks in ((core, pieces[:2]), (1 - core, pieces[2:])):
        for i in (0, 1):
            for piece, at, rel in slots_of(chunks[i], rels[i]):
                copies.append(
                    (
                        piece.at[pl.ds(at * rows, rows), :],
                        w_down.at[block_rows((chip ^ rel) * 2 + side, rows), pl.ds(i * half, half)],
                    )
                )
    started_down = run_copies(copies, down_sems)
    for at, copy in enumerate(started_up):
        copy.wait()
        lanes = pl.ds(at * tile, tile)
        pre = dot(normed_low[...], w_up[:, lanes])
        bell = 0.5 * (1.0 + lax.erf(pre * (0.5**0.5)))
        low_act = (pre * bell).astype(bf16)
        act[:, lanes] = low_act
        act_t[lanes, :] = low_act.T
        act_grad[:, lanes] = bell + pre * jnp.exp(pre * pre * -0.5) * (0.5 / math.pi) ** 0.5
    wait_all(started_down)
    vals, inv = norm_values(normed_one[...] + dot(act[...], w_down[...]))
    gain, shift = gains[2:3, :], gains[3:4, :]
    output[...] = (vals * gain + shift).astype(bf16)
    grad = cotangent[...].astype(f32)
    grad_gains[0:1, :] = jnp.sum(grad * vals, axis=0, keepdims=True)
    grad_gains[1:2, :] = jnp.sum(grad, axis=0, keepdims=True)
    grad_gains[2:8, :] = jnp.zeros((6, width), f32)
    resid = norm_backward(grad, vals, inv, gain)
    grad_resid[...] = resid
    low[...] = resid.astype(bf16)
    flushed = []
    for target, place in ((grad_other, 1 - core), (grad_mine, core)):
        for i in (0, 1):
            at = len(flushed)
            for slot, rel in enumerate(out_rels[i]):
                ordered[slot * rows : (slot + 1) * rows, :] = act_t[block_rows((chip ^ rel) * 2 + place, rows), :]
            grad_buf[at] = dot(ordered[...], low[:, i * half : (i + 1) * half]).astype(bf16)
            copy = pltpu.make_async_copy(grad_buf.at[at], target.at[:, pl.ds(i * half, half)], out_sems.at[at])
            copy.start()
            flushed.append(copy)

    def one_tile(at, carry):
        lanes = pl.ds(pl.multiple_of(at * tile, tile), tile)
        grad_pre[:, lanes] = (dot_nt(low[...], w_down[lanes, :]) * act_grad[:, lanes]).astype(bf16)
        return carry

    lax.fori_loop(0, ff // tile, one_tile, 0)
    wait_all(flushed)


def ffn(meta, normed_low, normed_one, gains, cotangent, wide, pieces, rels, out_rels, ff):
    count, width = normed_one.shape
    tile = 512
    flat = [array for chunk in pieces for array in chunk]
    return pl.pallas_call(
        partial(ffn_kernel, rels, out_rels, tile),
        out_shape=[
            shape((count, width), bf16),
            shape((count, width), f32),
            shape((8, width), f32),
            shape((count, ff), bf16),
        ]
        + [shape((ff // 2, width), bf16)] * 2,
        in_specs=[smem_spec()] + [vmem_spec()] * 4 + [any_spec()] * (1 + len(flat)),
        out_specs=[vmem_spec()] * 4 + [any_spec()] * 2,
        scratch_shapes=[
            pltpu.VMEM((width, ff), bf16),
            pltpu.VMEM((ff, width), bf16),
            pltpu.VMEM((count, ff), bf16),
            pltpu.VMEM((count, ff), f32),
            pltpu.VMEM((ff, count), bf16),
            pltpu.VMEM((ff // 2, count), bf16),
            pltpu.VMEM((count, width), bf16),
            pltpu.VMEM((4, ff // 2, width // 2), bf16),
            pltpu.SemaphoreType.DMA((ff // tile,)),
            pltpu.SemaphoreType.DMA((2 * sum(map(len, rels[0] + rels[1])),)),
            pltpu.SemaphoreType.DMA((4,)),
        ],
        compiler_params=params(),
        cost_estimate=cost(2 * 2.4e9, 25e6),
        name="ffn",
    )(meta, normed_low, normed_one, gains, cotangent, wide, *flat)


def permute_rows(source, target, chip, out_rels):
    rows = source.shape[0] // BLOCKS
    for slot, rel in enumerate(out_rels):
        target[slot * rows : (slot + 1) * rows, :] = source[block_rows(chip ^ rel, rows), :]


def ffn_back_kernel(
    tile, meta, grad_pre, w_out, grad_resid_two, normed_vals, inv_std, gains, grad_gains, wide, grad_resid, low,
    grad_ctx_mine, grad_ctx_send, all_gains, w_up, sems
):
    core = meta[1]
    width = w_up.shape[0]
    half = width // 2
    started = run_copies(tile_copies(wide, w_up, tile), sems)
    grad = grad_resid_two[...]
    for at, copy in enumerate(started):
        copy.wait()
        lanes = pl.ds(at * tile, tile)
        grad = grad + dot_nt(grad_pre[:, lanes], w_up[:, lanes])
    vals = normed_vals[...]
    resid = norm_backward(grad, vals, inv_std[...], gains[0:1, :])
    grad_resid[...] = resid
    low[...] = resid.astype(bf16)
    grad_ctx_mine[...] = dot_nt(low[...], w_out[block_rows(core, half), :]).astype(bf16)
    grad_ctx_send[...] = dot_nt(low[...], w_out[block_rows(1 - core, half), :]).astype(bf16)
    all_gains[0:1, :] = jnp.sum(grad * vals, axis=0, keepdims=True)
    all_gains[1:2, :] = jnp.sum(grad, axis=0, keepdims=True)
    all_gains[2:4, :] = grad_gains[0:2, :]
    all_gains[4:8, :] = jnp.zeros((4, width), f32)


def ffn_back(meta, grad_pre, w_out, grad_resid_two, normed_vals, inv_std, gains, grad_gains, wide):
    count, ff = grad_pre.shape
    width = w_out.shape[0]
    half = width // 2
    tile = 1024
    return pl.pallas_call(
        partial(ffn_back_kernel, tile),
        out_shape=[
            shape((count, width), f32),
            shape((count, width), bf16),
            shape((count, half), bf16),
            shape((count, half), bf16),
            shape((8, width), f32),
        ],
        in_specs=[smem_spec()] + [vmem_spec()] * 7 + [any_spec()],
        out_specs=[vmem_spec()] * 5,
        scratch_shapes=[pltpu.VMEM((width, ff), bf16), pltpu.SemaphoreType.DMA((ff // tile,))],
        compiler_params=params(),
        cost_estimate=cost(2 * 0.8e9, 10e6),
        name="ffn_back",
    )(meta, grad_pre, w_out, grad_resid_two, normed_vals, inv_std, gains, grad_gains, wide)


def digit_scales(devices):
    base = 1 << ((256 // devices + 1).bit_length() - 1)
    if base < 8:
        return None
    exponents = np.full((2 * LANES, 1), 126.0)
    for half in (0, 1):
        for row in range(2, LANES):
            exponents[half * LANES + row, 0] = 123 - 3 * ((row - 2) % 42 + 42 * half)
    return np.exp2(exponents).astype(np.float32)


def digits_of(sums, places):
    row = lax.broadcasted_iota(jnp.int32, (LANES, 1), 0)
    totals = [jnp.sum(sums[i : i + 1, :], axis=1, keepdims=True) for i in range(3)]
    value = jnp.where(row < 44, totals[0], jnp.where(row < 86, totals[1], totals[2]))
    whole = jnp.floor(jnp.minimum(value / places, 2.0**30))
    return whole - 8.0 * jnp.floor(whole * 0.125)


def weight_grads_kernel(
    out_rels, tile, meta, grad_pre, normed_low, low, all_gains, ctx_mine, ctx_recv, sums, places, *refs
):
    grads, (turned, ordered_one, ordered_two, gain_buf) = refs[:2], refs[2:]
    chip, core = meta[0], meta[1]
    width, ff = turned.shape[0], grad_pre.shape[1]
    half, ff_half = width // 2, ff // 2
    rows = width // BLOCKS
    turned[...] = normed_low[...].T
    permute_rows(turned, ordered_one, chip, out_rels[0])
    permute_rows(turned, ordered_two, chip, out_rels[1])
    rest = ff_half - UP_CHUNK
    for grad, place in ((grads[0], core), (grads[1], 1 - core)):

        def one_tile(at, carry, grad=grad, place=place):
            lanes = pl.ds(pl.multiple_of(place * ff_half + at * tile, tile), tile)
            target = pl.ds(pl.multiple_of(at * tile, tile), tile)
            grad[:, target] = dot(ordered_one[...], grad_pre[:, lanes]).astype(bf16)
            return carry

        lax.fori_loop(0, UP_CHUNK // tile, one_tile, 0)
        lanes = pl.ds(pl.multiple_of(place * ff_half + UP_CHUNK, LANES), rest)
        grad[:, UP_CHUNK:ff_half] = dot(ordered_two[...], grad_pre[:, lanes]).astype(bf16)
    turned[block_rows(core, half), :] = ctx_mine[...].T
    turned[block_rows(1 - core, half), :] = ctx_recv[...].T
    permute_rows(turned, ordered_two, chip, out_rels[1])
    first, second = all_gains[0:2, :], all_gains[2:4, :]
    at_first = (core == 0).astype(f32)
    pair = (first * at_first + second * (1.0 - at_first), first * (1.0 - at_first) + second * at_first)
    for side, place in ((0, core), (1, 1 - core)):
        grad = grads[side]
        grad[:, ff_half : ff_half + half] = dot(ordered_two[...], low[:, core_lanes(place, half)]).astype(bf16)
        digits = digits_of(sums[...], places[block_rows(place, LANES), :])[2:]
        padded = jnp.concatenate([pair[side], jnp.broadcast_to(digits, (LANES - 2, width))], axis=0)
        gain_buf[...] = padded.T.astype(bf16)
        for slot, rel in enumerate(out_rels[1]):
            grad[slot * rows : (slot + 1) * rows, ff_half + half :] = gain_buf[block_rows(chip ^ rel, rows), :]


def weight_grads(meta, grad_pre, normed_low, low, all_gains, ctx_mine, ctx_recv, sums, places, out_rels):
    count, ff = grad_pre.shape
    width = normed_low.shape[1]
    return pl.pallas_call(
        partial(weight_grads_kernel, out_rels, 512),
        out_shape=[shape((width, ff // 2 + width // 2 + LANES), bf16)] * 2,
        in_specs=[smem_spec()] + [vmem_spec()] * 8,
        out_specs=[vmem_spec()] * 2,
        scratch_shapes=[pltpu.VMEM((width, count), bf16)] * 3 + [pltpu.VMEM((width, LANES), bf16)],
        compiler_params=params(),
        cost_estimate=cost(2 * 0.8e9, 10e6),
        name="weight_grads",
    )(meta, grad_pre, normed_low, low, all_gains, ctx_mine, ctx_recv, sums, places)


def attend_backward_kernel(
    out_rels, split, scale, head_dim, meta, x2_t, sin, cos, sin_t, cos_t, feats, feats_t, query, key, value, w_pos, probs,
    grad_own, grad_par, grad_qkv, *refs
):
    outs, refs = (refs[:2], refs[2:]) if split else (refs[:1], refs[1:])
    grad_ctx, coeff_q, coeff_k, x2_rel, pos_buf = refs
    chip = meta[0]
    tokens, width = feats.shape
    row_len = tokens // 2
    half = width // 2
    grad_ctx[0:row_len, :] = grad_own[...]
    grad_ctx[row_len:, :] = grad_par[...]
    q_pair, k_pair, v_pair, w_pair, g_pair = query[...], key[...], value[...], w_pos[...], grad_ctx[...]
    q_t, v_t, g_t, w_t = q_pair.T, v_pair.T, g_pair.T, w_pair.T
    grad_q = [None, None]
    grad_k = [None, None]
    grad_v = [None, None]

    def plus(total, term):
        return term if total is None else total + term

    grad_q_coeff = None
    grad_k_coeff = None
    pos_q = None
    pos_k = None
    for which in (0, 1):
        lane_mask = head_mask((1, LANES), 1, which, head_dim, bf16)
        row_mask = head_mask((LANES, 1), 0, which, head_dim, bf16)
        k_head, g_head, w_head = k_pair * lane_mask, g_pair * lane_mask, w_pair * lane_mask
        q_t_head, g_t_head, w_t_head = q_t * row_mask, g_t * row_mask, w_t * row_mask
        for row in (0, 1):
            span = slice(row * row_len, (row + 1) * row_len)
            prob = probs[0, which * 2 + row]
            grad_probs = dot(g_head[span], v_t[:, span])
            inner = jnp.sum(prob * grad_probs, axis=-1, keepdims=True)
            grad_scores = (prob * (grad_probs - inner) * scale).astype(bf16)
            grad_v[row] = plus(grad_v[row], dot(g_t_head[:, span], prob.astype(bf16)))
            grad_k[row] = plus(grad_k[row], dot(q_t_head[:, span], grad_scores))
            grad_q[row] = plus(grad_q[row], dot(grad_scores, k_head[span]))
            pos = dot(grad_scores, feats[span, :])
            first, second = pos[:, :half], pos[:, half:]
            sin_row, cos_row = sin[span, :], cos[span, :]
            coeff_q[span, 0:half] = (second * sin_row - first * cos_row).astype(bf16)
            coeff_q[span, half:] = (first * sin_row + second * cos_row).astype(bf16)
            pos = dot(feats_t[:, span], grad_scores)
            first, second = pos[:half], pos[half:]
            sin_row, cos_row = sin_t[:, span], cos_t[:, span]
            coeff_k[0:half, span] = (second * sin_row - first * cos_row).astype(bf16)
            coeff_k[half:, span] = (first * sin_row + second * cos_row).astype(bf16)
        grad_q_coeff = plus(grad_q_coeff, dot(coeff_q[...], w_head))
        grad_k_coeff = plus(grad_k_coeff, dot(w_t_head, coeff_k[...]))
        pos_q = plus(pos_q, dot(q_t_head, coeff_q[...]))
        pos_k = plus(pos_k, dot(coeff_k[...], k_head))
    d_q = (jnp.concatenate(grad_q, axis=0) + grad_q_coeff).astype(bf16)
    d_k = (jnp.concatenate(grad_k, axis=1) + grad_k_coeff).astype(bf16).T
    d_v = jnp.concatenate(grad_v, axis=1).astype(bf16).T
    grad_qkv[:, 0:LANES] = d_q
    grad_qkv[:, LANES : 2 * LANES] = d_k
    grad_qkv[:, 2 * LANES :] = d_v
    pos_buf[...] = (pos_k + pos_q.T).astype(bf16)
    rows = width // BLOCKS
    cuts = (0, 2 * LANES, 3 * LANES) if split else (0, 3 * LANES)
    for at, out in enumerate(outs):
        size = cuts[at + 1] - cuts[at]
        permute_rows(x2_t, x2_rel, chip, out_rels[at])
        out[:, 0:size] = dot(x2_rel[...], grad_qkv[:, cuts[at] : cuts[at + 1]]).astype(bf16)
    for slot, rel in enumerate(out_rels[-1]):
        outs[-1][slot * rows : (slot + 1) * rows, size:] = pos_buf[block_rows(pos_block(chip ^ rel), rows), :]


def attend_backward(
    meta, pair, x2_t, tables, query, key, value, w_pos, probs, place, grad_own, grad_par, out_rels, scale, head_dim
):
    width, tokens = x2_t.shape
    row_len = tokens // 2

    def whole(array):
        return pl.BlockSpec(array.shape, lambda i: (0,) * array.ndim)

    def columns(rows):
        return pl.BlockSpec((rows, LANES), lambda i: (0, pair))

    split = len(out_rels) > 1
    pieces = [shape((width, (2 if split else 4) * LANES), bf16)] * (2 if split else 1)
    return pl.pallas_call(
        partial(attend_backward_kernel, out_rels, split, scale, head_dim),
        grid=(1,),
        out_shape=[shape((tokens, 3 * LANES), bf16)] + pieces,
        in_specs=[smem_spec(), whole(x2_t)]
        + [whole(table) for table in tables]
        + [columns(tokens)] * 3
        + [columns(width), pl.BlockSpec((1, 4, row_len, row_len), lambda i: (place, 0, 0, 0))]
        + [columns(row_len)] * 2,
        out_specs=[pl.BlockSpec((tokens, 3 * LANES), lambda i: (0, 0))]
        + [pl.BlockSpec(piece.shape, lambda i: (0, 0)) for piece in pieces],
        scratch_shapes=[
            pltpu.VMEM((tokens, LANES), bf16),
            pltpu.VMEM((tokens, width), bf16),
            pltpu.VMEM((width, tokens), bf16),
            pltpu.VMEM((width, tokens), bf16),
            pltpu.VMEM((width, LANES), bf16),
        ],
        compiler_params=params(),
        cost_estimate=cost(2 * 1.3e9, 10e6),
        name="attend_backward",
    )(meta, x2_t, *tables, query, key, value, w_pos, probs, grad_own, grad_par)


def row_tables(boxes):
    rates = jnp.exp(jnp.arange(FREQS, dtype=f32) * (-math.log(10000.0) / FREQS))
    angles = boxes.astype(f32)[:, :, None] * rates[None, None, :]
    angles = jnp.transpose(angles, (1, 0, 2)).reshape(boxes.shape[1], 2 * FREQS)
    sin, cos = jnp.sin(angles), jnp.cos(angles)
    feats = jnp.concatenate([sin, cos], axis=1).astype(bf16)
    return sin, cos, sin.T, cos.T, feats, feats.T


def body(
    tokens_in, boxes, page_lengths, cotangent, w_qkv, w_out, w_pos, gain_attn, bias_attn, w_up, w_down, gain_ffn, bias_ffn
):
    row_len, width = tokens_in.shape
    ff = w_up.shape[1]
    half, ff_half = width // 2, ff // 2
    head_dim = width // HEADS
    scale = head_dim ** (-0.5)
    dp, rep = lax.axis_size("dp"), lax.axis_size("rep")
    chips = dp * rep // 2
    core = lax.axis_index("rep") % 2
    chip = lax.axis_index("dp") * (rep // 2) + lax.axis_index("rep") // 2
    fast = chips == BLOCKS
    meta = jnp.stack([chip if fast else 0 * chip, core]).astype(jnp.int32)
    gains_in = jnp.stack([gain_attn, bias_attn, gain_ffn, bias_ffn], axis=1)
    pad = jnp.zeros((w_up.shape[0], LANES - 4), bf16)
    wide = lax.all_gather(jnp.concatenate([w_up, w_out, gains_in, pad], axis=1), ("dp", "rep"), axis=0, tiled=True)

    x, y, z_wide, z = tree_stages()
    heads_orders = (z_wide + x + y, z_wide + y + x)
    orders = (z + x + y, z + y + x)
    heads_rels = [slot_chips(order) for order in heads_orders]
    all_rels = [slot_chips(order) for order in orders]

    def split_columns(stack, cut, *others):
        stack = hold(stack, others)
        return [[columns_of(stack, 0, cut)], [columns_of(stack, cut, stack[0].shape[1])]]

    def move(stacks, stages, *others):
        moved = []
        for stack, stage in zip(stacks, stages):
            stack = stack[:1] + hold(stack[1:], others if len(stack) > 1 else ())
            whole = stack[0] if len(stack) == 1 else jnp.concatenate(stack, axis=0)
            moved.append([whole] + [swap(whole, axis, mask) for axis, mask, _ in stage])
        return moved

    def sent(stacks):
        return [stack[0] for stack in stacks]

    def came(stacks):
        return [piece for stack in stacks for piece in stack[1:]]

    def heads_half(side):
        parts = [w_qkv[:, at * width + side * half : at * width + (side + 1) * half] for at in range(3)]
        return jnp.concatenate(parts + [w_pos[:, side * half : (side + 1) * half]], axis=1)

    heads_block = pair_block(core, [heads_half(s) for s in (0, 1)])
    heads_z = gather_first(heads_block, z_wide)
    x2 = jnp.concatenate([tokens_in, swap_core(after(tokens_in, heads_block))], axis=0)
    ends = jnp.cumsum(page_lengths, axis=1)
    places = jnp.arange(row_len, dtype=jnp.int32)
    segment = jnp.sum((places[None, :, None] >= ends[:, None, :]).astype(jnp.int32), axis=2)
    marks = after(jnp.concatenate([boxes, segment], axis=0), heads_block)
    marks_other = swap_core(marks)
    segments = jnp.stack([marks[2], marks_other[2]])
    bias = jnp.where(segments[:, :, None] == segments[:, None, :], 0.0, masked_value).astype(f32)
    tables = row_tables(jnp.concatenate([marks[:2], marks_other[:2]], axis=1))

    heads = move(split_columns(heads_z, width), (x[0], y[0]))
    deep_z = gather_first(w_down, z[:-1], *sent(heads))
    heads = move(heads, (y[0], x[0]), *deep_z[1:])
    deep_z = gather_first(jnp.concatenate(deep_z[:1] + hold(deep_z[1:], sent(heads)), axis=0), z[-1:])
    deep = move(split_columns(deep_z[:1] + hold(deep_z[1:], came(heads)), half), (x[0], y[0]))

    def tabled(stacks, rels):
        done = [natural_pieces(stack, table, chip, fast) for stack, table in zip(stacks, rels * 2)]
        return [pieces for pieces, _ in done], [table for _, table in done[:2]]

    (stack_qk, stack_vp), (table_qk, table_vp) = tabled(heads, heads_rels)
    first_pairs, last_pairs = (0, 1), (1, half // LANES)
    w_qk, w_v, w_pos_half, query, key, value, probs_first, own_first, par_first = attend_first(
        meta, after(x2, *sent(deep)), tables, bias, stack_qk, table_qk, stack_vp, table_vp, first_pairs, scale, head_dim
    )
    deep = move(deep, (y[0], x[0]), own_first)
    deep_sent = sent(deep)
    deep, table_deep = tabled(deep + [[swap_core(piece) for piece in stack] for stack in deep], all_rels)
    if not fast:
        plain, deep = deep, [None] * 4
        for i in (0, 1):
            mine, other = [stack[0].reshape(chips, 1, -1, half) for stack in (plain[i], plain[2 + i])]
            cut = by_core(core, mine, other, 1).reshape(BLOCKS, 2, -1, half)
            deep[i] = [jnp.where(core == 0, cut[:, 0], cut[:, 1]).reshape(-1, half)]
            deep[2 + i] = [jnp.where(core == 0, cut[:, 1], cut[:, 0]).reshape(-1, half)]

    probs_last, ctx_mine, ctx_send = attend_second(
        tables, bias, after(query, *deep_sent), key, value, w_pos_half, own_first, par_first, last_pairs, scale, head_dim
    )
    ctx_recv = swap_core(ctx_send)
    w_out_whole, gains, normed_one, normed_vals, inv_std, normed_low, sums = out_proj(
        meta, ctx_mine, ctx_recv, tokens_in, wide, ff
    )
    natural = list(range(BLOCKS))
    out_rels = tuple(all_rels) if fast else (natural, natural)
    output, grad_resid_two, grad_gains, grad_pre, deep_mine, deep_other = ffn(
        meta, normed_low, normed_one, gains, cotangent, wide, deep, table_deep, out_rels, ff
    )
    if not fast:
        mine, other = [grads.reshape(BLOCKS, 1, -1, width) for grads in (deep_mine, deep_other)]
        cut = by_core(core, mine, other, 1).reshape(chips, 2, -1, width)
        deep_mine = jnp.where(core == 0, cut[:, 0], cut[:, 1]).reshape(-1, width)
        deep_other = jnp.where(core == 0, cut[:, 1], cut[:, 0]).reshape(-1, width)

    def two_arrays(terms, cut):
        parts = [[term[:, :cut] for term in terms], [term[:, cut:] for term in terms]]
        parts = [[in_slots(term, rels, chip, fast) for term in part] for part, rels in zip(parts, all_rels)]
        return Scatter(parts, orders, z)

    places = digit_scales(dp * rep)
    deep_core = swap_core(deep_other)
    grad_resid_one, grad_low, grad_ctx_mine, grad_ctx_send, all_gains = ffn_back(
        meta, grad_pre, w_out_whole, grad_resid_two, normed_vals, inv_std, gains, grad_gains, wide
    )
    grad_ctx_recv = swap_core(grad_ctx_send)
    s_deep = two_arrays([deep_mine, after(deep_core, grad_low)], half)
    token = s_deep.step()
    wide_mine, wide_other = weight_grads(
        meta, after(grad_pre, *token), normed_low, grad_low, all_gains, ctx_mine, ctx_recv, sums,
        jnp.ones((2 * LANES, 1), f32) if places is None else jnp.asarray(places), out_rels
    )
    wide_core = swap_core(wide_other)
    x2_t = x2.T

    def back_pair(pair, rels, *others):
        probs, place = (probs_first, pair) if pair < first_pairs[1] else (probs_last, pair - first_pairs[1])
        return attend_backward(
            meta, pair, x2_t, tables, query, key, value, w_pos_half, probs, place, after(grad_ctx_mine, *others),
            grad_ctx_recv, rels, scale, head_dim
        )

    pair_grads = [None] * 3
    pair_grads[0], pair_zero = back_pair(0, out_rels[:1], wide_mine)
    token = s_deep.step(pair_zero)
    s_wide = two_arrays([wide_mine, after(wide_core, *token)], UP_CHUNK)
    token = s_wide.step()
    pair_grads[1], pair_one, pair_two = back_pair(1, out_rels, *token)
    pair_grads[2], pair_three = back_pair(2, out_rels[1:], pair_one)
    s_pair = Scatter(
        [
            [in_slots(jnp.concatenate(pieces, axis=1), rels, chip, fast)]
            for pieces, rels in zip(((pair_zero, pair_one), (pair_two, pair_three)), all_rels)
        ],
        orders,
        z,
    )
    token = s_deep.step(pair_three)
    token = s_wide.step(*token)
    grad_q, grad_k, grad_v = [
        jnp.concatenate([grads[:, i * LANES : (i + 1) * LANES] for grads in pair_grads], axis=1) for i in range(3)
    ]
    grad_x2 = dot_nt(after(jnp.concatenate([grad_q, grad_k], axis=1), *token), w_qk) + dot_nt(grad_v, w_v)
    grad_tokens = grad_resid_one + grad_x2[:row_len] + swap_core(grad_x2[row_len:])
    deep_sum = s_deep.finish(*token)
    token = s_pair.step(*token)
    token = s_wide.step(*token)
    token = s_pair.step(*token)
    wide_sum = s_wide.finish(*token)
    pair_sum = s_pair.finish()
    wide_sum = s_wide.finish(*token)
    pair_sum = s_pair.finish()

    def own_rows(values):
        rows = values.shape[0] // 2
        mine = jnp.where(core == 0, values[:rows], values[rows:])
        send = jnp.where(core == 0, values[rows:], values[:rows])
        return mine, swap_core(send)

    def sides(pieces, start, size):
        return by_core(core, pieces[0][:, start : start + size], pieces[1][:, start : start + size], 1)

    wide_rows = own_rows(wide_sum)
    pair_rows = own_rows(pair_sum)

    starts = [[0, 1, 2, 3], [4, 5, 6, 7], [8, 9, 10, 11]]

    def pair_columns(which):
        picked = [
            jnp.concatenate([rows[:, at[which] * LANES : (at[which] + 1) * LANES] for at in starts], axis=1)
            for rows in pair_rows
        ]
        return by_core(core, picked[0], picked[1], 1)

    gain_rows = sides(wide_rows, ff_half + half, LANES)
    if places is None:
        totals = after(jnp.sum(sums[:3], axis=1), pair_sum)
        for axis, size in (("rep", rep), ("dp", dp)):
            for bit in range(size.bit_length() - 1):
                totals = totals + swap(totals, axis, 1 << bit)
    else:
        parts = gain_rows[0].reshape(2, LANES) * jnp.asarray(places).reshape(2, LANES)
        totals = jnp.sum(jnp.transpose(parts[:, 2:].reshape(2, 3, 42), (1, 0, 2)).reshape(3, 84), axis=1)
    rms = jnp.sqrt(totals / (row_len * width * dp * rep))
    return (
        output,
        grad_tokens,
        rms,
        jnp.concatenate([pair_columns(0), pair_columns(1), pair_columns(2)], axis=1),
        sides(wide_rows, ff_half, half),
        pair_columns(3),
        gain_rows[:, 0],
        gain_rows[:, 1],
        sides(wide_rows, 0, ff_half),
        deep_sum,
        gain_rows[:, LANES],
        gain_rows[:, LANES + 1],
    )


def solution(mesh):
    rows = P(("dp", "rep"), None)
    line = P(("dp", "rep"))
    in_specs = (rows, P(None, ("dp", "rep")), rows, rows, rows, rows, rows, line, line, rows, rows, line, line)
    out_specs = (rows, rows, P(), rows, rows, rows, line, line, rows, rows, line, line)
    return jax.shard_map(body, mesh=mesh, in_specs=in_specs, out_specs=out_specs, check_vma=False)
```

```python
from functools import partial
import math

import jax
import jax.numpy as jnp
import numpy as np
from jax import lax
from jax.experimental import pallas as pl
from jax.experimental.pallas import tpu as pltpu
from jax.sharding import PartitionSpec as P

HEADS = 12
FREQS = 192
BLOCKS = 16
LANES = 128
UP_CHUNK = 1024
COST_SCALE = 100.0
ATTEND_SCALE = 5.0
BACK_SCALES = (100.0, 100.0, 100.0)

epsilon = 1e-05
masked_value = -1e30
f32 = jnp.float32
bf16 = jnp.bfloat16
VMEM_LIMIT = 48 * 1024 * 1024


def swap(values, axis, mask):
    size = lax.axis_size(axis)
    return lax.ppermute(values, axis, [(i, i ^ mask) for i in range(size)])


def swap_core(values):
    return swap(values, "rep", 1)


def tree_stages():
    dp, rep = lax.axis_size("dp"), lax.axis_size("rep")
    half = rep // 2
    y = [[("rep", 2 * k, k) for k in range(1, half)]] if half > 1 else []
    x = [[("dp", 1, half)]]
    z_wide, z_thin = [], []
    bit = 2
    while bit < dp:
        z_thin.insert(0, [("dp", bit, bit * half)])
        bit *= 2
    bit = 2
    while bit < dp:
        if 2 * bit < dp:
            z_wide.append([("dp", k * bit, k * bit * half) for k in (1, 2, 3)])
            bit *= 4
        else:
            z_wide.append([("dp", bit, bit * half)])
            bit *= 2
    return x, y, z_wide, z_thin


def slot_chips(stages):
    rels = [0]
    for stage in stages:
        rels = rels + [rel ^ chip for _, _, chip in stage for rel in rels]
    return rels


def after(value, *others):
    return lax.optimization_barrier((value,) + others)[0] if others else value


def hold(values, others):
    return list(lax.optimization_barrier(tuple(values) + tuple(others))[: len(values)]) if others else list(values)


def gather_first(block, stages, *others):
    stack = [after(block, *others)]
    for at, stage in enumerate(stages):
        whole = stack[0] if len(stack) == 1 else jnp.concatenate(stack, axis=0)
        stack = [whole] + [swap(whole, axis, mask) for axis, mask, _ in stage]
    return stack


def columns_of(stack, start, stop):
    return jnp.concatenate([piece[:, start:stop] for piece in stack], axis=0)


def gather_rest(stack, stages):
    for stage in stages:
        whole = stack[0] if len(stack) == 1 else jnp.concatenate(stack, axis=0)
        stack = [whole] + [swap(whole, axis, mask) for axis, mask, _ in stage]
    return stack


def add_up(terms):
    total = terms[0].astype(f32)
    for term in terms[1:]:
        total = total + term.astype(f32)
    return total


def split_rows(terms, parts):
    rows = terms[0].shape[0] // parts
    return [[term[i * rows : (i + 1) * rows] for term in terms] for i in range(parts)]


class Scatter:
    def __init__(self, arrays, orders):
        self.arrays = arrays
        self.fresh = []
        self.stages = list(zip(*[order[::-1] for order in orders]))
        self.widths = [terms[0].shape[1] for terms in arrays]

    def take_in(self, others):
        fresh = hold(self.fresh, others if self.fresh else ())
        if self.joined:
            cut = self.widths[0]
            fresh = [[array[:, :cut] for array in fresh], [array[:, cut:] for array in fresh]]
        else:
            fresh = [fresh[: self.count], fresh[self.count :]]
        self.arrays = [terms + more for terms, more in zip(self.arrays, fresh)]
        self.fresh = []

    def load(self, *others):
        if self.fresh:
            self.take_in(others)
        elif others:
            self.arrays = [hold(terms, others) for terms in self.arrays]
        self.now = self.stages.pop(0)
        self.joined = self.now[0] == self.now[1]
        self.count = len(self.now[0])
        self.chunks = [split_rows(terms, len(stage) + 1) for terms, stage in zip(self.arrays, self.now)]
        sends = [[add_up(chunk).astype(bf16) for chunk in chunks[1:]] for chunks in self.chunks]
        if self.joined:
            self.sends = [jnp.concatenate(pair, axis=1) for pair in zip(*sends)]
        else:
            self.sends = sends[0] + sends[1]
        return self.sends

    def move(self):
        moves = self.now[0] if self.joined else self.now[0] + self.now[1]
        self.arrays = [chunks[0] for chunks in self.chunks]
        self.fresh = [swap(send, axis, mask) for (axis, mask, _), send in zip(moves, self.sends)]

    def step(self, *others):
        sends = self.load(*others)
        self.move()
        return sends

    def finish(self, *others):
        while self.stages:
            self.step(*others)
        self.take_in(others)
        return jnp.concatenate([add_up(terms) for terms in self.arrays], axis=1)


def natural_pieces(stack, rels, chip, fast):
    if fast:
        per = len(rels) // len(stack)
        return stack, [rels[i * per : (i + 1) * per] for i in range(len(stack))]
    whole = jnp.concatenate(stack, axis=0)
    count = len(rels)
    where = np.zeros(count, np.int32)
    for slot, rel in enumerate(rels):
        where[rel] = slot
    order = jnp.asarray(where)[chip ^ jnp.arange(count, dtype=jnp.int32)]
    whole = whole.reshape(count, whole.shape[0] // count, whole.shape[1])
    whole = jnp.take(whole, order, axis=0).reshape(-1, whole.shape[2])
    return [whole], [list(range(BLOCKS))]


def in_slots(whole, rels, chip, fast):
    if fast:
        return whole
    count = len(rels)
    whole = whole.reshape(count, whole.shape[0] // count, whole.shape[1])
    order = jnp.asarray(np.array(rels, np.int32)) ^ chip
    return jnp.take(whole, order, axis=0).reshape(-1, whole.shape[2])


def by_core(core, mine, other, axis):
    return jnp.where(
        core == 0,
        jnp.concatenate([mine, other], axis=axis),
        jnp.concatenate([other, mine], axis=axis),
    )


def pair_block(core, halves):
    mine = jnp.where(core == 0, halves[0], halves[1])
    send = jnp.where(core == 0, halves[1], halves[0])
    return by_core(core, mine, swap_core(send), 0)


def dot(left, right):
    return lax.dot_general(left, right, (((1,), (0,)), ((), ())), preferred_element_type=f32)


def dot_nt(left, right):
    return lax.dot_general(left, right, (((1,), (1,)), ((), ())), preferred_element_type=f32)


def run_copies(copies, sems):
    started = []
    for at, (source, target) in enumerate(copies):
        copy = pltpu.make_async_copy(source, target, sems.at[at])
        copy.start()
        started.append(copy)
    return started


def wait_all(started):
    for copy in started:
        copy.wait()


def slots_of(pieces, rels):
    return [(piece, at, rel) for piece, table in zip(pieces, rels) for at, rel in enumerate(table)]


def block_rows(index, size):
    return pl.ds(pl.multiple_of(index * size, size), size)


def pos_block(index):
    quarter, within = index // (BLOCKS // 4), index % (BLOCKS // 4)
    return ((quarter % 2) * 2 + quarter // 2) * (BLOCKS // 4) + within


def core_lanes(core, width):
    return pl.ds(pl.multiple_of(core * width, LANES), width)


def head_mask(shape, dim, which, head_dim, kind):
    place = lax.broadcasted_iota(jnp.int32, shape, dim)
    return ((place // head_dim) == which).astype(f32).astype(kind)


def attend_pairs(pairs, scale, head_dim, tables, bias, query, key, value, w_pos, probs, ctx_own, ctx_par, lhs, rhs):
    sin, cos, sin_t, cos_t, feats, feats_t = tables
    width = feats.shape[1]
    half = width // 2
    row_len = bias.shape[1]
    lhs[:, width : 2 * width] = feats[...]
    rhs[0:width, :] = feats_t[...]

    def one_pair(pair, carry):
        lanes = pl.ds(pl.multiple_of(pair * LANES, LANES), LANES)
        q_pair, k_pair, v_pair, w_pair = query[:, lanes], key[:, lanes], value[:, lanes], w_pos[:, lanes]
        rhs[2 * width : 2 * width + LANES, :] = k_pair.T
        mixed = [None, None]
        for which in (0, 1):
            lane_mask = head_mask((1, LANES), 1, which, head_dim, bf16)
            q_head = q_pair * lane_mask
            k_head = k_pair * lane_mask
            lhs[:, 2 * width :] = q_head
            for row in (0, 1):
                span = slice(row * row_len, (row + 1) * row_len)
                coeff = dot_nt(q_head[span], w_pair)
                along_sin, along_cos = coeff[:, :half], coeff[:, half:]
                sin_row, cos_row = sin[span, :], cos[span, :]
                lhs[span, 0:half] = (along_cos * sin_row - along_sin * cos_row).astype(bf16)
                lhs[span, half:width] = (along_sin * sin_row + along_cos * cos_row).astype(bf16)
                coeff = dot_nt(w_pair, k_head[span])
                along_sin, along_cos = coeff[:half], coeff[half:]
                sin_row, cos_row = sin_t[:, span], cos_t[:, span]
                rhs[width : width + half, span] = (along_cos * sin_row - along_sin * cos_row).astype(bf16)
                rhs[width + half : 2 * width, span] = (along_sin * sin_row + along_cos * cos_row).astype(bf16)
            for row in (0, 1):
                span = slice(row * row_len, (row + 1) * row_len)
                scores = dot(lhs[span, :], rhs[:, span]) * scale + bias[row]
                top = jnp.max(scores, axis=-1, keepdims=True)
                expo = jnp.exp(scores - top)
                prob = expo / jnp.sum(expo, axis=-1, keepdims=True)
                probs[pair - pairs[0], which * 2 + row] = prob
                piece = dot(prob.astype(bf16), v_pair[span] * lane_mask)
                mixed[row] = piece if mixed[row] is None else mixed[row] + piece
        ctx_own[:, lanes] = mixed[0].astype(bf16)
        ctx_par[:, lanes] = mixed[1].astype(bf16)
        return carry

    if pairs[1] - pairs[0] == 1:
        one_pair(pairs[0], 0)
    else:
        lax.fori_loop(pairs[0], pairs[1], one_pair, 0)


def project_kernel(rels_one, rels_two, meta, own, par, *refs):
    (pieces_one, pieces_two), refs = take_lists(refs, [len(rels_one), len(rels_two)])
    w_qk, w_v, w_pos, query, key, value, sems = refs
    chip = meta[0]
    row_len, width = own.shape
    part = w_v.shape[1]
    rows = width // BLOCKS
    copies = []
    for piece, at, rel in slots_of(pieces_one, rels_one):
        copies.append((piece.at[pl.ds(at * rows, rows), :], w_qk.at[block_rows(chip ^ rel, rows), :]))
    for piece, at, rel in slots_of(pieces_two, rels_two):
        source = piece.at[pl.ds(at * rows, rows), :]
        copies.append((source.at[:, pl.ds(0, part)], w_v.at[block_rows(chip ^ rel, rows), :]))
        copies.append((source.at[:, pl.ds(part, part)], w_pos.at[block_rows(pos_block(chip ^ rel), rows), :]))
    wait_all(run_copies(copies, sems))
    for row, tokens in enumerate((own, par)):
        span = slice(row * row_len, (row + 1) * row_len)
        query[span, :] = dot(tokens[...], w_qk[:, 0:part]).astype(bf16)
        key[span, :] = dot(tokens[...], w_qk[:, part:]).astype(bf16)
        value[span, :] = dot(tokens[...], w_v[...]).astype(bf16)


def attend_kernel(pairs, scale, head_dim, *refs):
    tables, bias, (query, key, value, w_pos), refs = refs[:6], refs[6], refs[7:11], refs[11:]
    before = pairs[0] * LANES
    if before:
        own_before, par_before = refs[:2]
        refs = refs[2:]
    probs, ctx_own, ctx_par, lhs, rhs = refs
    if before:
        ctx_own[:, 0:before] = own_before[:, 0:before]
        ctx_par[:, 0:before] = par_before[:, 0:before]
    attend_pairs(pairs, scale, head_dim, tables, bias, query, key, value, w_pos, probs, ctx_own, ctx_par, lhs, rhs)


def take_lists(refs, sizes):
    taken = []
    for size in sizes:
        taken.append(refs[:size])
        refs = refs[size:]
    return taken, refs


def vmem_spec():
    return pl.BlockSpec(memory_space=pltpu.VMEM)


def any_spec():
    return pl.BlockSpec(memory_space=pltpu.HBM)


def smem_spec():
    return pl.BlockSpec(memory_space=pltpu.SMEM)


def params():
    return pltpu.CompilerParams(vmem_limit_bytes=VMEM_LIMIT)


def shape(dims, kind):
    return jax.ShapeDtypeStruct(dims, kind)


def cost(flops, moved, scale=COST_SCALE):
    return pl.CostEstimate(flops=int(flops * scale), bytes_accessed=int(moved * scale), transcendentals=0)


def project(meta, own, par, stack_one, rels_one, stack_two, rels_two):
    row_len, width = own.shape
    part = width // 2
    tokens = 2 * row_len
    copies = sum(map(len, rels_one)) + 2 * sum(map(len, rels_two))
    return pl.pallas_call(
        partial(project_kernel, rels_one, rels_two),
        out_shape=[
            shape((width, 2 * part), bf16),
            shape((width, part), bf16),
            shape((width, part), bf16),
            shape((tokens, part), bf16),
            shape((tokens, part), bf16),
            shape((tokens, part), bf16),
        ],
        in_specs=[smem_spec()] + [vmem_spec()] * 2 + [any_spec()] * (len(stack_one) + len(stack_two)),
        out_specs=[vmem_spec()] * 6,
        scratch_shapes=[pltpu.SemaphoreType.DMA((copies,))],
        compiler_params=params(),
        cost_estimate=cost(2 * 0.5e9, 6e6, ATTEND_SCALE),
        name="project",
    )(meta, own, par, *stack_one, *stack_two)


def attend(tables, bias, query, key, value, w_pos, before, pairs, scale, head_dim):
    tokens, part = query.shape
    width = 2 * part
    row_len = tokens // 2
    return pl.pallas_call(
        partial(attend_kernel, pairs, scale, head_dim),
        out_shape=[
            shape((pairs[1] - pairs[0], 4, row_len, row_len), f32),
            shape((row_len, part), bf16),
            shape((row_len, part), bf16),
        ],
        in_specs=[vmem_spec()] * (11 + len(before)),
        out_specs=[vmem_spec()] * 3,
        scratch_shapes=[
            pltpu.VMEM((tokens, 2 * width + LANES), bf16),
            pltpu.VMEM((2 * width + LANES, tokens), bf16),
        ],
        compiler_params=params(),
        cost_estimate=cost(2 * 1.0e9, 12e6, ATTEND_SCALE),
        name="attend",
    )(*tables, bias, query, key, value, w_pos, *before)


def norm_values(values):
    centered = values - jnp.mean(values, axis=-1, keepdims=True)
    inv_std = lax.rsqrt(jnp.mean(centered * centered, axis=-1, keepdims=True) + epsilon)
    return centered * inv_std, inv_std


def norm_backward(grad, normed_vals, inv_std, gain):
    grad_normed = grad * gain
    centered_grad = grad_normed - jnp.mean(grad_normed, axis=-1, keepdims=True)
    return inv_std * (
        centered_grad - normed_vals * jnp.mean(grad_normed * normed_vals, axis=-1, keepdims=True)
    )


def column_copies(pieces, rels, chip, rows, start, size, target, lanes):
    place = pl.ds(pl.multiple_of(lanes, LANES), size)
    return [
        (piece.at[pl.ds(at * rows, rows), pl.ds(start, size)], target.at[block_rows(chip ^ rel, rows), place])
        for piece, at, rel in slots_of(pieces, rels)
    ]


def middle_kernel(wide_rels, rels, out_rels, tile, meta, ctx_mine, ctx_recv, tokens, cotangent, *refs):
    wide, refs = take_lists(refs, [len(wide_rels[0]), len(wide_rels[1])] * 2)
    pieces, refs = take_lists(refs, [len(rels[0]), len(rels[1])] * 2)
    output, grad_resid, normed_low, low, grad_ctx_mine, grad_ctx_send, grad_gains, sums, grad_pre = refs[:9]
    grad_mine, grad_other = refs[9:11]
    w_out, w_up, w_down, act, act_grad, act_t, ordered, low_two, grad_buf = refs[11:20]
    out_sems, up_sems, down_sems, flush_sems, row_sems, *row_bufs = refs[20:]
    row_inputs = (ctx_mine, ctx_recv, tokens, cotangent)
    started_rows = run_copies(list(zip(row_inputs, row_bufs)), row_sems)
    ctx_mine, ctx_recv, tokens, cotangent = row_bufs
    chip, core = meta[0], meta[1]
    ff, width = w_down.shape
    half = width // 2
    rows = ff // BLOCKS // 2
    ff_half, piece_rows, side_width = ff // 2, width // BLOCKS, half + LANES
    rest = ff_half - UP_CHUNK
    copies_out, copies_up = [], []
    for side, chunks in ((core, wide[:2]), (1 - core, wide[2:])):
        copies_up += column_copies(chunks[0], wide_rels[0], chip, piece_rows, 0, UP_CHUNK, w_up, side * ff_half)
        copies_up += column_copies(chunks[1], wide_rels[1], chip, piece_rows, 0, rest, w_up, side * ff_half + UP_CHUNK)
        copies_out += column_copies(chunks[1], wide_rels[1], chip, piece_rows, rest, side_width, w_out, side * side_width)
    started_out = run_copies(copies_out, out_sems)
    started_up = run_copies(copies_up, up_sems)
    copies = []
    for side, chunks in ((core, pieces[:2]), (1 - core, pieces[2:])):
        for i in (0, 1):
            for piece, at, rel in slots_of(chunks[i], rels[i]):
                copies.append(
                    (
                        piece.at[pl.ds(at * rows, rows), :],
                        w_down.at[block_rows((chip ^ rel) * 2 + side, rows), pl.ds(i * half, half)],
                    )
                )
    started_down = run_copies(copies, down_sems)

    wait_all(started_rows)
    wait_all(started_out)
    lanes_of = [slice(side * side_width, side * side_width + half) for side in (0, 1)]
    attn_out = jnp.concatenate(
        [
            dot(ctx_mine[...], w_out[block_rows(core, half), lanes])
            + dot(ctx_recv[...], w_out[block_rows(1 - core, half), lanes])
            for lanes in lanes_of
        ],
        axis=1,
    )
    gains_one, gains_two = [
        w_out[:, side * side_width + half : (side + 1) * side_width].astype(f32).T[0:8] for side in (0, 1)
    ]
    tokens_f = tokens[...].astype(f32)
    resid = tokens_f + attn_out
    vals_one, inv_one = norm_values(resid)
    normed_one = vals_one * gains_one[0:1, :] + gains_one[1:2, :]
    normed_low[...] = normed_one.astype(bf16)
    sums[0:1, :] = jnp.sum(tokens_f * tokens_f, axis=0, keepdims=True)
    sums[1:2, :] = jnp.sum(attn_out * attn_out, axis=0, keepdims=True)
    sums[2:3, :] = jnp.sum(resid * resid, axis=0, keepdims=True)
    sums[3:8, :] = jnp.zeros((5, width), f32)

    wait_all(started_up)
    for at in range(0, ff, tile):
        lanes = pl.ds(at, tile)
        pre = dot(normed_low[...], w_up[:, lanes])
        bell = 0.5 * (1.0 + lax.erf(pre * (0.5**0.5)))
        low_act = (pre * bell).astype(bf16)
        act[:, lanes] = low_act
        act_t[lanes, :] = low_act.T
        act_grad[:, lanes] = bell + pre * jnp.exp(pre * pre * -0.5) * (0.5 / math.pi) ** 0.5
    wait_all(started_down)
    vals, inv = norm_values(normed_one + dot(act[...], w_down[...]))
    gain, shift = gains_two[0:1, :], gains_two[1:2, :]
    output[...] = (vals * gain + shift).astype(bf16)
    grad = cotangent[...].astype(f32)
    grad_gains[2:3, :] = jnp.sum(grad * vals, axis=0, keepdims=True)
    grad_gains[3:4, :] = jnp.sum(grad, axis=0, keepdims=True)
    grad_gains[4:8, :] = jnp.zeros((4, width), f32)
    grad_two = norm_backward(grad, vals, inv, gain)
    low_two[...] = grad_two.astype(bf16)
    flushed = []
    for target, place in ((grad_other, 1 - core), (grad_mine, core)):
        for i in (0, 1):
            at = len(flushed)
            for slot, rel in enumerate(out_rels[i]):
                ordered[slot * rows : (slot + 1) * rows, :] = act_t[block_rows((chip ^ rel) * 2 + place, rows), :]
            grad_buf[at] = dot(ordered[...], low_two[:, i * half : (i + 1) * half]).astype(bf16)
            copy = pltpu.make_async_copy(grad_buf.at[at], target.at[:, pl.ds(i * half, half)], flush_sems.at[at])
            copy.start()
            flushed.append(copy)

    grad = grad_two
    for at in range(0, ff, tile):
        lanes = pl.ds(at, tile)
        piece = (dot_nt(low_two[...], w_down[lanes, :]) * act_grad[:, lanes]).astype(bf16)
        grad_pre[:, lanes] = piece
        grad = grad + dot_nt(piece, w_up[:, lanes])
    back = norm_backward(grad, vals_one, inv_one, gains_one[0:1, :])
    grad_resid[...] = back
    low[...] = back.astype(bf16)
    for target, side in ((grad_ctx_mine, core), (grad_ctx_send, 1 - core)):
        parts = [dot_nt(low[:, i * half : (i + 1) * half], w_out[block_rows(side, half), lanes_of[i]]) for i in (0, 1)]
        target[...] = (parts[0] + parts[1]).astype(bf16)
    grad_gains[0:1, :] = jnp.sum(grad * vals_one, axis=0, keepdims=True)
    grad_gains[1:2, :] = jnp.sum(grad, axis=0, keepdims=True)
    wait_all(flushed)


def middle(meta, ctx_mine, ctx_recv, tokens, cotangent, wide, wide_rels, pieces, rels, out_rels, ff):
    count, width = tokens.shape
    half = width // 2
    tile = 512
    flat = [array for chunk in wide + pieces for array in chunk]
    slots_wide = [2 * sum(map(len, table)) for table in wide_rels]
    return pl.pallas_call(
        partial(middle_kernel, wide_rels, rels, out_rels, tile),
        out_shape=[
            shape((count, width), bf16),
            shape((count, width), f32),
            shape((count, width), bf16),
            shape((count, width), bf16),
            shape((count, half), bf16),
            shape((count, half), bf16),
            shape((8, width), f32),
            shape((8, width), f32),
            shape((count, ff), bf16),
        ]
        + [shape((ff // 2, width), bf16)] * 2,
        in_specs=[smem_spec()] + [any_spec()] * (4 + len(flat)),
        out_specs=[vmem_spec()] * 9 + [any_spec()] * 2,
        scratch_shapes=[
            pltpu.VMEM((width, width + 2 * LANES), bf16),
            pltpu.VMEM((width, ff), bf16),
            pltpu.VMEM((ff, width), bf16),
            pltpu.VMEM((count, ff), bf16),
            pltpu.VMEM((count, ff), f32),
            pltpu.VMEM((ff, count), bf16),
            pltpu.VMEM((ff // 2, count), bf16),
            pltpu.VMEM((count, width), bf16),
            pltpu.VMEM((4, ff // 2, half), bf16),
            pltpu.SemaphoreType.DMA((slots_wide[1],)),
            pltpu.SemaphoreType.DMA((slots_wide[0] + slots_wide[1],)),
            pltpu.SemaphoreType.DMA((2 * sum(map(len, rels[0] + rels[1])),)),
            pltpu.SemaphoreType.DMA((4,)),
            pltpu.SemaphoreType.DMA((4,)),
            pltpu.VMEM((count, half), bf16),
            pltpu.VMEM((count, half), bf16),
            pltpu.VMEM((count, width), bf16),
            pltpu.VMEM((count, width), bf16),
        ],
        compiler_params=params(),
        cost_estimate=cost(2 * 3.2e9, 30e6),
        name="middle",
    )(meta, ctx_mine, ctx_recv, tokens, cotangent, *flat)


def permute_rows(source, target, chip, out_rels):
    rows = source.shape[0] // BLOCKS
    for slot, rel in enumerate(out_rels):
        target[slot * rows : (slot + 1) * rows, :] = source[block_rows(chip ^ rel, rows), :]


def digit_scales(devices):
    base = 1 << ((256 // devices + 1).bit_length() - 1)
    if base < 8:
        return None
    exponents = np.full((2 * LANES, 1), 126.0)
    for half in (0, 1):
        for row in range(2, LANES):
            exponents[half * LANES + row, 0] = 123 - 3 * ((row - 2) % 42 + 42 * half)
    return np.exp2(exponents).astype(np.float32)


def digits_of(sums, places):
    row = lax.broadcasted_iota(jnp.int32, (LANES, 1), 0)
    totals = [jnp.sum(sums[i : i + 1, :], axis=1, keepdims=True) for i in range(3)]
    value = jnp.where(row < 44, totals[0], jnp.where(row < 86, totals[1], totals[2]))
    whole = jnp.floor(jnp.minimum(value / places, 2.0**30))
    return whole - 8.0 * jnp.floor(whole * 0.125)


def weight_grads_kernel(
    out_rels, tile, meta, normed_low, low, all_gains, ctx_mine, ctx_recv, sums, places, grad_pre_in, *refs
):
    targets, grads, refs = refs[:2], refs[2:4], refs[4:]
    grad_pre, turned, ordered_one, ordered_two, gain_buf, in_sems, flush_sems = refs
    chip, core = meta[0], meta[1]
    width, ff = turned.shape[0], grad_pre.shape[1]
    half, ff_half = width // 2, ff // 2
    rows = width // BLOCKS
    rest = ff_half - UP_CHUNK
    tiles = [
        (side, place * ff_half, start, tile if start < UP_CHUNK else rest)
        for side, place in ((1, 1 - core), (0, core))
        for start in [*range(0, UP_CHUNK, tile), UP_CHUNK]
    ]
    places_of = [pl.ds(pl.multiple_of(base + start, LANES), size) for _, base, start, size in tiles]
    loads = run_copies([(grad_pre_in.at[:, lanes], grad_pre.at[:, lanes]) for lanes in places_of], in_sems)
    flushed = []

    def flush(side, start, size):
        lanes = pl.ds(start, size)
        copy = pltpu.make_async_copy(grads[side].at[:, lanes], targets[side].at[:, lanes], flush_sems.at[len(flushed)])
        copy.start()
        flushed.append(copy)

    turned[...] = normed_low[...].T
    permute_rows(turned, ordered_one, chip, out_rels[0])
    permute_rows(turned, ordered_two, chip, out_rels[1])
    for load, lanes, (side, _, start, size) in zip(loads, places_of, tiles):
        load.wait()
        ordered = ordered_one if start < UP_CHUNK else ordered_two
        grads[side][:, start : start + size] = dot(ordered[...], grad_pre[:, lanes]).astype(bf16)
        if start < UP_CHUNK:
            flush(side, start, size)
    turned[block_rows(core, half), :] = ctx_mine[...].T
    turned[block_rows(1 - core, half), :] = ctx_recv[...].T
    permute_rows(turned, ordered_two, chip, out_rels[1])
    first, second = all_gains[0:2, :], all_gains[2:4, :]
    at_first = (core == 0).astype(f32)
    pair = (first * at_first + second * (1.0 - at_first), first * (1.0 - at_first) + second * at_first)
    for side, place in ((1, 1 - core), (0, core)):
        grad = grads[side]
        grad[:, ff_half : ff_half + half] = dot(ordered_two[...], low[:, core_lanes(place, half)]).astype(bf16)
        digits = digits_of(sums[...], places[block_rows(place, LANES), :])[2:]
        padded = jnp.concatenate([pair[side], jnp.broadcast_to(digits, (LANES - 2, width))], axis=0)
        gain_buf[...] = padded.T.astype(bf16)
        for slot, rel in enumerate(out_rels[1]):
            grad[slot * rows : (slot + 1) * rows, ff_half + half :] = gain_buf[block_rows(chip ^ rel, rows), :]
        flush(side, UP_CHUNK, rest + half + LANES)
    wait_all(flushed)


def weight_grads(meta, grad_pre, normed_low, low, all_gains, ctx_mine, ctx_recv, sums, places, out_rels):
    count, ff = grad_pre.shape
    width = normed_low.shape[1]
    out = (width, ff // 2 + width // 2 + LANES)
    tile = 512
    tiles = 2 * (UP_CHUNK // tile + 1)
    return pl.pallas_call(
        partial(weight_grads_kernel, out_rels, tile),
        out_shape=[shape(out, bf16)] * 2,
        in_specs=[smem_spec()] + [vmem_spec()] * 7 + [any_spec()],
        out_specs=[any_spec()] * 2,
        scratch_shapes=[pltpu.VMEM(out, bf16)] * 2
        + [pltpu.VMEM((count, ff), bf16)]
        + [pltpu.VMEM((width, count), bf16)] * 3
        + [
            pltpu.VMEM((width, LANES), bf16),
            pltpu.SemaphoreType.DMA((tiles,)),
            pltpu.SemaphoreType.DMA((tiles,)),
        ],
        compiler_params=params(),
        cost_estimate=cost(2 * 0.8e9, 10e6),
        name="weight_grads",
    )(meta, normed_low, low, all_gains, ctx_mine, ctx_recv, sums, places, grad_pre)


def attend_backward_kernel(
    out_rels, split, scale, head_dim, meta, own_t, par_t, sin, cos, sin_t, cos_t, feats, feats_t, query, key, value, w_pos, probs,
    grad_own, grad_par, grad_qkv, *refs
):
    outs, refs = (refs[:2], refs[2:]) if split else (refs[:1], refs[1:])
    grad_ctx, coeff_q, coeff_k, x2_rel, pos_buf = refs
    chip = meta[0]
    tokens, width = feats.shape
    row_len = tokens // 2
    half = width // 2
    grad_ctx[0:row_len, :] = grad_own[...]
    grad_ctx[row_len:, :] = grad_par[...]
    q_pair, k_pair, v_pair, w_pair, g_pair = query[...], key[...], value[...], w_pos[...], grad_ctx[...]
    q_t, v_t, g_t, w_t = q_pair.T, v_pair.T, g_pair.T, w_pair.T
    grad_q = [None, None]
    grad_k = [None, None]
    grad_v = [None, None]

    def plus(total, term):
        return term if total is None else total + term

    grad_q_coeff = None
    grad_k_coeff = None
    pos_q = None
    pos_k = None
    for which in (0, 1):
        lane_mask = head_mask((1, LANES), 1, which, head_dim, bf16)
        row_mask = head_mask((LANES, 1), 0, which, head_dim, bf16)
        k_head, g_head, w_head = k_pair * lane_mask, g_pair * lane_mask, w_pair * lane_mask
        q_t_head, g_t_head, w_t_head = q_t * row_mask, g_t * row_mask, w_t * row_mask
        for row in (0, 1):
            span = slice(row * row_len, (row + 1) * row_len)
            prob = probs[0, which * 2 + row]
            grad_probs = dot(g_head[span], v_t[:, span])
            inner = jnp.sum(prob * grad_probs, axis=-1, keepdims=True)
            grad_scores = (prob * (grad_probs - inner) * scale).astype(bf16)
            grad_v[row] = plus(grad_v[row], dot(g_t_head[:, span], prob.astype(bf16)))
            grad_k[row] = plus(grad_k[row], dot(q_t_head[:, span], grad_scores))
            grad_q[row] = plus(grad_q[row], dot(grad_scores, k_head[span]))
            pos = dot(grad_scores, feats[span, :])
            first, second = pos[:, :half], pos[:, half:]
            sin_row, cos_row = sin[span, :], cos[span, :]
            coeff_q[span, 0:half] = (second * sin_row - first * cos_row).astype(bf16)
            coeff_q[span, half:] = (first * sin_row + second * cos_row).astype(bf16)
            pos = dot(feats_t[:, span], grad_scores)
            first, second = pos[:half], pos[half:]
            sin_row, cos_row = sin_t[:, span], cos_t[:, span]
            coeff_k[0:half, span] = (second * sin_row - first * cos_row).astype(bf16)
            coeff_k[half:, span] = (first * sin_row + second * cos_row).astype(bf16)
        grad_q_coeff = plus(grad_q_coeff, dot(coeff_q[...], w_head))
        grad_k_coeff = plus(grad_k_coeff, dot(w_t_head, coeff_k[...]))
        pos_q = plus(pos_q, dot(q_t_head, coeff_q[...]))
        pos_k = plus(pos_k, dot(coeff_k[...], k_head))
    d_q = (jnp.concatenate(grad_q, axis=0) + grad_q_coeff).astype(bf16)
    d_k = (jnp.concatenate(grad_k, axis=1) + grad_k_coeff).astype(bf16).T
    d_v = jnp.concatenate(grad_v, axis=1).astype(bf16).T
    grad_qkv[:, 0:LANES] = d_q
    grad_qkv[:, LANES : 2 * LANES] = d_k
    grad_qkv[:, 2 * LANES :] = d_v
    pos_buf[...] = (pos_k + pos_q.T).astype(bf16)
    rows = width // BLOCKS
    cuts = (0, 2 * LANES, 3 * LANES) if split else (0, 3 * LANES)
    for at, out in enumerate(outs):
        size = cuts[at + 1] - cuts[at]
        permute_rows(own_t, x2_rel.at[:, 0:row_len], chip, out_rels[at])
        permute_rows(par_t, x2_rel.at[:, row_len:], chip, out_rels[at])
        out[:, 0:size] = dot(x2_rel[...], grad_qkv[:, cuts[at] : cuts[at + 1]]).astype(bf16)
    for slot, rel in enumerate(out_rels[-1]):
        outs[-1][slot * rows : (slot + 1) * rows, size:] = pos_buf[block_rows(pos_block(chip ^ rel), rows), :]


def attend_backward(
    meta, pair, own_t, par_t, tables, query, key, value, w_pos, probs, place, grad_own, grad_par, out_rels, scale, head_dim
):
    width, row_len = own_t.shape
    tokens = 2 * row_len

    def whole(array):
        return pl.BlockSpec(array.shape, lambda i: (0,) * array.ndim)

    def columns(rows):
        return pl.BlockSpec((rows, LANES), lambda i: (0, pair))

    split = len(out_rels) > 1
    pieces = [shape((width, (2 if split else 4) * LANES), bf16)] * (2 if split else 1)
    return pl.pallas_call(
        partial(attend_backward_kernel, out_rels, split, scale, head_dim),
        grid=(1,),
        out_shape=[shape((tokens, 3 * LANES), bf16)] + pieces,
        in_specs=[smem_spec(), whole(own_t), whole(par_t)]
        + [whole(table) for table in tables]
        + [columns(tokens)] * 3
        + [columns(width), pl.BlockSpec((1, 4, row_len, row_len), lambda i: (place, 0, 0, 0))]
        + [columns(row_len)] * 2,
        out_specs=[pl.BlockSpec((tokens, 3 * LANES), lambda i: (0, 0))]
        + [pl.BlockSpec(piece.shape, lambda i: (0, 0)) for piece in pieces],
        scratch_shapes=[
            pltpu.VMEM((tokens, LANES), bf16),
            pltpu.VMEM((tokens, width), bf16),
            pltpu.VMEM((width, tokens), bf16),
            pltpu.VMEM((width, tokens), bf16),
            pltpu.VMEM((width, LANES), bf16),
        ],
        compiler_params=params(),
        cost_estimate=cost(2 * 1.3e9, 10e6, BACK_SCALES[pair]),
        name="attend_backward",
    )(meta, own_t, par_t, *tables, query, key, value, w_pos, probs, grad_own, grad_par)


def row_tables(boxes):
    rates = jnp.exp(jnp.arange(FREQS, dtype=f32) * (-math.log(10000.0) / FREQS))
    angles = boxes.astype(f32)[:, :, None] * rates[None, None, :]
    angles = jnp.transpose(angles, (1, 0, 2)).reshape(boxes.shape[1], 2 * FREQS)
    sin, cos = jnp.sin(angles), jnp.cos(angles)
    feats = jnp.concatenate([sin, cos], axis=1).astype(bf16)
    return sin, cos, sin.T, cos.T, feats, feats.T


def body(
    tokens_in, boxes, page_lengths, cotangent, w_qkv, w_out, w_pos, gain_attn, bias_attn, w_up, w_down, gain_ffn, bias_ffn
):
    row_len, width = tokens_in.shape
    ff = w_up.shape[1]
    half, ff_half = width // 2, ff // 2
    head_dim = width // HEADS
    scale = head_dim ** (-0.5)
    dp, rep = lax.axis_size("dp"), lax.axis_size("rep")
    chips = dp * rep // 2
    core = lax.axis_index("rep") % 2
    chip = lax.axis_index("dp") * (rep // 2) + lax.axis_index("rep") // 2
    fast = chips == BLOCKS
    meta = jnp.stack([chip if fast else 0 * chip, core]).astype(jnp.int32)
    x, y, z_wide, z = tree_stages()
    heads_orders = (z_wide + x + y, z_wide + y + x)
    deep_orders = (x + z + y, y + z + x)
    orders = (z + x + y, z + y + x)
    heads_rels, deep_rels, all_rels = [
        [slot_chips(order) for order in pair] for pair in (heads_orders, deep_orders, orders)
    ]

    def split_columns(stack, cut, *others):
        stack = hold(stack, others)
        return [[columns_of(stack, 0, cut)], [columns_of(stack, cut, stack[0].shape[1])]]

    def move(stacks, stages, *others):
        moved = []
        for stack, stage in zip(stacks, stages):
            stack = stack[:1] + hold(stack[1:], others if len(stack) > 1 else ())
            whole = stack[0] if len(stack) == 1 else jnp.concatenate(stack, axis=0)
            moved.append([whole] + [swap(whole, axis, mask) for axis, mask, _ in stage])
        return moved

    def sent(stacks):
        return [stack[0] for stack in stacks]

    def came(stacks):
        return [piece for stack in stacks for piece in stack[1:]]

    def joined(stacks):
        return jnp.concatenate([jnp.concatenate(stack, axis=0) for stack in stacks], axis=1)

    def heads_half(side):
        parts = [w_qkv[:, at * width + side * half : at * width + (side + 1) * half] for at in range(3)]
        return jnp.concatenate(parts + [w_pos[:, side * half : (side + 1) * half]], axis=1)

    heads_block = pair_block(core, [heads_half(s) for s in (0, 1)])
    heads_z = gather_first(heads_block, z_wide)
    tokens_late, boxes, page_lengths, w_up, w_out, w_down, gain_attn, bias_attn, gain_ffn, bias_ffn = hold(
        [tokens_in, boxes, page_lengths, w_up, w_out, w_down, gain_attn, bias_attn, gain_ffn, bias_ffn], [heads_block]
    )
    deep = move([[w_down[:, :half]], [w_down[:, half:]]], (x[0], y[0]))
    gain_sets = ((gain_attn, bias_attn), (gain_ffn, bias_ffn))
    pad = jnp.zeros((w_up.shape[0], LANES - 2), bf16)
    wide_block = pair_block(
        core,
        [
            jnp.concatenate(
                [
                    w_up[:, s * ff_half : (s + 1) * ff_half],
                    w_out[:, s * half : (s + 1) * half],
                    jnp.stack(gain_sets[s], axis=1),
                    pad,
                ],
                axis=1,
            )
            for s in (0, 1)
        ],
    )

    tokens_par = swap_core(tokens_late)
    ends = jnp.cumsum(page_lengths, axis=1)
    places = jnp.arange(row_len, dtype=jnp.int32)
    segment = jnp.sum((places[None, :, None] >= ends[:, None, :]).astype(jnp.int32), axis=2)
    marks = jnp.concatenate([boxes, segment], axis=0)
    marks_other = swap_core(marks)
    segments = jnp.stack([marks[2], marks_other[2]])
    bias = jnp.where(segments[:, :, None] == segments[:, None, :], 0.0, masked_value).astype(f32)
    tables = row_tables(jnp.concatenate([marks[:2], marks_other[:2]], axis=1))

    def thin(stack, stage):
        return stack + [swap(piece, axis, mask) for axis, mask, _ in stage for piece in stack]

    heads = move(split_columns(heads_z, width), (x[0], y[0]))
    wide_z = [after(wide_block, *heads_z[1:])]
    for stage in z[:-1]:
        wide_z = thin(wide_z, stage)
    heads = move(heads, (y[0], x[0]), *wide_z[1:])
    wide_z = thin([jnp.concatenate(wide_z[:1] + hold(wide_z[1:], sent(heads)), axis=0)], z[-1])
    deep_z = [joined([stack[:1] + hold(stack[1:], [wide_z[0]]) for stack in deep])]
    for stage in z[:-1]:
        deep_z = thin(deep_z, stage)
    wide = move(split_columns(wide_z[:1] + hold(wide_z[1:], came(heads)), UP_CHUNK), (x[0], y[0]))

    def tabled(stacks, rels):
        done = [natural_pieces(stack, table, chip, fast) for stack, table in zip(stacks, rels * 2)]
        return [pieces for pieces, _ in done], [table for _, table in done[:2]]

    (stack_qk, stack_vp), (table_qk, table_vp) = tabled(heads, heads_rels)
    w_qk, w_v, w_pos_half, query, key, value = project(
        meta, after(tokens_in, *sent(wide)), tokens_par, stack_qk, table_qk, stack_vp, table_vp
    )
    wide = move(wide, (y[0], x[0]), query)
    deep_z = thin([jnp.concatenate(deep_z[:1] + hold(deep_z[1:], sent(wide)), axis=0)], z[-1])
    probs, ctx_mine, ctx_send = attend(
        tables, bias, after(query, deep_z[0]), key, value, w_pos_half, [], (0, half // LANES), scale, head_dim
    )
    ctx_recv = swap_core(ctx_send)
    wide = [stack[:1] + hold(stack[1:], [ctx_mine]) for stack in wide]
    deep = move(split_columns(deep_z[:1] + hold(deep_z[1:], [ctx_mine]), half), (y[0], x[0]))
    wide, table_wide = tabled(wide + [[swap_core(piece) for piece in stack] for stack in wide], all_rels)
    deep, table_deep = tabled(deep + [[swap_core(piece) for piece in stack] for stack in deep], deep_rels)
    if not fast:
        plain, deep = deep, [None] * 4
        for i in (0, 1):
            mine, other = [stack[0].reshape(chips, 1, -1, half) for stack in (plain[i], plain[2 + i])]
            cut = by_core(core, mine, other, 1).reshape(BLOCKS, 2, -1, half)
            deep[i] = [jnp.where(core == 0, cut[:, 0], cut[:, 1]).reshape(-1, half)]
            deep[2 + i] = [jnp.where(core == 0, cut[:, 1], cut[:, 0]).reshape(-1, half)]

    natural = list(range(BLOCKS))
    pair_rels, out_rels = [tuple(rels) if fast else (natural, natural) for rels in (heads_rels, all_rels)]
    output, grad_resid_one, normed_low, grad_low, grad_ctx_mine, grad_ctx_send, all_gains, sums, grad_pre, deep_mine, deep_other = middle(
        meta, ctx_mine, ctx_recv, tokens_in, cotangent, wide, table_wide, deep, table_deep, out_rels, ff
    )
    if not fast:
        mine, other = [grads.reshape(BLOCKS, 1, -1, width) for grads in (deep_mine, deep_other)]
        cut = by_core(core, mine, other, 1).reshape(chips, 2, -1, width)
        deep_mine = jnp.where(core == 0, cut[:, 0], cut[:, 1]).reshape(-1, width)
        deep_other = jnp.where(core == 0, cut[:, 1], cut[:, 0]).reshape(-1, width)

    def two_arrays(terms, cut, orders, all_rels):
        parts = [[term[:, :cut] for term in terms], [term[:, cut:] for term in terms]]
        parts = [[in_slots(term, rels, chip, fast) for term in part] for part, rels in zip(parts, all_rels)]
        return Scatter(parts, orders)

    places = digit_scales(dp * rep)
    deep_core = swap_core(deep_other)
    wide_mine, wide_other = weight_grads(
        meta, grad_pre, normed_low, grad_low, all_gains, ctx_mine, ctx_recv, sums,
        jnp.ones((2 * LANES, 1), f32) if places is None else jnp.asarray(places), out_rels
    )
    grad_ctx_recv = swap_core(grad_ctx_send)
    s_deep = two_arrays([deep_mine, after(deep_core, wide_mine)], half, orders, all_rels)
    token = s_deep.step()
    wide_core = swap_core(wide_other)
    own_t, par_t = tokens_in.T, tokens_par.T

    def back_pair(pair, rels, *others):
        return attend_backward(
            meta, pair, own_t, par_t, tables, query, key, value, w_pos_half, probs, pair, after(grad_ctx_mine, *others),
            grad_ctx_recv, rels, scale, head_dim
        )

    pair_grads = [None] * 3
    pair_grads[0], pair_zero = back_pair(0, pair_rels[:1], *token)
    s_wide = two_arrays([wide_mine, after(wide_core, pair_zero)], UP_CHUNK, orders, all_rels)
    token = s_wide.step()
    pair_grads[1], pair_one, pair_two = back_pair(1, pair_rels, *token)
    pair_grads[2], pair_three = back_pair(2, pair_rels[1:], pair_one)
    s_pair = Scatter(
        [
            [in_slots(jnp.concatenate(pieces, axis=1), rels, chip, fast)]
            for pieces, rels in zip(((pair_zero, pair_one), (pair_two, pair_three)), heads_rels)
        ],
        heads_orders,
    )
    token = s_deep.step(pair_three)
    token = s_wide.step(*token)
    grad_q, grad_k, grad_v = [
        jnp.concatenate([grads[:, i * LANES : (i + 1) * LANES] for grads in pair_grads], axis=1) for i in range(3)
    ]
    grad_x2 = dot_nt(after(jnp.concatenate([grad_q, grad_k], axis=1), *token), w_qk) + dot_nt(grad_v, w_v)
    grad_tokens = grad_resid_one + grad_x2[:row_len] + swap_core(grad_x2[row_len:])
    token = s_pair.step(*token)
    token = s_deep.step(*token)
    token = s_wide.step(*token)
    token = s_deep.step(*token)
    token = s_pair.step(*token)
    token = s_wide.step(*token)
    deep_sum = s_deep.finish(*token)
    wide_sum = s_wide.finish(*token)
    pair_sum = s_pair.finish(*token)

    def own_rows(values):
        rows = values.shape[0] // 2
        mine = jnp.where(core == 0, values[:rows], values[rows:])
        send = jnp.where(core == 0, values[rows:], values[:rows])
        return mine, swap_core(send)

    def sides(pieces, start, size):
        return by_core(core, pieces[0][:, start : start + size], pieces[1][:, start : start + size], 1)

    wide_rows = own_rows(wide_sum)
    pair_rows = own_rows(pair_sum)

    starts = [[0, 1, 2, 3], [4, 5, 6, 7], [8, 9, 10, 11]]

    def pair_columns(which):
        picked = [
            jnp.concatenate([rows[:, at[which] * LANES : (at[which] + 1) * LANES] for at in starts], axis=1)
            for rows in pair_rows
        ]
        return by_core(core, picked[0], picked[1], 1)

    gain_rows = sides(wide_rows, ff_half + half, LANES)
    if places is None:
        totals = after(jnp.sum(sums[:3], axis=1), pair_sum)
        for axis, size in (("rep", rep), ("dp", dp)):
            for bit in range(size.bit_length() - 1):
                totals = totals + swap(totals, axis, 1 << bit)
    else:
        parts = gain_rows[0].reshape(2, LANES) * jnp.asarray(places).reshape(2, LANES)
        totals = jnp.sum(jnp.transpose(parts[:, 2:].reshape(2, 3, 42), (1, 0, 2)).reshape(3, 84), axis=1)
    rms = jnp.sqrt(totals / (row_len * width * dp * rep))
    return (
        output,
        grad_tokens,
        rms,
        jnp.concatenate([pair_columns(0), pair_columns(1), pair_columns(2)], axis=1),
        sides(wide_rows, ff_half, half),
        pair_columns(3),
        gain_rows[:, 0],
        gain_rows[:, 1],
        sides(wide_rows, 0, ff_half),
        deep_sum,
        gain_rows[:, LANES],
        gain_rows[:, LANES + 1],
    )


def solution(mesh):
    rows = P(("dp", "rep"), None)
    line = P(("dp", "rep"))
    in_specs = (rows, P(None, ("dp", "rep")), rows, rows, rows, rows, rows, line, line, rows, rows, line, line)
    out_specs = (rows, rows, P(), rows, rows, rows, line, line, rows, rows, line, line)
    return jax.shard_map(body, mesh=mesh, in_specs=in_specs, out_specs=out_specs, check_vma=False)
```

```python
from functools import partial
import math

import jax
import jax.numpy as jnp
import numpy as np
from jax import lax
from jax.experimental import pallas as pl
from jax.experimental.pallas import tpu as pltpu
from jax.sharding import PartitionSpec as P

HEADS = 12
FREQS = 192
BLOCKS = 16
LANES = 128
UP_CHUNK = 1024
BACK_TILE = 1536
DEEP_THREE = False
WIDE_THREE = False
COST_SCALE = 100.0
ATTEND_SCALE = 5.0
BACK_SCALES = (100.0, 100.0, 100.0)

epsilon = 1e-05
masked_value = -1e30
f32 = jnp.float32
bf16 = jnp.bfloat16
VMEM_LIMIT = 48 * 1024 * 1024


def swap(values, axis, mask):
    size = lax.axis_size(axis)
    return lax.ppermute(values, axis, [(i, i ^ mask) for i in range(size)])


def swap_core(values):
    return swap(values, "rep", 1)


def tree_stages():
    dp, rep = lax.axis_size("dp"), lax.axis_size("rep")
    half = rep // 2
    y = [[("rep", 2 * k, k) for k in range(1, half)]] if half > 1 else []
    x = [[("dp", 1, half)]]
    z_wide, z_thin = [], []
    bit = 2
    while bit < dp:
        z_thin.insert(0, [("dp", bit, bit * half)])
        bit *= 2
    bit = 2
    while bit < dp:
        if 2 * bit < dp:
            z_wide.append([("dp", k * bit, k * bit * half) for k in (1, 2, 3)])
            bit *= 4
        else:
            z_wide.append([("dp", bit, bit * half)])
            bit *= 2
    return x, y, z_wide, z_thin


def slot_chips(stages):
    rels = [0]
    for stage in stages:
        rels = rels + [rel ^ chip for _, _, chip in stage for rel in rels]
    return rels


def after(value, *others):
    return lax.optimization_barrier((value,) + others)[0] if others else value


def half_slots(firsts, orders):
    tables = []
    for rels, stages in zip(firsts, orders):
        for stage in stages:
            rels = rels + [rel ^ chip for _, _, chip in stage for rel in rels]
        tables.append(rels)
    return tables


def hold(values, others):
    return list(lax.optimization_barrier(tuple(values) + tuple(others))[: len(values)]) if others else list(values)


def gather_first(block, stages, *others):
    stack = [after(block, *others)]
    for at, stage in enumerate(stages):
        whole = stack[0] if len(stack) == 1 else jnp.concatenate(stack, axis=0)
        stack = [whole] + [swap(whole, axis, mask) for axis, mask, _ in stage]
    return stack


def columns_of(stack, start, stop):
    return jnp.concatenate([piece[:, start:stop] for piece in stack], axis=0)


def gather_rest(stack, stages):
    for stage in stages:
        whole = stack[0] if len(stack) == 1 else jnp.concatenate(stack, axis=0)
        stack = [whole] + [swap(whole, axis, mask) for axis, mask, _ in stage]
    return stack


def add_up(terms):
    total = terms[0].astype(f32)
    for term in terms[1:]:
        total = total + term.astype(f32)
    return total


def split_rows(terms, parts):
    rows = terms[0].shape[0] // parts
    return [[term[i * rows : (i + 1) * rows] for term in terms] for i in range(parts)]


class Scatter:
    def __init__(self, arrays, orders):
        self.arrays = arrays
        self.fresh = []
        self.stages = list(zip(*[order[::-1] for order in orders]))
        self.widths = [terms[0].shape[1] for terms in arrays]

    def take_in(self, others):
        fresh = hold(self.fresh, others if self.fresh else ())
        if self.joined:
            cut = self.widths[0]
            fresh = [[array[:, :cut] for array in fresh], [array[:, cut:] for array in fresh]]
        else:
            fresh = [fresh[i * self.count : (i + 1) * self.count] for i in range(len(self.arrays))]
        self.arrays = [terms + more for terms, more in zip(self.arrays, fresh)]
        self.fresh = []

    def load(self, *others):
        if self.fresh:
            self.take_in(others)
        elif others:
            self.arrays = [hold(terms, others) for terms in self.arrays]
        self.now = self.stages.pop(0)
        self.joined = len(self.now) == 2 and self.now[0] == self.now[1]
        self.count = len(self.now[0])
        self.chunks = [split_rows(terms, len(stage) + 1) for terms, stage in zip(self.arrays, self.now)]
        sends = [[add_up(chunk).astype(bf16) for chunk in chunks[1:]] for chunks in self.chunks]
        if self.joined:
            self.sends = [jnp.concatenate(pair, axis=1) for pair in zip(*sends)]
        else:
            self.sends = sum(sends, [])
        return self.sends

    def move(self):
        moves = self.now[0] if self.joined else sum(self.now, [])
        self.arrays = [chunks[0] for chunks in self.chunks]
        self.fresh = [swap(send, axis, mask) for (axis, mask, _), send in zip(moves, self.sends)]

    def step(self, *others):
        sends = self.load(*others)
        self.move()
        return sends

    def finish(self, *others):
        while self.stages:
            self.step(*others)
        self.take_in(others)
        return jnp.concatenate([add_up(terms) for terms in self.arrays], axis=1)


def natural_pieces(stack, rels, chip, fast):
    if fast:
        per = len(rels) // len(stack)
        return stack, [rels[i * per : (i + 1) * per] for i in range(len(stack))]
    whole = jnp.concatenate(stack, axis=0)
    count = len(rels)
    where = np.zeros(count, np.int32)
    for slot, rel in enumerate(rels):
        where[rel] = slot
    order = jnp.asarray(where)[chip ^ jnp.arange(count, dtype=jnp.int32)]
    whole = whole.reshape(count, whole.shape[0] // count, whole.shape[1])
    whole = jnp.take(whole, order, axis=0).reshape(-1, whole.shape[2])
    return [whole], [list(range(BLOCKS))]


def natural_halves(stacks, tables, chip, fast):
    if fast:
        done = [natural_pieces(stack, rels, chip, fast) for stack, rels in zip(stacks, tables)]
        return done[0][0] + done[1][0], done[0][1] + done[1][1]
    return natural_pieces(stacks[0] + stacks[1], tables[0] + tables[1], chip, fast)


def in_slots(whole, rels, chip, fast):
    if fast:
        return whole
    count = len(rels)
    whole = whole.reshape(count, whole.shape[0] // count, whole.shape[1])
    order = jnp.asarray(np.array(rels, np.int32)) ^ chip
    return jnp.take(whole, order, axis=0).reshape(-1, whole.shape[2])


def by_core(core, mine, other, axis):
    return jnp.where(
        core == 0,
        jnp.concatenate([mine, other], axis=axis),
        jnp.concatenate([other, mine], axis=axis),
    )


def pair_block(core, halves):
    mine = jnp.where(core == 0, halves[0], halves[1])
    send = jnp.where(core == 0, halves[1], halves[0])
    return by_core(core, mine, swap_core(send), 0)


def dot(left, right):
    return lax.dot_general(left, right, (((1,), (0,)), ((), ())), preferred_element_type=f32)


def dot_nt(left, right):
    return lax.dot_general(left, right, (((1,), (1,)), ((), ())), preferred_element_type=f32)


def run_copies(copies, sems):
    started = []
    for at, (source, target) in enumerate(copies):
        copy = pltpu.make_async_copy(source, target, sems.at[at])
        copy.start()
        started.append(copy)
    return started


def wait_all(started):
    for copy in started:
        copy.wait()


def slots_of(pieces, rels):
    return [(piece, at, rel) for piece, table in zip(pieces, rels) for at, rel in enumerate(table)]


def block_rows(index, size):
    return pl.ds(pl.multiple_of(index * size, size), size)


def pos_block(index):
    quarter, within = index // (BLOCKS // 4), index % (BLOCKS // 4)
    return ((quarter % 2) * 2 + quarter // 2) * (BLOCKS // 4) + within


def core_lanes(core, width):
    return pl.ds(pl.multiple_of(core * width, LANES), width)


def head_mask(shape, dim, which, head_dim, kind):
    place = lax.broadcasted_iota(jnp.int32, shape, dim)
    return ((place // head_dim) == which).astype(f32).astype(kind)


def attend_pairs(pairs, scale, head_dim, tables, bias, query, key, value, w_pos, probs, ctx_own, ctx_par, lhs, rhs):
    sin, cos, sin_t, cos_t, feats, feats_t = tables
    width = feats.shape[1]
    half = width // 2
    row_len = bias.shape[1]
    lhs[:, width : 2 * width] = feats[...]
    rhs[0:width, :] = feats_t[...]

    def one_pair(pair, carry):
        lanes = pl.ds(pl.multiple_of(pair * LANES, LANES), LANES)
        q_pair, k_pair, v_pair, w_pair = query[:, lanes], key[:, lanes], value[:, lanes], w_pos[:, lanes]
        rhs[2 * width : 2 * width + LANES, :] = k_pair.T
        mixed = [None, None]
        for which in (0, 1):
            lane_mask = head_mask((1, LANES), 1, which, head_dim, bf16)
            q_head = q_pair * lane_mask
            k_head = k_pair * lane_mask
            lhs[:, 2 * width :] = q_head
            for row in (0, 1):
                span = slice(row * row_len, (row + 1) * row_len)
                coeff = dot_nt(q_head[span], w_pair)
                along_sin, along_cos = coeff[:, :half], coeff[:, half:]
                sin_row, cos_row = sin[span, :], cos[span, :]
                lhs[span, 0:half] = (along_cos * sin_row - along_sin * cos_row).astype(bf16)
                lhs[span, half:width] = (along_sin * sin_row + along_cos * cos_row).astype(bf16)
                coeff = dot_nt(w_pair, k_head[span])
                along_sin, along_cos = coeff[:half], coeff[half:]
                sin_row, cos_row = sin_t[:, span], cos_t[:, span]
                rhs[width : width + half, span] = (along_cos * sin_row - along_sin * cos_row).astype(bf16)
                rhs[width + half : 2 * width, span] = (along_sin * sin_row + along_cos * cos_row).astype(bf16)
            for row in (0, 1):
                span = slice(row * row_len, (row + 1) * row_len)
                scores = dot(lhs[span, :], rhs[:, span]) * scale + bias[row]
                top = jnp.max(scores, axis=-1, keepdims=True)
                expo = jnp.exp(scores - top)
                prob = expo / jnp.sum(expo, axis=-1, keepdims=True)
                probs[pair - pairs[0], which * 2 + row] = prob
                piece = dot(prob.astype(bf16), v_pair[span] * lane_mask)
                mixed[row] = piece if mixed[row] is None else mixed[row] + piece
        ctx_own[:, lanes] = mixed[0].astype(bf16)
        ctx_par[:, lanes] = mixed[1].astype(bf16)
        return carry

    if pairs[1] - pairs[0] == 1:
        one_pair(pairs[0], 0)
    else:
        lax.fori_loop(pairs[0], pairs[1], one_pair, 0)


def project_kernel(rels, meta, own, par, *refs):
    pieces, (w_qk, w_v, w_pos, query, key, value, sems) = refs[: len(rels)], refs[len(rels) :]
    chip = meta[0]
    row_len, width = own.shape
    part = w_v.shape[1]
    rows = width // BLOCKS
    copies = []
    for piece, at, rel in slots_of(pieces, rels):
        source = piece.at[pl.ds(at * rows, rows), :]
        copies.append((source.at[:, pl.ds(0, 2 * part)], w_qk.at[block_rows(chip ^ rel, rows), :]))
        copies.append((source.at[:, pl.ds(2 * part, part)], w_v.at[block_rows(chip ^ rel, rows), :]))
        copies.append((source.at[:, pl.ds(3 * part, part)], w_pos.at[block_rows(pos_block(chip ^ rel), rows), :]))
    wait_all(run_copies(copies, sems))
    for row, tokens in enumerate((own, par)):
        span = slice(row * row_len, (row + 1) * row_len)
        query[span, :] = dot(tokens[...], w_qk[:, 0:part]).astype(bf16)
        key[span, :] = dot(tokens[...], w_qk[:, part:]).astype(bf16)
        value[span, :] = dot(tokens[...], w_v[...]).astype(bf16)


def attend_kernel(pairs, scale, head_dim, *refs):
    tables, bias, (query, key, value, w_pos), refs = refs[:6], refs[6], refs[7:11], refs[11:]
    before = pairs[0] * LANES
    if before:
        own_before, par_before = refs[:2]
        refs = refs[2:]
    probs, ctx_own, ctx_par, lhs, rhs = refs
    if before:
        ctx_own[:, 0:before] = own_before[:, 0:before]
        ctx_par[:, 0:before] = par_before[:, 0:before]
    attend_pairs(pairs, scale, head_dim, tables, bias, query, key, value, w_pos, probs, ctx_own, ctx_par, lhs, rhs)


def take_lists(refs, sizes):
    taken = []
    for size in sizes:
        taken.append(refs[:size])
        refs = refs[size:]
    return taken, refs


def vmem_spec():
    return pl.BlockSpec(memory_space=pltpu.VMEM)


def any_spec():
    return pl.BlockSpec(memory_space=pltpu.HBM)


def smem_spec():
    return pl.BlockSpec(memory_space=pltpu.SMEM)


def params(limit=VMEM_LIMIT):
    return pltpu.CompilerParams(vmem_limit_bytes=limit)


def shape(dims, kind):
    return jax.ShapeDtypeStruct(dims, kind)


def cost(flops, moved, scale=COST_SCALE):
    return pl.CostEstimate(flops=int(flops * scale), bytes_accessed=int(moved * scale), transcendentals=0)


def project(meta, own, par, pieces, rels):
    row_len, width = own.shape
    part = width // 2
    tokens = 2 * row_len
    copies = 3 * sum(map(len, rels))
    return pl.pallas_call(
        partial(project_kernel, rels),
        out_shape=[
            shape((width, 2 * part), bf16),
            shape((width, part), bf16),
            shape((width, part), bf16),
            shape((tokens, part), bf16),
            shape((tokens, part), bf16),
            shape((tokens, part), bf16),
        ],
        in_specs=[smem_spec()] + [vmem_spec()] * 2 + [any_spec()] * len(pieces),
        out_specs=[vmem_spec()] * 6,
        scratch_shapes=[pltpu.SemaphoreType.DMA((copies,))],
        compiler_params=params(),
        cost_estimate=cost(2 * 0.5e9, 6e6, ATTEND_SCALE),
        name="project",
    )(meta, own, par, *pieces)


def attend(tables, bias, query, key, value, w_pos, before, pairs, scale, head_dim):
    tokens, part = query.shape
    width = 2 * part
    row_len = tokens // 2
    return pl.pallas_call(
        partial(attend_kernel, pairs, scale, head_dim),
        out_shape=[
            shape((pairs[1] - pairs[0], 4, row_len, row_len), f32),
            shape((row_len, part), bf16),
            shape((row_len, part), bf16),
        ],
        in_specs=[vmem_spec()] * (11 + len(before)),
        out_specs=[vmem_spec()] * 3,
        scratch_shapes=[
            pltpu.VMEM((tokens, 2 * width + LANES), bf16),
            pltpu.VMEM((2 * width + LANES, tokens), bf16),
        ],
        compiler_params=params(),
        cost_estimate=cost(2 * 1.0e9, 12e6, ATTEND_SCALE),
        name="attend",
    )(*tables, bias, query, key, value, w_pos, *before)


def norm_values(values):
    centered = values - jnp.mean(values, axis=-1, keepdims=True)
    inv_std = lax.rsqrt(jnp.mean(centered * centered, axis=-1, keepdims=True) + epsilon)
    return centered * inv_std, inv_std


def norm_backward(grad, normed_vals, inv_std, gain):
    grad_normed = grad * gain
    centered_grad = grad_normed - jnp.mean(grad_normed, axis=-1, keepdims=True)
    return inv_std * (
        centered_grad - normed_vals * jnp.mean(grad_normed * normed_vals, axis=-1, keepdims=True)
    )


def column_copies(pieces, rels, chip, rows, start, size, target, lanes):
    place = pl.ds(pl.multiple_of(lanes, LANES), size)
    return [
        (piece.at[pl.ds(at * rows, rows), pl.ds(start, size)], target.at[block_rows(chip ^ rel, rows), place])
        for piece, at, rel in slots_of(pieces, rels)
    ]


def middle_kernel(wide_rels, rels, out_rels, cuts, tile, meta, ctx_mine, ctx_recv, tokens, cotangent, *refs):
    wide, refs = take_lists(refs, [len(wide_rels)] * 2)
    pieces, refs = take_lists(refs, [len(rels[0]), len(rels[1])] * 2)
    output, grad_resid, normed_low, low, grad_ctx_mine, grad_ctx_send, grad_gains, sums = refs[:8]
    grad_pre_to, grad_mine, grad_other = refs[8:11]
    w_out, w_up, w_down, act, act_grad, act_t, ordered, low_two, grad_buf, grad_pre = refs[11:21]
    out_sems, up_sems, down_sems, flush_sems, row_sems, *row_bufs = refs[21:]
    row_inputs = (ctx_mine, ctx_recv, tokens, cotangent)
    started_rows = run_copies(list(zip(row_inputs, row_bufs)), row_sems)
    ctx_mine, ctx_recv, tokens, cotangent = row_bufs
    chip, core = meta[0], meta[1]
    ff, width = w_down.shape
    half = width // 2
    rows = ff // BLOCKS // 2
    ff_half, piece_rows, side_width = ff // 2, width // BLOCKS, half + LANES
    copies_out, groups = [], []
    for side, halves in ((core, wide[0]), (1 - core, wide[1])):
        for start, size in ((0, UP_CHUNK), (UP_CHUNK, ff_half - UP_CHUNK)):
            lanes = side * ff_half + start
            groups.append((column_copies(halves, wide_rels, chip, piece_rows, start, size, w_up, lanes), lanes, size))
        copies_out += column_copies(halves, wide_rels, chip, piece_rows, ff_half, side_width, w_out, side * side_width)
    started_out = run_copies(copies_out, out_sems)
    started_up, base = [], 0
    for copies, lanes, size in groups:
        started_up.append((run_copies(copies, up_sems.at[pl.ds(base, len(copies))]), lanes, size))
        base += len(copies)
    copies = []
    for side, chunks in ((core, pieces[:2]), (1 - core, pieces[2:])):
        for i in (0, 1):
            for piece, at, rel in slots_of(chunks[i], rels[i]):
                copies.append(
                    (
                        piece.at[pl.ds(at * rows, rows), :],
                        w_down.at[block_rows((chip ^ rel) * 2 + side, rows), pl.ds(i * half, half)],
                    )
                )
    started_down = run_copies(copies, down_sems)

    wait_all(started_rows)
    wait_all(started_out)
    lanes_of = [slice(side * side_width, side * side_width + half) for side in (0, 1)]
    attn_out = jnp.concatenate(
        [
            dot(ctx_mine[...], w_out[block_rows(core, half), lanes])
            + dot(ctx_recv[...], w_out[block_rows(1 - core, half), lanes])
            for lanes in lanes_of
        ],
        axis=1,
    )
    gains_one, gains_two = [
        w_out[:, side * side_width + half : (side + 1) * side_width].astype(f32).T[0:8] for side in (0, 1)
    ]
    tokens_f = tokens[...].astype(f32)
    resid = tokens_f + attn_out
    vals_one, inv_one = norm_values(resid)
    normed_one = vals_one * gains_one[0:1, :] + gains_one[1:2, :]
    normed_low[...] = normed_one.astype(bf16)
    sums[0:1, :] = jnp.sum(tokens_f * tokens_f, axis=0, keepdims=True)
    sums[1:2, :] = jnp.sum(attn_out * attn_out, axis=0, keepdims=True)
    sums[2:3, :] = jnp.sum(resid * resid, axis=0, keepdims=True)
    sums[3:8, :] = jnp.zeros((5, width), f32)

    for copies, start, size in started_up:
        wait_all(copies)
        for at in range(0, size, tile):
            lanes = pl.ds(pl.multiple_of(start + at, tile), tile)
            pre = dot(normed_low[...], w_up[:, lanes])
            bell = 0.5 * (1.0 + lax.erf(pre * (0.5**0.5)))
            low_act = (pre * bell).astype(bf16)
            act[:, lanes] = low_act
            act_t[lanes, :] = low_act.T
            act_grad[:, lanes] = bell + pre * jnp.exp(pre * pre * -0.5) * (0.5 / math.pi) ** 0.5
    wait_all(started_down)
    vals, inv = norm_values(normed_one + dot(act[...], w_down[...]))
    gain, shift = gains_two[0:1, :], gains_two[1:2, :]
    output[...] = (vals * gain + shift).astype(bf16)
    grad = cotangent[...].astype(f32)
    grad_gains[2:3, :] = jnp.sum(grad * vals, axis=0, keepdims=True)
    grad_gains[3:4, :] = jnp.sum(grad, axis=0, keepdims=True)
    grad_gains[4:8, :] = jnp.zeros((4, width), f32)
    grad_two = norm_backward(grad, vals, inv, gain)
    low_two[...] = grad_two.astype(bf16)
    flushed = []
    for target, place in ((grad_other, 1 - core), (grad_mine, core)):
        for start, stop, order in zip(cuts, cuts[1:], out_rels):
            for slot, rel in enumerate(order):
                ordered[slot * rows : (slot + 1) * rows, :] = act_t[block_rows((chip ^ rel) * 2 + place, rows), :]
            buf = grad_buf.at[len(flushed) // (len(cuts) - 1), :, pl.ds(start, stop - start)]
            buf[...] = dot(ordered[...], low_two[:, start:stop]).astype(bf16)
            copy = pltpu.make_async_copy(buf, target.at[:, pl.ds(start, stop - start)], flush_sems.at[len(flushed)])
            copy.start()
            flushed.append(copy)

    grad = grad_two
    for at in range(0, ff, BACK_TILE):
        lanes = pl.ds(at, BACK_TILE)
        piece = (dot_nt(low_two[...], w_down[lanes, :]) * act_grad[:, lanes]).astype(bf16)
        grad_pre[:, lanes] = piece
        copy = pltpu.make_async_copy(grad_pre.at[:, lanes], grad_pre_to.at[:, lanes], flush_sems.at[len(flushed)])
        copy.start()
        flushed.append(copy)
        grad = grad + dot_nt(piece, w_up[:, lanes])
    back = norm_backward(grad, vals_one, inv_one, gains_one[0:1, :])
    grad_resid[...] = back
    low[...] = back.astype(bf16)
    for target, side in ((grad_ctx_mine, core), (grad_ctx_send, 1 - core)):
        parts = [dot_nt(low[:, i * half : (i + 1) * half], w_out[block_rows(side, half), lanes_of[i]]) for i in (0, 1)]
        target[...] = (parts[0] + parts[1]).astype(bf16)
    grad_gains[0:1, :] = jnp.sum(grad * vals_one, axis=0, keepdims=True)
    grad_gains[1:2, :] = jnp.sum(grad, axis=0, keepdims=True)
    wait_all(flushed)


def middle(meta, ctx_mine, ctx_recv, tokens, cotangent, wide, wide_rels, pieces, rels, out_rels, cuts, ff):
    count, width = tokens.shape
    half = width // 2
    tile = 512
    flat = [array for chunk in wide + pieces for array in chunk]
    slots_wide = 2 * sum(map(len, wide_rels))
    return pl.pallas_call(
        partial(middle_kernel, wide_rels, rels, out_rels, cuts, tile),
        out_shape=[
            shape((count, width), bf16),
            shape((count, width), f32),
            shape((count, width), bf16),
            shape((count, width), bf16),
            shape((count, half), bf16),
            shape((count, half), bf16),
            shape((8, width), f32),
            shape((8, width), f32),
            shape((count, ff), bf16),
        ]
        + [shape((ff // 2, width), bf16)] * 2,
        in_specs=[smem_spec()] + [any_spec()] * (4 + len(flat)),
        out_specs=[vmem_spec()] * 8 + [any_spec()] * 3,
        scratch_shapes=[
            pltpu.VMEM((width, width + 2 * LANES), bf16),
            pltpu.VMEM((width, ff), bf16),
            pltpu.VMEM((ff, width), bf16),
            pltpu.VMEM((count, ff), bf16),
            pltpu.VMEM((count, ff), f32),
            pltpu.VMEM((ff, count), bf16),
            pltpu.VMEM((ff // 2, count), bf16),
            pltpu.VMEM((count, width), bf16),
            pltpu.VMEM((2, ff // 2, width), bf16),
            pltpu.VMEM((count, ff), bf16),
            pltpu.SemaphoreType.DMA((slots_wide,)),
            pltpu.SemaphoreType.DMA((2 * slots_wide,)),
            pltpu.SemaphoreType.DMA((2 * sum(map(len, rels[0] + rels[1])),)),
            pltpu.SemaphoreType.DMA((2 * (len(cuts) - 1) + ff // BACK_TILE,)),
            pltpu.SemaphoreType.DMA((4,)),
            pltpu.VMEM((count, half), bf16),
            pltpu.VMEM((count, half), bf16),
            pltpu.VMEM((count, width), bf16),
            pltpu.VMEM((count, width), bf16),
        ],
        compiler_params=params(60 * 1024 * 1024),
        cost_estimate=cost(2 * 3.2e9, 30e6),
        name="middle",
    )(meta, ctx_mine, ctx_recv, tokens, cotangent, *flat)


def permute_rows(source, target, chip, out_rels):
    rows = source.shape[0] // BLOCKS
    for slot, rel in enumerate(out_rels):
        target[slot * rows : (slot + 1) * rows, :] = source[block_rows(chip ^ rel, rows), :]


def digit_scales(devices):
    base = 1 << ((256 // devices + 1).bit_length() - 1)
    if base < 8:
        return None
    exponents = np.full((2 * LANES, 1), 126.0)
    for half in (0, 1):
        for row in range(2, LANES):
            exponents[half * LANES + row, 0] = 123 - 3 * ((row - 2) % 42 + 42 * half)
    return np.exp2(exponents).astype(np.float32)


def digits_of(sums, places):
    row = lax.broadcasted_iota(jnp.int32, (LANES, 1), 0)
    totals = [jnp.sum(sums[i : i + 1, :], axis=1, keepdims=True) for i in range(3)]
    value = jnp.where(row < 44, totals[0], jnp.where(row < 86, totals[1], totals[2]))
    whole = jnp.floor(jnp.minimum(value / places, 2.0**30))
    return whole - 8.0 * jnp.floor(whole * 0.125)


def weight_grads_kernel(
    out_rels, cuts, meta, all_gains, sums, places, normed_in, mine_in, recv_in, low_in, grad_pre_in, *refs
):
    targets, grads, refs = refs[:2], refs[2:4], refs[4:]
    grad_pre, turned, ordered_one, ordered_two, gain_buf, in_sems, flush_sems, row_sems, *row_bufs = refs
    row_loads = run_copies(list(zip((normed_in, mine_in, recv_in, low_in), row_bufs)), row_sems)
    normed_low, ctx_mine, ctx_recv, low = row_bufs
    chip, core = meta[0], meta[1]
    width, ff = turned.shape[0], grad_pre.shape[1]
    half, ff_half = width // 2, ff // 2
    rows = width // BLOCKS
    stops = [min(cut, ff_half) for cut in cuts]
    tiles = [
        (side, place * ff_half, start, stop - start, ordered)
        for side, place in ((1, 1 - core), (0, core))
        for start, stop, ordered in zip(stops, stops[1:], (ordered_one, ordered_two))
    ]
    places_of = [pl.ds(pl.multiple_of(base + start, LANES), size) for _, base, start, size, _ in tiles]
    loads = run_copies([(grad_pre_in.at[:, lanes], grad_pre.at[:, lanes]) for lanes in places_of], in_sems)
    flushed = []

    def flush(side, start, size):
        lanes = pl.ds(start, size)
        copy = pltpu.make_async_copy(grads[side].at[:, lanes], targets[side].at[:, lanes], flush_sems.at[len(flushed)])
        copy.start()
        flushed.append(copy)

    row_loads[0].wait()
    turned[...] = normed_low[...].T
    permute_rows(turned, ordered_one, chip, out_rels[0])
    permute_rows(turned, ordered_two, chip, out_rels[1])
    for load, lanes, (side, _, start, size, ordered) in zip(loads, places_of, tiles):
        load.wait()
        grads[side][:, start : start + size] = dot(ordered[...], grad_pre[:, lanes]).astype(bf16)
        flush(side, start, size)
    wait_all(row_loads[1:])
    turned[block_rows(core, half), :] = ctx_mine[...].T
    turned[block_rows(1 - core, half), :] = ctx_recv[...].T
    permute_rows(turned, ordered_two, chip, out_rels[-1])
    first, second = all_gains[0:2, :], all_gains[2:4, :]
    at_first = (core == 0).astype(f32)
    pair = (first * at_first + second * (1.0 - at_first), first * (1.0 - at_first) + second * at_first)
    for side, place in ((1, 1 - core), (0, core)):
        grad = grads[side]
        grad[:, ff_half : ff_half + half] = dot(ordered_two[...], low[:, core_lanes(place, half)]).astype(bf16)
        digits = digits_of(sums[...], places[block_rows(place, LANES), :])[2:]
        padded = jnp.concatenate([pair[side], jnp.broadcast_to(digits, (LANES - 2, width))], axis=0)
        gain_buf[...] = padded.T.astype(bf16)
        for slot, rel in enumerate(out_rels[-1]):
            grad[slot * rows : (slot + 1) * rows, ff_half + half :] = gain_buf[block_rows(chip ^ rel, rows), :]
        flush(side, ff_half, half + LANES)
    wait_all(flushed)


def weight_grads(meta, grad_pre, normed_low, low, all_gains, ctx_mine, ctx_recv, sums, places, out_rels, cuts):
    count, ff = grad_pre.shape
    width = normed_low.shape[1]
    out = (width, ff // 2 + width // 2 + LANES)
    return pl.pallas_call(
        partial(weight_grads_kernel, out_rels, cuts),
        out_shape=[shape(out, bf16)] * 2,
        in_specs=[smem_spec()] + [vmem_spec()] * 3 + [any_spec()] * 5,
        out_specs=[any_spec()] * 2,
        scratch_shapes=[pltpu.VMEM(out, bf16)] * 2
        + [pltpu.VMEM((count, ff), bf16)]
        + [pltpu.VMEM((width, count), bf16)] * 3
        + [
            pltpu.VMEM((width, LANES), bf16),
            pltpu.SemaphoreType.DMA((4,)),
            pltpu.SemaphoreType.DMA((6,)),
            pltpu.SemaphoreType.DMA((4,)),
            pltpu.VMEM((count, width), bf16),
            pltpu.VMEM((count, width // 2), bf16),
            pltpu.VMEM((count, width // 2), bf16),
            pltpu.VMEM((count, width), bf16),
        ],
        compiler_params=params(60 * 1024 * 1024),
        cost_estimate=cost(2 * 0.8e9, 10e6),
        name="weight_grads",
    )(meta, all_gains, sums, places, normed_low, ctx_mine, ctx_recv, low, grad_pre)


def attend_backward_kernel(
    out_rels, split, scale, head_dim, meta, own_t, par_t, sin, cos, sin_t, cos_t, feats, feats_t, query, key, value, w_pos, probs,
    grad_own, grad_par, grad_qkv, *refs
):
    outs, refs = (refs[:2], refs[2:]) if split else (refs[:1], refs[1:])
    grad_ctx, coeff_q, coeff_k, x2_rel, pos_buf = refs
    chip = meta[0]
    tokens, width = feats.shape
    row_len = tokens // 2
    half = width // 2
    grad_ctx[0:row_len, :] = grad_own[...]
    grad_ctx[row_len:, :] = grad_par[...]
    q_pair, k_pair, v_pair, w_pair, g_pair = query[...], key[...], value[...], w_pos[...], grad_ctx[...]
    q_t, v_t, g_t, w_t = q_pair.T, v_pair.T, g_pair.T, w_pair.T
    grad_q = [None, None]
    grad_k = [None, None]
    grad_v = [None, None]

    def plus(total, term):
        return term if total is None else total + term

    grad_q_coeff = None
    grad_k_coeff = None
    pos_q = None
    pos_k = None
    for which in (0, 1):
        lane_mask = head_mask((1, LANES), 1, which, head_dim, bf16)
        row_mask = head_mask((LANES, 1), 0, which, head_dim, bf16)
        k_head, g_head, w_head = k_pair * lane_mask, g_pair * lane_mask, w_pair * lane_mask
        q_t_head, g_t_head, w_t_head = q_t * row_mask, g_t * row_mask, w_t * row_mask
        for row in (0, 1):
            span = slice(row * row_len, (row + 1) * row_len)
            prob = probs[0, which * 2 + row]
            grad_probs = dot(g_head[span], v_t[:, span])
            inner = jnp.sum(prob * grad_probs, axis=-1, keepdims=True)
            grad_scores = (prob * (grad_probs - inner) * scale).astype(bf16)
            grad_v[row] = plus(grad_v[row], dot(g_t_head[:, span], prob.astype(bf16)))
            grad_k[row] = plus(grad_k[row], dot(q_t_head[:, span], grad_scores))
            grad_q[row] = plus(grad_q[row], dot(grad_scores, k_head[span]))
            pos = dot(grad_scores, feats[span, :])
            first, second = pos[:, :half], pos[:, half:]
            sin_row, cos_row = sin[span, :], cos[span, :]
            coeff_q[span, 0:half] = (second * sin_row - first * cos_row).astype(bf16)
            coeff_q[span, half:] = (first * sin_row + second * cos_row).astype(bf16)
            pos = dot(feats_t[:, span], grad_scores)
            first, second = pos[:half], pos[half:]
            sin_row, cos_row = sin_t[:, span], cos_t[:, span]
            coeff_k[0:half, span] = (second * sin_row - first * cos_row).astype(bf16)
            coeff_k[half:, span] = (first * sin_row + second * cos_row).astype(bf16)
        grad_q_coeff = plus(grad_q_coeff, dot(coeff_q[...], w_head))
        grad_k_coeff = plus(grad_k_coeff, dot(w_t_head, coeff_k[...]))
        pos_q = plus(pos_q, dot(q_t_head, coeff_q[...]))
        pos_k = plus(pos_k, dot(coeff_k[...], k_head))
    d_q = (jnp.concatenate(grad_q, axis=0) + grad_q_coeff).astype(bf16)
    d_k = (jnp.concatenate(grad_k, axis=1) + grad_k_coeff).astype(bf16).T
    d_v = jnp.concatenate(grad_v, axis=1).astype(bf16).T
    grad_qkv[:, 0:LANES] = d_q
    grad_qkv[:, LANES : 2 * LANES] = d_k
    grad_qkv[:, 2 * LANES :] = d_v
    pos_buf[...] = (pos_k + pos_q.T).astype(bf16)
    rows = width // BLOCKS
    cuts = (0, 2 * LANES, 3 * LANES) if split else (0, 3 * LANES)
    for at, out in enumerate(outs):
        size = cuts[at + 1] - cuts[at]
        permute_rows(own_t, x2_rel.at[:, 0:row_len], chip, out_rels[at])
        permute_rows(par_t, x2_rel.at[:, row_len:], chip, out_rels[at])
        out[:, 0:size] = dot(x2_rel[...], grad_qkv[:, cuts[at] : cuts[at + 1]]).astype(bf16)
    for slot, rel in enumerate(out_rels[-1]):
        outs[-1][slot * rows : (slot + 1) * rows, size:] = pos_buf[block_rows(pos_block(chip ^ rel), rows), :]


def attend_backward(
    meta, pair, own_t, par_t, tables, query, key, value, w_pos, probs, place, grad_own, grad_par, out_rels, scale, head_dim
):
    width, row_len = own_t.shape
    tokens = 2 * row_len

    def whole(array):
        return pl.BlockSpec(array.shape, lambda i: (0,) * array.ndim)

    def columns(rows):
        return pl.BlockSpec((rows, LANES), lambda i: (0, pair))

    split = len(out_rels) > 1
    pieces = [shape((width, (2 if split else 4) * LANES), bf16)] * (2 if split else 1)
    return pl.pallas_call(
        partial(attend_backward_kernel, out_rels, split, scale, head_dim),
        grid=(1,),
        out_shape=[shape((tokens, 3 * LANES), bf16)] + pieces,
        in_specs=[smem_spec(), whole(own_t), whole(par_t)]
        + [whole(table) for table in tables]
        + [columns(tokens)] * 3
        + [columns(width), pl.BlockSpec((1, 4, row_len, row_len), lambda i: (place, 0, 0, 0))]
        + [columns(row_len)] * 2,
        out_specs=[pl.BlockSpec((tokens, 3 * LANES), lambda i: (0, 0))]
        + [pl.BlockSpec(piece.shape, lambda i: (0, 0)) for piece in pieces],
        scratch_shapes=[
            pltpu.VMEM((tokens, LANES), bf16),
            pltpu.VMEM((tokens, width), bf16),
            pltpu.VMEM((width, tokens), bf16),
            pltpu.VMEM((width, tokens), bf16),
            pltpu.VMEM((width, LANES), bf16),
        ],
        compiler_params=params(),
        cost_estimate=cost(2 * 1.3e9, 10e6, BACK_SCALES[pair]),
        name="attend_backward",
    )(meta, own_t, par_t, *tables, query, key, value, w_pos, probs, grad_own, grad_par)


def row_tables(boxes):
    rates = jnp.exp(jnp.arange(FREQS, dtype=f32) * (-math.log(10000.0) / FREQS))
    angles = boxes.astype(f32)[:, :, None] * rates[None, None, :]
    angles = jnp.transpose(angles, (1, 0, 2)).reshape(boxes.shape[1], 2 * FREQS)
    sin, cos = jnp.sin(angles), jnp.cos(angles)
    feats = jnp.concatenate([sin, cos], axis=1).astype(bf16)
    return sin, cos, sin.T, cos.T, feats, feats.T


def body(
    tokens_in, boxes, page_lengths, cotangent, w_qkv, w_out, w_pos, gain_attn, bias_attn, w_up, w_down, gain_ffn, bias_ffn
):
    row_len, width = tokens_in.shape
    ff = w_up.shape[1]
    half, ff_half = width // 2, ff // 2
    head_dim = width // HEADS
    scale = head_dim ** (-0.5)
    dp, rep = lax.axis_size("dp"), lax.axis_size("rep")
    chips = dp * rep // 2
    core = lax.axis_index("rep") % 2
    chip = lax.axis_index("dp") * (rep // 2) + lax.axis_index("rep") // 2
    fast = chips == BLOCKS
    meta = jnp.stack([chip if fast else 0 * chip, core]).astype(jnp.int32)
    x, y, z_wide, z = tree_stages()
    heads_orders = (z_wide + x + y, z_wide + y + x)
    deep_orders = (x + z + y, y + z + x)
    orders = (z + x + y, z + y + x)
    heads_rels, deep_rels, all_rels = [
        [slot_chips(order) for order in pair] for pair in (heads_orders, deep_orders, orders)
    ]

    def split_columns(stack, cut, *others):
        stack = hold(stack, others)
        return [[columns_of(stack, 0, cut)], [columns_of(stack, cut, stack[0].shape[1])]]

    def move(stacks, stages, *others):
        moved = []
        for stack, stage in zip(stacks, stages):
            stack = stack[:1] + hold(stack[1:], others if len(stack) > 1 else ())
            whole = stack[0] if len(stack) == 1 else jnp.concatenate(stack, axis=0)
            moved.append([whole] + [swap(whole, axis, mask) for axis, mask, _ in stage])
        return moved

    half_xy = 2 * (rep // 2)

    def heads_z_halves(stack):
        count = len(stack) // 2
        return [[piece[0] if len(piece) == 1 else jnp.concatenate(piece, axis=0)] for piece in (stack[:count], stack[count:])]

    def sent(stacks):
        return [stack[0] for stack in stacks]

    def came(stacks):
        return [piece for stack in stacks for piece in stack[1:]]

    def joined(stacks):
        return jnp.concatenate([jnp.concatenate(stack, axis=0) for stack in stacks], axis=1)

    def heads_half(side):
        parts = [w_qkv[:, at * width + side * half : at * width + (side + 1) * half] for at in range(3)]
        return jnp.concatenate(parts + [w_pos[:, side * half : (side + 1) * half]], axis=1)

    heads_block = pair_block(core, [heads_half(s) for s in (0, 1)])
    heads_z = gather_first(heads_block, z_wide)
    tokens_late, boxes, page_lengths, w_up, w_out, w_down, gain_attn, bias_attn, gain_ffn, bias_ffn = hold(
        [tokens_in, boxes, page_lengths, w_up, w_out, w_down, gain_attn, bias_attn, gain_ffn, bias_ffn], [heads_block]
    )
    deep = move([[w_down[:, :half]], [w_down[:, half:]]], (x[0], y[0]))
    gain_sets = ((gain_attn, bias_attn), (gain_ffn, bias_ffn))
    pad = jnp.zeros((w_up.shape[0], LANES - 2), bf16)
    wide_block = pair_block(
        core,
        [
            jnp.concatenate(
                [
                    w_up[:, s * ff_half : (s + 1) * ff_half],
                    w_out[:, s * half : (s + 1) * half],
                    jnp.stack(gain_sets[s], axis=1),
                    pad,
                ],
                axis=1,
            )
            for s in (0, 1)
        ],
    )

    tokens_par = swap_core(tokens_late)
    ends = jnp.cumsum(page_lengths, axis=1)
    places = jnp.arange(row_len, dtype=jnp.int32)
    segment = jnp.sum((places[None, :, None] >= ends[:, None, :]).astype(jnp.int32), axis=2)
    marks = jnp.concatenate([boxes, segment], axis=0)
    marks_other = swap_core(marks)
    segments = jnp.stack([marks[2], marks_other[2]])
    bias = jnp.where(segments[:, :, None] == segments[:, None, :], 0.0, masked_value).astype(f32)
    tables = row_tables(jnp.concatenate([marks[:2], marks_other[:2]], axis=1))

    def thin(stack, stage):
        return stack + [swap(piece, axis, mask) for axis, mask, _ in stage for piece in stack]

    wide_rels = half_slots(
        [slot_chips(z)[: chips // (2 * half_xy)], slot_chips(z)[chips // (2 * half_xy) :]], (x + y, y + x)
    )
    firsts = slot_chips(z_wide)
    heads_rels_in = half_slots([firsts[: len(firsts) // 2], firsts[len(firsts) // 2 :]], (x + y, y + x))
    heads = move(heads_z_halves(heads_z), (x[0], y[0]))
    wide_z = [after(wide_block, *heads_z[1:])]
    for stage in z[:-1]:
        wide_z = thin(wide_z, stage)
    heads = move(heads, (y[0], x[0]), *wide_z[1:])
    wide_z = thin([jnp.concatenate(wide_z[:1] + hold(wide_z[1:], sent(heads)), axis=0)], z[-1])
    deep_z = [joined([stack[:1] + hold(stack[1:], [wide_z[0]]) for stack in deep])]
    for stage in z[:-1]:
        deep_z = thin(deep_z, stage)
    wide = move([wide_z[:1], hold(wide_z[1:], came(heads))], (x[0], y[0]))

    def tabled(stacks, rels):
        done = [natural_pieces(stack, table, chip, fast) for stack, table in zip(stacks, rels * 2)]
        return [pieces for pieces, _ in done], [table for _, table in done[:2]]

    heads, table_heads = natural_halves(heads, heads_rels_in, chip, fast)
    w_qk, w_v, w_pos_half, query, key, value = project(
        meta, after(tokens_in, *sent(wide)), tokens_par, heads, table_heads
    )
    wide = move(wide, (y[0], x[0]), query)
    deep_z = thin([jnp.concatenate(deep_z[:1] + hold(deep_z[1:], sent(wide)), axis=0)], z[-1])
    probs, ctx_mine, ctx_send = attend(
        tables, bias, after(query, deep_z[0]), key, value, w_pos_half, [], (0, half // LANES), scale, head_dim
    )
    ctx_recv = swap_core(ctx_send)
    wide = [stack[:1] + hold(stack[1:], [ctx_mine]) for stack in wide]
    deep = move(split_columns(deep_z[:1] + hold(deep_z[1:], [ctx_mine]), half), (y[0], x[0]))
    wide_other, _ = natural_halves([[swap_core(piece) for piece in stack] for stack in wide], wide_rels, chip, fast)
    wide, table_wide = natural_halves(wide, wide_rels, chip, fast)
    wide = [wide, wide_other]
    deep, table_deep = tabled(deep + [[swap_core(piece) for piece in stack] for stack in deep], deep_rels)
    if not fast:
        plain, deep = deep, [None] * 4
        for i in (0, 1):
            mine, other = [stack[0].reshape(chips, 1, -1, half) for stack in (plain[i], plain[2 + i])]
            cut = by_core(core, mine, other, 1).reshape(BLOCKS, 2, -1, half)
            deep[i] = [jnp.where(core == 0, cut[:, 0], cut[:, 1]).reshape(-1, half)]
            deep[2 + i] = [jnp.where(core == 0, cut[:, 1], cut[:, 0]).reshape(-1, half)]

    natural = list(range(BLOCKS))
    order_three = y + x + z
    rels_three = slot_chips(order_three)
    deep_cuts = (0, 256, 512, 768) if DEEP_THREE else (0, half, width)
    wide_cuts = (0, ff_half // 2, ff_half, ff_half + half + LANES) if WIDE_THREE else (0, UP_CHUNK, ff_half + half + LANES)
    sum_orders, sum_rels = orders + (order_three,), all_rels + [rels_three]
    pair_rels, out_rels = [tuple(rels) if fast else (natural,) * len(rels) for rels in (all_rels, sum_rels)]
    deep_out, wide_out = out_rels[: len(deep_cuts) - 1], out_rels[: len(wide_cuts) - 1]
    output, grad_resid_one, normed_low, grad_low, grad_ctx_mine, grad_ctx_send, all_gains, sums, grad_pre, deep_mine, deep_other = middle(
        meta, ctx_mine, ctx_recv, tokens_in, cotangent, wide, table_wide, deep, table_deep, deep_out, deep_cuts, ff
    )
    if not fast:
        mine, other = [grads.reshape(BLOCKS, 1, -1, width) for grads in (deep_mine, deep_other)]
        cut = by_core(core, mine, other, 1).reshape(chips, 2, -1, width)
        deep_mine = jnp.where(core == 0, cut[:, 0], cut[:, 1]).reshape(-1, width)
        deep_other = jnp.where(core == 0, cut[:, 1], cut[:, 0]).reshape(-1, width)

    def sums_of(terms, cuts):
        parts = [
            [in_slots(term[:, start:stop], rels, chip, fast) for term in terms]
            for start, stop, rels in zip(cuts, cuts[1:], sum_rels)
        ]
        third = Scatter(parts[2:], sum_orders[2:]) if len(parts) > 2 else None
        return Scatter(parts[:2], sum_orders[:2]), third

    def whole_sum(first, third, token):
        total = first.finish(*token)
        return total if third is None else jnp.concatenate([total, third.finish(*token)], axis=1)

    def more(scatter, token):
        return token if scatter is None else scatter.step(*token)

    places = digit_scales(dp * rep)
    deep_core = swap_core(deep_other)
    wide_mine, wide_other = weight_grads(
        meta, grad_pre, normed_low, grad_low, all_gains, ctx_mine, ctx_recv, sums,
        jnp.ones((2 * LANES, 1), f32) if places is None else jnp.asarray(places), wide_out, wide_cuts
    )
    grad_ctx_recv = swap_core(grad_ctx_send)
    s_deep, s_deep_z = sums_of([deep_mine, after(deep_core, wide_mine)], deep_cuts)
    token = s_deep.step() + more(s_deep_z, [])
    wide_core = swap_core(wide_other)
    own_t, par_t = tokens_in.T, tokens_par.T

    def back_pair(pair, rels, *others):
        return attend_backward(
            meta, pair, own_t, par_t, tables, query, key, value, w_pos_half, probs, pair, after(grad_ctx_mine, *others),
            grad_ctx_recv, rels, scale, head_dim
        )

    pair_grads = [None] * 3
    pair_grads[0], pair_zero = back_pair(0, pair_rels[:1], *token)
    s_wide, s_wide_z = sums_of([wide_mine, after(wide_core, pair_zero)], wide_cuts)
    token = s_wide.step() + more(s_wide_z, [])
    pair_grads[1], pair_one, pair_two = back_pair(1, pair_rels, *token)
    pair_grads[2], pair_three = back_pair(2, pair_rels[1:], pair_one)
    s_pair = Scatter(
        [
            [in_slots(jnp.concatenate(pieces, axis=1), rels, chip, fast)]
            for pieces, rels in zip(((pair_zero, pair_one), (pair_two, pair_three)), all_rels)
        ],
        orders,
    )
    token = s_deep.step(pair_three)
    token = more(s_deep_z, token)
    token = more(s_wide_z, token)
    token = s_wide.step(*token)
    token = s_pair.step(*token)
    grad_q, grad_k, grad_v = [
        jnp.concatenate([grads[:, i * LANES : (i + 1) * LANES] for grads in pair_grads], axis=1) for i in range(3)
    ]
    grad_x2 = dot_nt(after(jnp.concatenate([grad_q, grad_k], axis=1), *token), w_qk) + dot_nt(grad_v, w_v)
    grad_tokens = grad_resid_one + grad_x2[:row_len] + swap_core(grad_x2[row_len:])
    token = s_deep.step(*token)
    token = more(s_deep_z, token)
    token = s_wide.step(*token)
    token = more(s_wide_z, token)
    token = s_deep.step(*token)
    token = s_pair.step(*token)
    token = more(s_deep_z, token)
    token = s_wide.step(*token)
    token = s_pair.step(*token)
    deep_sum = whole_sum(s_deep, s_deep_z, token)
    wide_sum = whole_sum(s_wide, s_wide_z, token)
    pair_sum = s_pair.finish()

    def own_rows(values):
        rows = values.shape[0] // 2
        mine = jnp.where(core == 0, values[:rows], values[rows:])
        send = jnp.where(core == 0, values[rows:], values[:rows])
        return mine, swap_core(send)

    def sides(pieces, start, size):
        return by_core(core, pieces[0][:, start : start + size], pieces[1][:, start : start + size], 1)

    wide_rows = own_rows(wide_sum)
    pair_rows = own_rows(pair_sum)

    starts = [[0, 1, 2, 3], [4, 5, 6, 7], [8, 9, 10, 11]]

    def pair_columns(which):
        picked = [
            jnp.concatenate([rows[:, at[which] * LANES : (at[which] + 1) * LANES] for at in starts], axis=1)
            for rows in pair_rows
        ]
        return by_core(core, picked[0], picked[1], 1)

    gain_rows = sides(wide_rows, ff_half + half, LANES)
    if places is None:
        totals = after(jnp.sum(sums[:3], axis=1), pair_sum)
        for axis, size in (("rep", rep), ("dp", dp)):
            for bit in range(size.bit_length() - 1):
                totals = totals + swap(totals, axis, 1 << bit)
    else:
        parts = gain_rows[0].reshape(2, LANES) * jnp.asarray(places).reshape(2, LANES)
        totals = jnp.sum(jnp.transpose(parts[:, 2:].reshape(2, 3, 42), (1, 0, 2)).reshape(3, 84), axis=1)
    rms = jnp.sqrt(totals / (row_len * width * dp * rep))
    return (
        output,
        grad_tokens,
        rms,
        jnp.concatenate([pair_columns(0), pair_columns(1), pair_columns(2)], axis=1),
        sides(wide_rows, ff_half, half),
        pair_columns(3),
        gain_rows[:, 0],
        gain_rows[:, 1],
        sides(wide_rows, 0, ff_half),
        deep_sum,
        gain_rows[:, LANES],
        gain_rows[:, LANES + 1],
    )


def solution(mesh):
    rows = P(("dp", "rep"), None)
    line = P(("dp", "rep"))
    in_specs = (rows, P(None, ("dp", "rep")), rows, rows, rows, rows, rows, line, line, rows, rows, line, line)
    out_specs = (rows, rows, P(), rows, rows, rows, line, line, rows, rows, line, line)
    return jax.shard_map(body, mesh=mesh, in_specs=in_specs, out_specs=out_specs, check_vma=False)
```

```python
from functools import partial
import math

import jax
import jax.numpy as jnp
import numpy as np
from jax import lax
from jax.experimental import pallas as pl
from jax.experimental.pallas import tpu as pltpu
from jax.sharding import PartitionSpec as P

HEADS = 12
FREQS = 192
BLOCKS = 16
LANES = 128
UP_CHUNK = 1024
BACK_TILE = 1536
DEEP_THREE = False
WIDE_THREE = False
COST_SCALE = 100.0
ATTEND_SCALE = 2.0
BACK_SCALES = (100.0, 100.0, 100.0)

epsilon = 1e-05
masked_value = -1e30
f32 = jnp.float32
bf16 = jnp.bfloat16
VMEM_LIMIT = 48 * 1024 * 1024


def swap(values, axis, mask):
    size = lax.axis_size(axis)
    return lax.ppermute(values, axis, [(i, i ^ mask) for i in range(size)])


def swap_core(values):
    return swap(values, "rep", 1)


def tree_stages():
    dp, rep = lax.axis_size("dp"), lax.axis_size("rep")
    half = rep // 2
    y = [[("rep", 2 * k, k) for k in range(1, half)]] if half > 1 else []
    x = [[("dp", 1, half)]]
    z_wide, z_thin = [], []
    bit = 2
    while bit < dp:
        z_thin.insert(0, [("dp", bit, bit * half)])
        bit *= 2
    bit = 2
    while bit < dp:
        if 2 * bit < dp:
            z_wide.append([("dp", k * bit, k * bit * half) for k in (1, 2, 3)])
            bit *= 4
        else:
            z_wide.append([("dp", bit, bit * half)])
            bit *= 2
    return x, y, z_wide, z_thin


def slot_chips(stages):
    rels = [0]
    for stage in stages:
        rels = rels + [rel ^ chip for _, _, chip in stage for rel in rels]
    return rels


def after(value, *others):
    return lax.optimization_barrier((value,) + others)[0] if others else value


def half_slots(firsts, orders):
    tables = []
    for rels, stages in zip(firsts, orders):
        for stage in stages:
            rels = rels + [rel ^ chip for _, _, chip in stage for rel in rels]
        tables.append(rels)
    return tables


def hold(values, others):
    return list(lax.optimization_barrier(tuple(values) + tuple(others))[: len(values)]) if others else list(values)


def gather_first(block, stages, *others):
    stack = [after(block, *others)]
    for at, stage in enumerate(stages):
        whole = stack[0] if len(stack) == 1 else jnp.concatenate(stack, axis=0)
        stack = [whole] + [swap(whole, axis, mask) for axis, mask, _ in stage]
    return stack


def columns_of(stack, start, stop):
    return jnp.concatenate([piece[:, start:stop] for piece in stack], axis=0)


def gather_rest(stack, stages):
    for stage in stages:
        whole = stack[0] if len(stack) == 1 else jnp.concatenate(stack, axis=0)
        stack = [whole] + [swap(whole, axis, mask) for axis, mask, _ in stage]
    return stack


def add_up(terms):
    total = terms[0].astype(f32)
    for term in terms[1:]:
        total = total + term.astype(f32)
    return total


def split_rows(terms, parts):
    rows = terms[0].shape[0] // parts
    return [[term[i * rows : (i + 1) * rows] for term in terms] for i in range(parts)]


class Scatter:
    def __init__(self, arrays, orders):
        self.arrays = arrays
        self.fresh = []
        self.stages = list(zip(*[order[::-1] for order in orders]))
        self.widths = [terms[0].shape[1] for terms in arrays]

    def take_in(self, others):
        fresh = hold(self.fresh, others if self.fresh else ())
        if self.joined:
            cut = self.widths[0]
            fresh = [[array[:, :cut] for array in fresh], [array[:, cut:] for array in fresh]]
        else:
            fresh = [fresh[i * self.count : (i + 1) * self.count] for i in range(len(self.arrays))]
        self.arrays = [terms + more for terms, more in zip(self.arrays, fresh)]
        self.fresh = []

    def load(self, *others):
        if self.fresh:
            self.take_in(others)
        elif others:
            self.arrays = [hold(terms, others) for terms in self.arrays]
        self.now = self.stages.pop(0)
        self.joined = len(self.now) == 2 and self.now[0] == self.now[1]
        self.count = len(self.now[0])
        self.chunks = [split_rows(terms, len(stage) + 1) for terms, stage in zip(self.arrays, self.now)]
        sends = [[add_up(chunk).astype(bf16) for chunk in chunks[1:]] for chunks in self.chunks]
        if self.joined:
            self.sends = [jnp.concatenate(pair, axis=1) for pair in zip(*sends)]
        else:
            self.sends = sum(sends, [])
        return self.sends

    def move(self):
        moves = self.now[0] if self.joined else sum(self.now, [])
        self.arrays = [chunks[0] for chunks in self.chunks]
        self.fresh = [swap(send, axis, mask) for (axis, mask, _), send in zip(moves, self.sends)]

    def step(self, *others):
        if not self.stages:
            return list(others)
        sends = self.load(*others)
        self.move()
        return sends

    def finish(self, *others):
        while self.stages:
            self.step(*others)
        self.take_in(others)
        return jnp.concatenate([add_up(terms) for terms in self.arrays], axis=1)


def natural_pieces(stack, rels, chip, fast):
    if fast:
        per = len(rels) // len(stack)
        return stack, [rels[i * per : (i + 1) * per] for i in range(len(stack))]
    whole = jnp.concatenate(stack, axis=0)
    count = len(rels)
    where = np.zeros(count, np.int32)
    for slot, rel in enumerate(rels):
        where[rel] = slot
    order = jnp.asarray(where)[chip ^ jnp.arange(count, dtype=jnp.int32)]
    whole = whole.reshape(count, whole.shape[0] // count, whole.shape[1])
    whole = jnp.take(whole, order, axis=0).reshape(-1, whole.shape[2])
    return [whole], [list(range(BLOCKS))]


def natural_halves(stacks, tables, chip, fast):
    if fast:
        done = [natural_pieces(stack, rels, chip, fast) for stack, rels in zip(stacks, tables)]
        return done[0][0] + done[1][0], done[0][1] + done[1][1]
    return natural_pieces(stacks[0] + stacks[1], tables[0] + tables[1], chip, fast)


def in_slots(whole, rels, chip, fast):
    if fast:
        return whole
    count = len(rels)
    whole = whole.reshape(count, whole.shape[0] // count, whole.shape[1])
    order = jnp.asarray(np.array(rels, np.int32)) ^ chip
    return jnp.take(whole, order, axis=0).reshape(-1, whole.shape[2])


def by_core(core, mine, other, axis):
    return jnp.where(
        core == 0,
        jnp.concatenate([mine, other], axis=axis),
        jnp.concatenate([other, mine], axis=axis),
    )


def pair_block(core, halves):
    mine = jnp.where(core == 0, halves[0], halves[1])
    send = jnp.where(core == 0, halves[1], halves[0])
    return by_core(core, mine, swap_core(send), 0)


def dot(left, right):
    return lax.dot_general(left, right, (((1,), (0,)), ((), ())), preferred_element_type=f32)


def dot_nt(left, right):
    return lax.dot_general(left, right, (((1,), (1,)), ((), ())), preferred_element_type=f32)


def run_copies(copies, sems):
    started = []
    for at, (source, target) in enumerate(copies):
        copy = pltpu.make_async_copy(source, target, sems.at[at])
        copy.start()
        started.append(copy)
    return started


def wait_all(started):
    for copy in started:
        copy.wait()


def slots_of(pieces, rels):
    return [(piece, at, rel) for piece, table in zip(pieces, rels) for at, rel in enumerate(table)]


def block_rows(index, size):
    return pl.ds(pl.multiple_of(index * size, size), size)


def pos_block(index):
    quarter, within = index // (BLOCKS // 4), index % (BLOCKS // 4)
    return ((quarter % 2) * 2 + quarter // 2) * (BLOCKS // 4) + within


def core_lanes(core, width):
    return pl.ds(pl.multiple_of(core * width, LANES), width)


def head_mask(shape, dim, which, head_dim, kind):
    place = lax.broadcasted_iota(jnp.int32, shape, dim)
    return ((place // head_dim) == which).astype(f32).astype(kind)


def attend_pairs(pairs, scale, head_dim, tables, bias, query, key, value, w_pos, probs, ctx_own, ctx_par, lhs, rhs):
    sin, cos, sin_t, cos_t, feats, feats_t = tables
    width = feats.shape[1]
    half = width // 2
    row_len = bias.shape[1]
    lhs[:, width : 2 * width] = feats[...]
    rhs[0:width, :] = feats_t[...]

    def one_pair(pair, carry):
        lanes = pl.ds(pl.multiple_of(pair * LANES, LANES), LANES)
        q_pair, k_pair, v_pair, w_pair = query[:, lanes], key[:, lanes], value[:, lanes], w_pos[:, lanes]
        rhs[2 * width : 2 * width + LANES, :] = k_pair.T
        mixed = [None, None]
        for which in (0, 1):
            lane_mask = head_mask((1, LANES), 1, which, head_dim, bf16)
            q_head = q_pair * lane_mask
            k_head = k_pair * lane_mask
            lhs[:, 2 * width :] = q_head
            for row in (0, 1):
                span = slice(row * row_len, (row + 1) * row_len)
                coeff = dot_nt(q_head[span], w_pair)
                along_sin, along_cos = coeff[:, :half], coeff[:, half:]
                sin_row, cos_row = sin[span, :], cos[span, :]
                lhs[span, 0:half] = (along_cos * sin_row - along_sin * cos_row).astype(bf16)
                lhs[span, half:width] = (along_sin * sin_row + along_cos * cos_row).astype(bf16)
                coeff = dot_nt(w_pair, k_head[span])
                along_sin, along_cos = coeff[:half], coeff[half:]
                sin_row, cos_row = sin_t[:, span], cos_t[:, span]
                rhs[width : width + half, span] = (along_cos * sin_row - along_sin * cos_row).astype(bf16)
                rhs[width + half : 2 * width, span] = (along_sin * sin_row + along_cos * cos_row).astype(bf16)
            for row in (0, 1):
                span = slice(row * row_len, (row + 1) * row_len)
                scores = dot(lhs[span, :], rhs[:, span]) * scale + bias[row]
                top = jnp.max(scores, axis=-1, keepdims=True)
                expo = jnp.exp(scores - top)
                prob = expo / jnp.sum(expo, axis=-1, keepdims=True)
                probs[pair - pairs[0], which * 2 + row] = prob
                piece = dot(prob.astype(bf16), v_pair[span] * lane_mask)
                mixed[row] = piece if mixed[row] is None else mixed[row] + piece
        ctx_own[:, lanes] = mixed[0].astype(bf16)
        ctx_par[:, lanes] = mixed[1].astype(bf16)
        return carry

    if pairs[1] - pairs[0] == 1:
        one_pair(pairs[0], 0)
    else:
        lax.fori_loop(pairs[0], pairs[1], one_pair, 0)


def project_kernel(rels, meta, own, par, *refs):
    pieces, (w_qk, w_v, w_pos, query, key, value, sems) = refs[: len(rels)], refs[len(rels) :]
    chip = meta[0]
    row_len, width = own.shape
    part = w_v.shape[1]
    rows = width // BLOCKS
    copies = []
    for piece, at, rel in slots_of(pieces, rels):
        source = piece.at[pl.ds(at * rows, rows), :]
        copies.append((source.at[:, pl.ds(0, 2 * part)], w_qk.at[block_rows(chip ^ rel, rows), :]))
        copies.append((source.at[:, pl.ds(2 * part, part)], w_v.at[block_rows(chip ^ rel, rows), :]))
        copies.append((source.at[:, pl.ds(3 * part, part)], w_pos.at[block_rows(pos_block(chip ^ rel), rows), :]))
    wait_all(run_copies(copies, sems))
    for row, tokens in enumerate((own, par)):
        span = slice(row * row_len, (row + 1) * row_len)
        query[span, :] = dot(tokens[...], w_qk[:, 0:part]).astype(bf16)
        key[span, :] = dot(tokens[...], w_qk[:, part:]).astype(bf16)
        value[span, :] = dot(tokens[...], w_v[...]).astype(bf16)


def attend_kernel(pairs, scale, head_dim, *refs):
    tables, bias, (query, key, value, w_pos), refs = refs[:6], refs[6], refs[7:11], refs[11:]
    before = pairs[0] * LANES
    if before:
        own_before, par_before = refs[:2]
        refs = refs[2:]
    probs, ctx_own, ctx_par, lhs, rhs = refs
    if before:
        ctx_own[:, 0:before] = own_before[:, 0:before]
        ctx_par[:, 0:before] = par_before[:, 0:before]
    attend_pairs(pairs, scale, head_dim, tables, bias, query, key, value, w_pos, probs, ctx_own, ctx_par, lhs, rhs)


def take_lists(refs, sizes):
    taken = []
    for size in sizes:
        taken.append(refs[:size])
        refs = refs[size:]
    return taken, refs


def vmem_spec():
    return pl.BlockSpec(memory_space=pltpu.VMEM)


def any_spec():
    return pl.BlockSpec(memory_space=pltpu.HBM)


def smem_spec():
    return pl.BlockSpec(memory_space=pltpu.SMEM)


def params(limit=VMEM_LIMIT):
    return pltpu.CompilerParams(vmem_limit_bytes=limit)


def shape(dims, kind):
    return jax.ShapeDtypeStruct(dims, kind)


def cost(flops, moved, scale=COST_SCALE):
    return pl.CostEstimate(flops=int(flops * scale), bytes_accessed=int(moved * scale), transcendentals=0)


def project(meta, own, par, pieces, rels):
    row_len, width = own.shape
    part = width // 2
    tokens = 2 * row_len
    copies = 3 * sum(map(len, rels))
    return pl.pallas_call(
        partial(project_kernel, rels),
        out_shape=[
            shape((width, 2 * part), bf16),
            shape((width, part), bf16),
            shape((width, part), bf16),
            shape((tokens, part), bf16),
            shape((tokens, part), bf16),
            shape((tokens, part), bf16),
        ],
        in_specs=[smem_spec()] + [vmem_spec()] * 2 + [any_spec()] * len(pieces),
        out_specs=[vmem_spec()] * 6,
        scratch_shapes=[pltpu.SemaphoreType.DMA((copies,))],
        compiler_params=params(),
        cost_estimate=cost(2 * 0.5e9, 6e6, ATTEND_SCALE),
        name="project",
    )(meta, own, par, *pieces)


def attend(tables, bias, query, key, value, w_pos, before, pairs, scale, head_dim):
    tokens, part = query.shape
    width = 2 * part
    row_len = tokens // 2
    return pl.pallas_call(
        partial(attend_kernel, pairs, scale, head_dim),
        out_shape=[
            shape((pairs[1] - pairs[0], 4, row_len, row_len), f32),
            shape((row_len, part), bf16),
            shape((row_len, part), bf16),
        ],
        in_specs=[vmem_spec()] * (11 + len(before)),
        out_specs=[vmem_spec()] * 3,
        scratch_shapes=[
            pltpu.VMEM((tokens, 2 * width + LANES), bf16),
            pltpu.VMEM((2 * width + LANES, tokens), bf16),
        ],
        compiler_params=params(),
        cost_estimate=cost(2 * 1.0e9, 12e6, ATTEND_SCALE),
        name="attend",
    )(*tables, bias, query, key, value, w_pos, *before)


def norm_values(values):
    centered = values - jnp.mean(values, axis=-1, keepdims=True)
    inv_std = lax.rsqrt(jnp.mean(centered * centered, axis=-1, keepdims=True) + epsilon)
    return centered * inv_std, inv_std


def norm_backward(grad, normed_vals, inv_std, gain):
    grad_normed = grad * gain
    centered_grad = grad_normed - jnp.mean(grad_normed, axis=-1, keepdims=True)
    return inv_std * (
        centered_grad - normed_vals * jnp.mean(grad_normed * normed_vals, axis=-1, keepdims=True)
    )


def column_copies(pieces, rels, chip, rows, start, size, target, lanes):
    place = pl.ds(pl.multiple_of(lanes, LANES), size)
    return [
        (piece.at[pl.ds(at * rows, rows), pl.ds(start, size)], target.at[block_rows(chip ^ rel, rows), place])
        for piece, at, rel in slots_of(pieces, rels)
    ]


def middle_kernel(wide_rels, rels, out_rels, cuts, tile, meta, ctx_mine, ctx_recv, tokens, cotangent, *refs):
    wide, refs = take_lists(refs, [len(wide_rels)] * 2)
    pieces, refs = take_lists(refs, [len(rels[0]), len(rels[1])] * 2)
    output, grad_resid, normed_low, low, grad_ctx_mine, grad_ctx_send, grad_gains, sums = refs[:8]
    grad_pre_to, grad_mine, grad_other = refs[8:11]
    w_out, w_up, w_down, act, act_grad, act_t, ordered, low_two, grad_buf, grad_pre = refs[11:21]
    out_sems, up_sems, down_sems, flush_sems, row_sems, *row_bufs = refs[21:]
    row_inputs = (ctx_mine, ctx_recv, tokens, cotangent)
    started_rows = run_copies(list(zip(row_inputs, row_bufs)), row_sems)
    ctx_mine, ctx_recv, tokens, cotangent = row_bufs
    chip, core = meta[0], meta[1]
    ff, width = w_down.shape
    half = width // 2
    rows = ff // BLOCKS // 2
    ff_half, piece_rows, side_width = ff // 2, width // BLOCKS, half + LANES
    copies_out, groups = [], []
    for side, halves in ((core, wide[0]), (1 - core, wide[1])):
        for start, size in ((0, UP_CHUNK), (UP_CHUNK, ff_half - UP_CHUNK)):
            lanes = side * ff_half + start
            groups.append((column_copies(halves, wide_rels, chip, piece_rows, start, size, w_up, lanes), lanes, size))
        copies_out += column_copies(halves, wide_rels, chip, piece_rows, ff_half, side_width, w_out, side * side_width)
    started_out = run_copies(copies_out, out_sems)
    started_up, base = [], 0
    for copies, lanes, size in groups:
        started_up.append((run_copies(copies, up_sems.at[pl.ds(base, len(copies))]), lanes, size))
        base += len(copies)
    copies = []
    for side, chunks in ((core, pieces[:2]), (1 - core, pieces[2:])):
        for i in (0, 1):
            for piece, at, rel in slots_of(chunks[i], rels[i]):
                copies.append(
                    (
                        piece.at[pl.ds(at * rows, rows), :],
                        w_down.at[block_rows((chip ^ rel) * 2 + side, rows), pl.ds(i * half, half)],
                    )
                )
    started_down = run_copies(copies, down_sems)

    wait_all(started_rows)
    wait_all(started_out)
    lanes_of = [slice(side * side_width, side * side_width + half) for side in (0, 1)]
    attn_out = jnp.concatenate(
        [
            dot(ctx_mine[...], w_out[block_rows(core, half), lanes])
            + dot(ctx_recv[...], w_out[block_rows(1 - core, half), lanes])
            for lanes in lanes_of
        ],
        axis=1,
    )
    gains_one, gains_two = [
        w_out[:, side * side_width + half : (side + 1) * side_width].astype(f32).T[0:8] for side in (0, 1)
    ]
    tokens_f = tokens[...].astype(f32)
    resid = tokens_f + attn_out
    vals_one, inv_one = norm_values(resid)
    normed_one = vals_one * gains_one[0:1, :] + gains_one[1:2, :]
    normed_low[...] = normed_one.astype(bf16)
    sums[0:1, :] = jnp.sum(tokens_f * tokens_f, axis=0, keepdims=True)
    sums[1:2, :] = jnp.sum(attn_out * attn_out, axis=0, keepdims=True)
    sums[2:3, :] = jnp.sum(resid * resid, axis=0, keepdims=True)
    sums[3:8, :] = jnp.zeros((5, width), f32)

    for copies, start, size in started_up:
        wait_all(copies)
        for at in range(0, size, tile):
            lanes = pl.ds(pl.multiple_of(start + at, tile), tile)
            pre = dot(normed_low[...], w_up[:, lanes])
            bell = 0.5 * (1.0 + lax.erf(pre * (0.5**0.5)))
            low_act = (pre * bell).astype(bf16)
            act[:, lanes] = low_act
            act_t[lanes, :] = low_act.T
            act_grad[:, lanes] = bell + pre * jnp.exp(pre * pre * -0.5) * (0.5 / math.pi) ** 0.5
    wait_all(started_down)
    vals, inv = norm_values(normed_one + dot(act[...], w_down[...]))
    gain, shift = gains_two[0:1, :], gains_two[1:2, :]
    output[...] = (vals * gain + shift).astype(bf16)
    grad = cotangent[...].astype(f32)
    grad_gains[2:3, :] = jnp.sum(grad * vals, axis=0, keepdims=True)
    grad_gains[3:4, :] = jnp.sum(grad, axis=0, keepdims=True)
    grad_gains[4:8, :] = jnp.zeros((4, width), f32)
    grad_two = norm_backward(grad, vals, inv, gain)
    low_two[...] = grad_two.astype(bf16)
    flushed = []
    for target, place in ((grad_other, 1 - core), (grad_mine, core)):
        for start, stop, order in zip(cuts, cuts[1:], out_rels):
            for slot, rel in enumerate(order):
                ordered[slot * rows : (slot + 1) * rows, :] = act_t[block_rows((chip ^ rel) * 2 + place, rows), :]
            buf = grad_buf.at[len(flushed) // (len(cuts) - 1), :, pl.ds(start, stop - start)]
            buf[...] = dot(ordered[...], low_two[:, start:stop]).astype(bf16)
            copy = pltpu.make_async_copy(buf, target.at[:, pl.ds(start, stop - start)], flush_sems.at[len(flushed)])
            copy.start()
            flushed.append(copy)

    grad = grad_two
    for at in range(0, ff, BACK_TILE):
        lanes = pl.ds(at, BACK_TILE)
        piece = (dot_nt(low_two[...], w_down[lanes, :]) * act_grad[:, lanes]).astype(bf16)
        grad_pre[:, lanes] = piece
        copy = pltpu.make_async_copy(grad_pre.at[:, lanes], grad_pre_to.at[:, lanes], flush_sems.at[len(flushed)])
        copy.start()
        flushed.append(copy)
        grad = grad + dot_nt(piece, w_up[:, lanes])
    back = norm_backward(grad, vals_one, inv_one, gains_one[0:1, :])
    grad_resid[...] = back
    low[...] = back.astype(bf16)
    for target, side in ((grad_ctx_mine, core), (grad_ctx_send, 1 - core)):
        parts = [dot_nt(low[:, i * half : (i + 1) * half], w_out[block_rows(side, half), lanes_of[i]]) for i in (0, 1)]
        target[...] = (parts[0] + parts[1]).astype(bf16)
    grad_gains[0:1, :] = jnp.sum(grad * vals_one, axis=0, keepdims=True)
    grad_gains[1:2, :] = jnp.sum(grad, axis=0, keepdims=True)
    wait_all(flushed)


def middle(meta, ctx_mine, ctx_recv, tokens, cotangent, wide, wide_rels, pieces, rels, out_rels, cuts, ff):
    count, width = tokens.shape
    half = width // 2
    tile = 512
    flat = [array for chunk in wide + pieces for array in chunk]
    slots_wide = 2 * sum(map(len, wide_rels))
    return pl.pallas_call(
        partial(middle_kernel, wide_rels, rels, out_rels, cuts, tile),
        out_shape=[
            shape((count, width), bf16),
            shape((count, width), f32),
            shape((count, width), bf16),
            shape((count, width), bf16),
            shape((count, half), bf16),
            shape((count, half), bf16),
            shape((8, width), f32),
            shape((8, width), f32),
            shape((count, ff), bf16),
        ]
        + [shape((ff // 2, width), bf16)] * 2,
        in_specs=[smem_spec()] + [any_spec()] * (4 + len(flat)),
        out_specs=[vmem_spec()] * 8 + [any_spec()] * 3,
        scratch_shapes=[
            pltpu.VMEM((width, width + 2 * LANES), bf16),
            pltpu.VMEM((width, ff), bf16),
            pltpu.VMEM((ff, width), bf16),
            pltpu.VMEM((count, ff), bf16),
            pltpu.VMEM((count, ff), f32),
            pltpu.VMEM((ff, count), bf16),
            pltpu.VMEM((ff // 2, count), bf16),
            pltpu.VMEM((count, width), bf16),
            pltpu.VMEM((2, ff // 2, width), bf16),
            pltpu.VMEM((count, ff), bf16),
            pltpu.SemaphoreType.DMA((slots_wide,)),
            pltpu.SemaphoreType.DMA((2 * slots_wide,)),
            pltpu.SemaphoreType.DMA((2 * sum(map(len, rels[0] + rels[1])),)),
            pltpu.SemaphoreType.DMA((2 * (len(cuts) - 1) + ff // BACK_TILE,)),
            pltpu.SemaphoreType.DMA((4,)),
            pltpu.VMEM((count, half), bf16),
            pltpu.VMEM((count, half), bf16),
            pltpu.VMEM((count, width), bf16),
            pltpu.VMEM((count, width), bf16),
        ],
        compiler_params=params(60 * 1024 * 1024),
        cost_estimate=cost(2 * 3.2e9, 30e6),
        name="middle",
    )(meta, ctx_mine, ctx_recv, tokens, cotangent, *flat)


def permute_rows(source, target, chip, out_rels):
    rows = source.shape[0] // BLOCKS
    for slot, rel in enumerate(out_rels):
        target[slot * rows : (slot + 1) * rows, :] = source[block_rows(chip ^ rel, rows), :]


def digit_scales(devices):
    base = 1 << ((256 // devices + 1).bit_length() - 1)
    if base < 8:
        return None
    exponents = np.full((2 * LANES, 1), 126.0)
    for half in (0, 1):
        for row in range(2, LANES):
            exponents[half * LANES + row, 0] = 123 - 3 * ((row - 2) % 42 + 42 * half)
    return np.exp2(exponents).astype(np.float32)


def digits_of(sums, places):
    row = lax.broadcasted_iota(jnp.int32, (LANES, 1), 0)
    totals = [jnp.sum(sums[i : i + 1, :], axis=1, keepdims=True) for i in range(3)]
    value = jnp.where(row < 44, totals[0], jnp.where(row < 86, totals[1], totals[2]))
    whole = jnp.floor(jnp.minimum(value / places, 2.0**30))
    return whole - 8.0 * jnp.floor(whole * 0.125)


def weight_grads_kernel(
    out_rels, cuts, meta, all_gains, sums, places, normed_in, mine_in, recv_in, low_in, grad_pre_in, *refs
):
    targets, grads, refs = refs[:2], refs[2:4], refs[4:]
    grad_pre, turned, ordered_one, ordered_two, gain_buf, in_sems, flush_sems, row_sems, *row_bufs = refs
    row_loads = run_copies(list(zip((normed_in, mine_in, recv_in, low_in), row_bufs)), row_sems)
    normed_low, ctx_mine, ctx_recv, low = row_bufs
    chip, core = meta[0], meta[1]
    width, ff = turned.shape[0], grad_pre.shape[1]
    half, ff_half = width // 2, ff // 2
    rows = width // BLOCKS
    stops = [min(cut, ff_half) for cut in cuts]
    tiles = [
        (side, place * ff_half, start, stop - start, ordered)
        for side, place in ((1, 1 - core), (0, core))
        for start, stop, ordered in zip(stops, stops[1:], (ordered_one, ordered_two))
    ]
    places_of = [pl.ds(pl.multiple_of(base + start, LANES), size) for _, base, start, size, _ in tiles]
    loads = run_copies([(grad_pre_in.at[:, lanes], grad_pre.at[:, lanes]) for lanes in places_of], in_sems)
    flushed = []

    def flush(side, start, size):
        lanes = pl.ds(start, size)
        copy = pltpu.make_async_copy(grads[side].at[:, lanes], targets[side].at[:, lanes], flush_sems.at[len(flushed)])
        copy.start()
        flushed.append(copy)

    row_loads[0].wait()
    turned[...] = normed_low[...].T
    permute_rows(turned, ordered_one, chip, out_rels[0])
    permute_rows(turned, ordered_two, chip, out_rels[1])
    for load, lanes, (side, _, start, size, ordered) in zip(loads, places_of, tiles):
        load.wait()
        grads[side][:, start : start + size] = dot(ordered[...], grad_pre[:, lanes]).astype(bf16)
        flush(side, start, size)
    wait_all(row_loads[1:])
    turned[block_rows(core, half), :] = ctx_mine[...].T
    turned[block_rows(1 - core, half), :] = ctx_recv[...].T
    permute_rows(turned, ordered_two, chip, out_rels[-1])
    first, second = all_gains[0:2, :], all_gains[2:4, :]
    at_first = (core == 0).astype(f32)
    pair = (first * at_first + second * (1.0 - at_first), first * (1.0 - at_first) + second * at_first)
    for side, place in ((1, 1 - core), (0, core)):
        grad = grads[side]
        grad[:, ff_half : ff_half + half] = dot(ordered_two[...], low[:, core_lanes(place, half)]).astype(bf16)
        digits = digits_of(sums[...], places[block_rows(place, LANES), :])[2:]
        padded = jnp.concatenate([pair[side], jnp.broadcast_to(digits, (LANES - 2, width))], axis=0)
        gain_buf[...] = padded.T.astype(bf16)
        for slot, rel in enumerate(out_rels[-1]):
            grad[slot * rows : (slot + 1) * rows, ff_half + half :] = gain_buf[block_rows(chip ^ rel, rows), :]
        flush(side, ff_half, half + LANES)
    wait_all(flushed)


def weight_grads(meta, grad_pre, normed_low, low, all_gains, ctx_mine, ctx_recv, sums, places, out_rels, cuts):
    count, ff = grad_pre.shape
    width = normed_low.shape[1]
    out = (width, ff // 2 + width // 2 + LANES)
    return pl.pallas_call(
        partial(weight_grads_kernel, out_rels, cuts),
        out_shape=[shape(out, bf16)] * 2,
        in_specs=[smem_spec()] + [vmem_spec()] * 3 + [any_spec()] * 5,
        out_specs=[any_spec()] * 2,
        scratch_shapes=[pltpu.VMEM(out, bf16)] * 2
        + [pltpu.VMEM((count, ff), bf16)]
        + [pltpu.VMEM((width, count), bf16)] * 3
        + [
            pltpu.VMEM((width, LANES), bf16),
            pltpu.SemaphoreType.DMA((4,)),
            pltpu.SemaphoreType.DMA((6,)),
            pltpu.SemaphoreType.DMA((4,)),
            pltpu.VMEM((count, width), bf16),
            pltpu.VMEM((count, width // 2), bf16),
            pltpu.VMEM((count, width // 2), bf16),
            pltpu.VMEM((count, width), bf16),
        ],
        compiler_params=params(60 * 1024 * 1024),
        cost_estimate=cost(2 * 0.8e9, 10e6),
        name="weight_grads",
    )(meta, all_gains, sums, places, normed_low, ctx_mine, ctx_recv, low, grad_pre)


def attend_backward_kernel(
    out_rels, split, scale, head_dim, meta, own_t, par_t, sin, cos, sin_t, cos_t, feats, feats_t, query, key, value, w_pos, probs,
    grad_own, grad_par, grad_qkv, *refs
):
    outs, refs = (refs[:2], refs[2:]) if split else (refs[:1], refs[1:])
    grad_ctx, coeff_q, coeff_k, x2_rel, pos_buf = refs
    chip = meta[0]
    tokens, width = feats.shape
    row_len = tokens // 2
    half = width // 2
    grad_ctx[0:row_len, :] = grad_own[...]
    grad_ctx[row_len:, :] = grad_par[...]
    q_pair, k_pair, v_pair, w_pair, g_pair = query[...], key[...], value[...], w_pos[...], grad_ctx[...]
    q_t, v_t, g_t, w_t = q_pair.T, v_pair.T, g_pair.T, w_pair.T
    grad_q = [None, None]
    grad_k = [None, None]
    grad_v = [None, None]

    def plus(total, term):
        return term if total is None else total + term

    grad_q_coeff = None
    grad_k_coeff = None
    pos_q = None
    pos_k = None
    for which in (0, 1):
        lane_mask = head_mask((1, LANES), 1, which, head_dim, bf16)
        row_mask = head_mask((LANES, 1), 0, which, head_dim, bf16)
        k_head, g_head, w_head = k_pair * lane_mask, g_pair * lane_mask, w_pair * lane_mask
        q_t_head, g_t_head, w_t_head = q_t * row_mask, g_t * row_mask, w_t * row_mask
        for row in (0, 1):
            span = slice(row * row_len, (row + 1) * row_len)
            prob = probs[0, which * 2 + row]
            grad_probs = dot(g_head[span], v_t[:, span])
            inner = jnp.sum(prob * grad_probs, axis=-1, keepdims=True)
            grad_scores = (prob * (grad_probs - inner) * scale).astype(bf16)
            grad_v[row] = plus(grad_v[row], dot(g_t_head[:, span], prob.astype(bf16)))
            grad_k[row] = plus(grad_k[row], dot(q_t_head[:, span], grad_scores))
            grad_q[row] = plus(grad_q[row], dot(grad_scores, k_head[span]))
            pos = dot(grad_scores, feats[span, :])
            first, second = pos[:, :half], pos[:, half:]
            sin_row, cos_row = sin[span, :], cos[span, :]
            coeff_q[span, 0:half] = (second * sin_row - first * cos_row).astype(bf16)
            coeff_q[span, half:] = (first * sin_row + second * cos_row).astype(bf16)
            pos = dot(feats_t[:, span], grad_scores)
            first, second = pos[:half], pos[half:]
            sin_row, cos_row = sin_t[:, span], cos_t[:, span]
            coeff_k[0:half, span] = (second * sin_row - first * cos_row).astype(bf16)
            coeff_k[half:, span] = (first * sin_row + second * cos_row).astype(bf16)
        grad_q_coeff = plus(grad_q_coeff, dot(coeff_q[...], w_head))
        grad_k_coeff = plus(grad_k_coeff, dot(w_t_head, coeff_k[...]))
        pos_q = plus(pos_q, dot(q_t_head, coeff_q[...]))
        pos_k = plus(pos_k, dot(coeff_k[...], k_head))
    d_q = (jnp.concatenate(grad_q, axis=0) + grad_q_coeff).astype(bf16)
    d_k = (jnp.concatenate(grad_k, axis=1) + grad_k_coeff).astype(bf16).T
    d_v = jnp.concatenate(grad_v, axis=1).astype(bf16).T
    grad_qkv[:, 0:LANES] = d_q
    grad_qkv[:, LANES : 2 * LANES] = d_k
    grad_qkv[:, 2 * LANES :] = d_v
    pos_buf[...] = (pos_k + pos_q.T).astype(bf16)
    rows = width // BLOCKS
    cuts = (0, 2 * LANES, 3 * LANES) if split else (0, 3 * LANES)
    for at, out in enumerate(outs):
        size = cuts[at + 1] - cuts[at]
        permute_rows(own_t, x2_rel.at[:, 0:row_len], chip, out_rels[at])
        permute_rows(par_t, x2_rel.at[:, row_len:], chip, out_rels[at])
        out[:, 0:size] = dot(x2_rel[...], grad_qkv[:, cuts[at] : cuts[at + 1]]).astype(bf16)
    for slot, rel in enumerate(out_rels[-1]):
        outs[-1][slot * rows : (slot + 1) * rows, size:] = pos_buf[block_rows(pos_block(chip ^ rel), rows), :]


def attend_backward(
    meta, pair, own_t, par_t, tables, query, key, value, w_pos, probs, place, grad_own, grad_par, out_rels, scale, head_dim
):
    width, row_len = own_t.shape
    tokens = 2 * row_len

    def whole(array):
        return pl.BlockSpec(array.shape, lambda i: (0,) * array.ndim)

    def columns(rows):
        return pl.BlockSpec((rows, LANES), lambda i: (0, pair))

    split = len(out_rels) > 1
    pieces = [shape((width, (2 if split else 4) * LANES), bf16)] * (2 if split else 1)
    return pl.pallas_call(
        partial(attend_backward_kernel, out_rels, split, scale, head_dim),
        grid=(1,),
        out_shape=[shape((tokens, 3 * LANES), bf16)] + pieces,
        in_specs=[smem_spec(), whole(own_t), whole(par_t)]
        + [whole(table) for table in tables]
        + [columns(tokens)] * 3
        + [columns(width), pl.BlockSpec((1, 4, row_len, row_len), lambda i: (place, 0, 0, 0))]
        + [columns(row_len)] * 2,
        out_specs=[pl.BlockSpec((tokens, 3 * LANES), lambda i: (0, 0))]
        + [pl.BlockSpec(piece.shape, lambda i: (0, 0)) for piece in pieces],
        scratch_shapes=[
            pltpu.VMEM((tokens, LANES), bf16),
            pltpu.VMEM((tokens, width), bf16),
            pltpu.VMEM((width, tokens), bf16),
            pltpu.VMEM((width, tokens), bf16),
            pltpu.VMEM((width, LANES), bf16),
        ],
        compiler_params=params(),
        cost_estimate=cost(2 * 1.3e9, 10e6, BACK_SCALES[pair]),
        name="attend_backward",
    )(meta, own_t, par_t, *tables, query, key, value, w_pos, probs, grad_own, grad_par)


def row_tables(boxes):
    rates = jnp.exp(jnp.arange(FREQS, dtype=f32) * (-math.log(10000.0) / FREQS))
    angles = boxes.astype(f32)[:, :, None] * rates[None, None, :]
    angles = jnp.transpose(angles, (1, 0, 2)).reshape(boxes.shape[1], 2 * FREQS)
    sin, cos = jnp.sin(angles), jnp.cos(angles)
    feats = jnp.concatenate([sin, cos], axis=1).astype(bf16)
    return sin, cos, sin.T, cos.T, feats, feats.T


def body(
    tokens_in, boxes, page_lengths, cotangent, w_qkv, w_out, w_pos, gain_attn, bias_attn, w_up, w_down, gain_ffn, bias_ffn
):
    row_len, width = tokens_in.shape
    ff = w_up.shape[1]
    half, ff_half = width // 2, ff // 2
    head_dim = width // HEADS
    scale = head_dim ** (-0.5)
    dp, rep = lax.axis_size("dp"), lax.axis_size("rep")
    chips = dp * rep // 2
    core = lax.axis_index("rep") % 2
    chip = lax.axis_index("dp") * (rep // 2) + lax.axis_index("rep") // 2
    fast = chips == BLOCKS
    meta = jnp.stack([chip if fast else 0 * chip, core]).astype(jnp.int32)
    x, y, z_wide, z = tree_stages()
    heads_orders = (z_wide + x + y, z_wide + y + x)
    deep_orders = (x + z + y, y + z + x)
    orders = (z + x + y, z + y + x)
    heads_rels, deep_rels, all_rels = [
        [slot_chips(order) for order in pair] for pair in (heads_orders, deep_orders, orders)
    ]

    def split_columns(stack, cut, *others):
        stack = hold(stack, others)
        return [[columns_of(stack, 0, cut)], [columns_of(stack, cut, stack[0].shape[1])]]

    def move(stacks, stages, *others):
        moved = []
        for stack, stage in zip(stacks, stages):
            stack = stack[:1] + hold(stack[1:], others if len(stack) > 1 else ())
            whole = stack[0] if len(stack) == 1 else jnp.concatenate(stack, axis=0)
            moved.append([whole] + [swap(whole, axis, mask) for axis, mask, _ in stage])
        return moved

    half_xy = 2 * (rep // 2)

    def heads_z_halves(stack):
        count = len(stack) // 2
        return [[piece[0] if len(piece) == 1 else jnp.concatenate(piece, axis=0)] for piece in (stack[:count], stack[count:])]

    def sent(stacks):
        return [stack[0] for stack in stacks]

    def came(stacks):
        return [piece for stack in stacks for piece in stack[1:]]

    def joined(stacks):
        return jnp.concatenate([jnp.concatenate(stack, axis=0) for stack in stacks], axis=1)

    def heads_half(side):
        parts = [w_qkv[:, at * width + side * half : at * width + (side + 1) * half] for at in range(3)]
        return jnp.concatenate(parts + [w_pos[:, side * half : (side + 1) * half]], axis=1)

    heads_block = pair_block(core, [heads_half(s) for s in (0, 1)])
    heads_z = gather_first(heads_block, z_wide)
    tokens_late, boxes, page_lengths, w_up, w_out, w_down, gain_attn, bias_attn, gain_ffn, bias_ffn = hold(
        [tokens_in, boxes, page_lengths, w_up, w_out, w_down, gain_attn, bias_attn, gain_ffn, bias_ffn], [heads_block]
    )
    deep = move([[w_down[:, :half]], [w_down[:, half:]]], (x[0], y[0]))
    gain_sets = ((gain_attn, bias_attn), (gain_ffn, bias_ffn))
    pad = jnp.zeros((w_up.shape[0], LANES - 2), bf16)
    wide_block = pair_block(
        core,
        [
            jnp.concatenate(
                [
                    w_up[:, s * ff_half : (s + 1) * ff_half],
                    w_out[:, s * half : (s + 1) * half],
                    jnp.stack(gain_sets[s], axis=1),
                    pad,
                ],
                axis=1,
            )
            for s in (0, 1)
        ],
    )

    tokens_par = swap_core(tokens_late)
    ends = jnp.cumsum(page_lengths, axis=1)
    places = jnp.arange(row_len, dtype=jnp.int32)
    segment = jnp.sum((places[None, :, None] >= ends[:, None, :]).astype(jnp.int32), axis=2)
    marks = jnp.concatenate([boxes, segment], axis=0)
    marks_other = swap_core(marks)
    segments = jnp.stack([marks[2], marks_other[2]])
    bias = jnp.where(segments[:, :, None] == segments[:, None, :], 0.0, masked_value).astype(f32)
    tables = row_tables(jnp.concatenate([marks[:2], marks_other[:2]], axis=1))

    def thin(stack, stage):
        return stack + [swap(piece, axis, mask) for axis, mask, _ in stage for piece in stack]

    wide_rels = half_slots(
        [slot_chips(z)[: chips // (2 * half_xy)], slot_chips(z)[chips // (2 * half_xy) :]], (x + y, y + x)
    )
    firsts = slot_chips(z_wide)
    heads_rels_in = half_slots([firsts[: len(firsts) // 2], firsts[len(firsts) // 2 :]], (x + y, y + x))
    heads = move(heads_z_halves(heads_z), (x[0], y[0]))
    wide_z = [after(wide_block, *heads_z[1:])]
    for stage in z[:-1]:
        wide_z = thin(wide_z, stage)
    heads = move(heads, (y[0], x[0]), *wide_z[1:])
    wide_z = thin([jnp.concatenate(wide_z[:1] + hold(wide_z[1:], sent(heads)), axis=0)], z[-1])
    deep_z = [joined([stack[:1] + hold(stack[1:], [wide_z[0]]) for stack in deep])]
    for stage in z[:-1]:
        deep_z = thin(deep_z, stage)
    wide = move([wide_z[:1], hold(wide_z[1:], came(heads))], (x[0], y[0]))

    def tabled(stacks, rels):
        done = [natural_pieces(stack, table, chip, fast) for stack, table in zip(stacks, rels * 2)]
        return [pieces for pieces, _ in done], [table for _, table in done[:2]]

    heads, table_heads = natural_halves(heads, heads_rels_in, chip, fast)
    w_qk, w_v, w_pos_half, query, key, value = project(
        meta, after(tokens_in, *sent(wide)), tokens_par, heads, table_heads
    )
    wide = move(wide, (y[0], x[0]), query)
    deep_z = thin([jnp.concatenate(deep_z[:1] + hold(deep_z[1:], sent(wide)), axis=0)], z[-1])
    probs, ctx_mine, ctx_send = attend(
        tables, bias, after(query, deep_z[0]), key, value, w_pos_half, [], (0, half // LANES), scale, head_dim
    )
    ctx_recv = swap_core(ctx_send)
    wide = [stack[:1] + hold(stack[1:], [ctx_mine]) for stack in wide]
    deep = move(split_columns(deep_z[:1] + hold(deep_z[1:], [ctx_mine]), half), (y[0], x[0]))
    wide_other, _ = natural_halves([[swap_core(piece) for piece in stack] for stack in wide], wide_rels, chip, fast)
    wide, table_wide = natural_halves(wide, wide_rels, chip, fast)
    wide = [wide, wide_other]
    deep, table_deep = tabled(deep + [[swap_core(piece) for piece in stack] for stack in deep], deep_rels)
    if not fast:
        plain, deep = deep, [None] * 4
        for i in (0, 1):
            mine, other = [stack[0].reshape(chips, 1, -1, half) for stack in (plain[i], plain[2 + i])]
            cut = by_core(core, mine, other, 1).reshape(BLOCKS, 2, -1, half)
            deep[i] = [jnp.where(core == 0, cut[:, 0], cut[:, 1]).reshape(-1, half)]
            deep[2 + i] = [jnp.where(core == 0, cut[:, 1], cut[:, 0]).reshape(-1, half)]

    natural = list(range(BLOCKS))
    order_three = y + x + z
    rels_three = slot_chips(order_three)
    deep_cuts = (0, 256, 512, 768) if DEEP_THREE else (0, half, width)
    wide_cuts = (0, ff_half // 2, ff_half, ff_half + half + LANES) if WIDE_THREE else (0, UP_CHUNK, ff_half + half + LANES)
    sum_orders, sum_rels = orders + (order_three,), all_rels + [rels_three]
    pair_rels, out_rels = [tuple(rels) if fast else (natural,) * len(rels) for rels in (all_rels, sum_rels)]
    deep_out, wide_out = out_rels[: len(deep_cuts) - 1], out_rels[: len(wide_cuts) - 1]
    output, grad_resid_one, normed_low, grad_low, grad_ctx_mine, grad_ctx_send, all_gains, sums, grad_pre, deep_mine, deep_other = middle(
        meta, ctx_mine, ctx_recv, tokens_in, cotangent, wide, table_wide, deep, table_deep, deep_out, deep_cuts, ff
    )
    if not fast:
        mine, other = [grads.reshape(BLOCKS, 1, -1, width) for grads in (deep_mine, deep_other)]
        cut = by_core(core, mine, other, 1).reshape(chips, 2, -1, width)
        deep_mine = jnp.where(core == 0, cut[:, 0], cut[:, 1]).reshape(-1, width)
        deep_other = jnp.where(core == 0, cut[:, 1], cut[:, 0]).reshape(-1, width)

    def sums_of(terms, cuts):
        parts = [
            [in_slots(term[:, start:stop], rels, chip, fast) for term in terms]
            for start, stop, rels in zip(cuts, cuts[1:], sum_rels)
        ]
        third = Scatter(parts[2:], sum_orders[2:]) if len(parts) > 2 else None
        return Scatter(parts[:2], sum_orders[:2]), third

    def whole_sum(first, third, token):
        total = first.finish(*token)
        return total if third is None else jnp.concatenate([total, third.finish(*token)], axis=1)

    def more(scatter, token):
        return token if scatter is None else scatter.step(*token)

    places = digit_scales(dp * rep)
    deep_core = swap_core(deep_other)
    wide_mine, wide_other = weight_grads(
        meta, grad_pre, normed_low, grad_low, all_gains, ctx_mine, ctx_recv, sums,
        jnp.ones((2 * LANES, 1), f32) if places is None else jnp.asarray(places), wide_out, wide_cuts
    )
    grad_ctx_recv = swap_core(grad_ctx_send)
    s_deep, s_deep_z = sums_of([deep_mine, after(deep_core, wide_mine)], deep_cuts)
    token = s_deep.step() + more(s_deep_z, [])
    wide_core = swap_core(wide_other)
    own_t, par_t = tokens_in.T, tokens_par.T

    def back_pair(pair, rels, *others):
        return attend_backward(
            meta, pair, own_t, par_t, tables, query, key, value, w_pos_half, probs, pair, after(grad_ctx_mine, *others),
            grad_ctx_recv, rels, scale, head_dim
        )

    pair_grads = [None] * 3
    pair_grads[0], pair_zero = back_pair(0, pair_rels[:1], *token)
    s_wide, s_wide_z = sums_of([wide_mine, after(wide_core, pair_zero)], wide_cuts)
    token = s_wide.step() + more(s_wide_z, [])
    pair_grads[1], pair_one, pair_two = back_pair(1, pair_rels, *token)
    pair_grads[2], pair_three = back_pair(2, pair_rels[1:], pair_one)
    s_pair = Scatter(
        [
            [in_slots(jnp.concatenate(pieces, axis=1), rels, chip, fast)]
            for pieces, rels in zip(((pair_zero, pair_one), (pair_two, pair_three)), all_rels)
        ],
        orders,
    )
    token = s_deep.step(pair_three)
    token = more(s_deep_z, token)
    token = more(s_wide_z, token)
    token = s_wide.step(*token)
    token = s_pair.step(*token)
    grad_q, grad_k, grad_v = [
        jnp.concatenate([grads[:, i * LANES : (i + 1) * LANES] for grads in pair_grads], axis=1) for i in range(3)
    ]
    grad_x2 = dot_nt(after(jnp.concatenate([grad_q, grad_k], axis=1), *token), w_qk) + dot_nt(grad_v, w_v)
    grad_tokens = grad_resid_one + grad_x2[:row_len] + swap_core(grad_x2[row_len:])
    token = s_deep.step(*token)
    token = more(s_deep_z, token)
    token = s_wide.step(*token)
    token = more(s_wide_z, token)
    token = s_deep.step(*token)
    token = s_pair.step(*token)
    token = more(s_deep_z, token)
    token = s_wide.step(*token)
    token = s_pair.step(*token)
    deep_sum = whole_sum(s_deep, s_deep_z, token)
    wide_sum = whole_sum(s_wide, s_wide_z, token)
    pair_sum = s_pair.finish()

    def own_rows(values):
        rows = values.shape[0] // 2
        mine = jnp.where(core == 0, values[:rows], values[rows:])
        send = jnp.where(core == 0, values[rows:], values[:rows])
        return mine, swap_core(send)

    def sides(pieces, start, size):
        return by_core(core, pieces[0][:, start : start + size], pieces[1][:, start : start + size], 1)

    wide_rows = own_rows(wide_sum)
    pair_rows = own_rows(pair_sum)

    starts = [[0, 1, 2, 3], [4, 5, 6, 7], [8, 9, 10, 11]]

    def pair_columns(which):
        picked = [
            jnp.concatenate([rows[:, at[which] * LANES : (at[which] + 1) * LANES] for at in starts], axis=1)
            for rows in pair_rows
        ]
        return by_core(core, picked[0], picked[1], 1)

    gain_rows = sides(wide_rows, ff_half + half, LANES)
    if places is None:
        totals = after(jnp.sum(sums[:3], axis=1), pair_sum)
        for axis, size in (("rep", rep), ("dp", dp)):
            for bit in range(size.bit_length() - 1):
                totals = totals + swap(totals, axis, 1 << bit)
    else:
        parts = gain_rows[0].reshape(2, LANES) * jnp.asarray(places).reshape(2, LANES)
        totals = jnp.sum(jnp.transpose(parts[:, 2:].reshape(2, 3, 42), (1, 0, 2)).reshape(3, 84), axis=1)
    rms = jnp.sqrt(totals / (row_len * width * dp * rep))
    return (
        output,
        grad_tokens,
        rms,
        jnp.concatenate([pair_columns(0), pair_columns(1), pair_columns(2)], axis=1),
        sides(wide_rows, ff_half, half),
        pair_columns(3),
        gain_rows[:, 0],
        gain_rows[:, 1],
        sides(wide_rows, 0, ff_half),
        deep_sum,
        gain_rows[:, LANES],
        gain_rows[:, LANES + 1],
    )


def solution(mesh):
    rows = P(("dp", "rep"), None)
    line = P(("dp", "rep"))
    in_specs = (rows, P(None, ("dp", "rep")), rows, rows, rows, rows, rows, line, line, rows, rows, line, line)
    out_specs = (rows, rows, P(), rows, rows, rows, line, line, rows, rows, line, line)
    return jax.shard_map(body, mesh=mesh, in_specs=in_specs, out_specs=out_specs, check_vma=False)
```

```python
from functools import partial
import math

import jax
import jax.numpy as jnp
import numpy as np
from jax import lax
from jax.experimental import pallas as pl
from jax.experimental.pallas import tpu as pltpu
from jax.sharding import PartitionSpec as P

HEADS = 12
FREQS = 192
BLOCKS = 16
LANES = 128
UP_CHUNK = 1024
BACK_TILE = 1536
DEEP_THREE = False
WIDE_THREE = False
COST_SCALE = 100.0
ATTEND_SCALE = 3.0
BACK_SCALES = (100.0, 100.0, 100.0)

epsilon = 1e-05
masked_value = -1e30
f32 = jnp.float32
bf16 = jnp.bfloat16
VMEM_LIMIT = 48 * 1024 * 1024


def swap(values, axis, mask):
    size = lax.axis_size(axis)
    return lax.ppermute(values, axis, [(i, i ^ mask) for i in range(size)])


def swap_core(values):
    return swap(values, "rep", 1)


def tree_stages():
    dp, rep = lax.axis_size("dp"), lax.axis_size("rep")
    half = rep // 2
    y = [[("rep", 2 * k, k) for k in range(1, half)]] if half > 1 else []
    x = [[("dp", 1, half)]]
    z_wide, z_thin = [], []
    bit = 2
    while bit < dp:
        z_thin.insert(0, [("dp", bit, bit * half)])
        bit *= 2
    bit = 2
    while bit < dp:
        if 2 * bit < dp:
            z_wide.append([("dp", k * bit, k * bit * half) for k in (1, 2, 3)])
            bit *= 4
        else:
            z_wide.append([("dp", bit, bit * half)])
            bit *= 2
    return x, y, z_wide, z_thin


def slot_chips(stages):
    rels = [0]
    for stage in stages:
        rels = rels + [rel ^ chip for _, _, chip in stage for rel in rels]
    return rels


def after(value, *others):
    return lax.optimization_barrier((value,) + others)[0] if others else value


def half_slots(firsts, orders):
    tables = []
    for rels, stages in zip(firsts, orders):
        for stage in stages:
            rels = rels + [rel ^ chip for _, _, chip in stage for rel in rels]
        tables.append(rels)
    return tables


def hold(values, others):
    return list(lax.optimization_barrier(tuple(values) + tuple(others))[: len(values)]) if others else list(values)


def gather_first(block, stages, *others):
    stack = [after(block, *others)]
    for at, stage in enumerate(stages):
        whole = stack[0] if len(stack) == 1 else jnp.concatenate(stack, axis=0)
        stack = [whole] + [swap(whole, axis, mask) for axis, mask, _ in stage]
    return stack


def columns_of(stack, start, stop):
    return jnp.concatenate([piece[:, start:stop] for piece in stack], axis=0)


def gather_rest(stack, stages):
    for stage in stages:
        whole = stack[0] if len(stack) == 1 else jnp.concatenate(stack, axis=0)
        stack = [whole] + [swap(whole, axis, mask) for axis, mask, _ in stage]
    return stack


def add_up(terms):
    total = terms[0].astype(f32)
    for term in terms[1:]:
        total = total + term.astype(f32)
    return total


def split_rows(terms, parts):
    rows = terms[0].shape[0] // parts
    return [[term[i * rows : (i + 1) * rows] for term in terms] for i in range(parts)]


class Scatter:
    def __init__(self, arrays, orders):
        self.arrays = arrays
        self.fresh = []
        self.stages = list(zip(*[order[::-1] for order in orders]))
        self.widths = [terms[0].shape[1] for terms in arrays]

    def take_in(self, others):
        fresh = hold(self.fresh, others if self.fresh else ())
        if self.joined:
            cut = self.widths[0]
            fresh = [[array[:, :cut] for array in fresh], [array[:, cut:] for array in fresh]]
        else:
            fresh = [fresh[i * self.count : (i + 1) * self.count] for i in range(len(self.arrays))]
        self.arrays = [terms + more for terms, more in zip(self.arrays, fresh)]
        self.fresh = []

    def load(self, *others):
        if self.fresh:
            self.take_in(others)
        elif others:
            self.arrays = [hold(terms, others) for terms in self.arrays]
        self.now = self.stages.pop(0)
        self.joined = len(self.now) == 2 and self.now[0] == self.now[1]
        self.count = len(self.now[0])
        self.chunks = [split_rows(terms, len(stage) + 1) for terms, stage in zip(self.arrays, self.now)]
        sends = [[add_up(chunk).astype(bf16) for chunk in chunks[1:]] for chunks in self.chunks]
        if self.joined:
            self.sends = [jnp.concatenate(pair, axis=1) for pair in zip(*sends)]
        else:
            self.sends = sum(sends, [])
        return self.sends

    def move(self):
        moves = self.now[0] if self.joined else sum(self.now, [])
        self.arrays = [chunks[0] for chunks in self.chunks]
        self.fresh = [swap(send, axis, mask) for (axis, mask, _), send in zip(moves, self.sends)]

    def step(self, *others):
        if not self.stages:
            return list(others)
        sends = self.load(*others)
        self.move()
        return sends

    def finish(self, *others):
        while self.stages:
            self.step(*others)
        self.take_in(others)
        return jnp.concatenate([add_up(terms) for terms in self.arrays], axis=1)


def natural_pieces(stack, rels, chip, fast):
    if fast:
        per = len(rels) // len(stack)
        return stack, [rels[i * per : (i + 1) * per] for i in range(len(stack))]
    whole = jnp.concatenate(stack, axis=0)
    count = len(rels)
    where = np.zeros(count, np.int32)
    for slot, rel in enumerate(rels):
        where[rel] = slot
    order = jnp.asarray(where)[chip ^ jnp.arange(count, dtype=jnp.int32)]
    whole = whole.reshape(count, whole.shape[0] // count, whole.shape[1])
    whole = jnp.take(whole, order, axis=0).reshape(-1, whole.shape[2])
    return [whole], [list(range(BLOCKS))]


def natural_halves(stacks, tables, chip, fast):
    if fast:
        done = [natural_pieces(stack, rels, chip, fast) for stack, rels in zip(stacks, tables)]
        return done[0][0] + done[1][0], done[0][1] + done[1][1]
    return natural_pieces(stacks[0] + stacks[1], tables[0] + tables[1], chip, fast)


def in_slots(whole, rels, chip, fast):
    if fast:
        return whole
    count = len(rels)
    whole = whole.reshape(count, whole.shape[0] // count, whole.shape[1])
    order = jnp.asarray(np.array(rels, np.int32)) ^ chip
    return jnp.take(whole, order, axis=0).reshape(-1, whole.shape[2])


def by_core(core, mine, other, axis):
    return jnp.where(
        core == 0,
        jnp.concatenate([mine, other], axis=axis),
        jnp.concatenate([other, mine], axis=axis),
    )


def pair_block(core, halves):
    mine = jnp.where(core == 0, halves[0], halves[1])
    send = jnp.where(core == 0, halves[1], halves[0])
    return by_core(core, mine, swap_core(send), 0)


def dot(left, right):
    return lax.dot_general(left, right, (((1,), (0,)), ((), ())), preferred_element_type=f32)


def dot_nt(left, right):
    return lax.dot_general(left, right, (((1,), (1,)), ((), ())), preferred_element_type=f32)


def run_copies(copies, sems):
    started = []
    for at, (source, target) in enumerate(copies):
        copy = pltpu.make_async_copy(source, target, sems.at[at])
        copy.start()
        started.append(copy)
    return started


def wait_all(started):
    for copy in started:
        copy.wait()


def slots_of(pieces, rels):
    return [(piece, at, rel) for piece, table in zip(pieces, rels) for at, rel in enumerate(table)]


def block_rows(index, size):
    return pl.ds(pl.multiple_of(index * size, size), size)


def pos_block(index):
    quarter, within = index // (BLOCKS // 4), index % (BLOCKS // 4)
    return ((quarter % 2) * 2 + quarter // 2) * (BLOCKS // 4) + within


def core_lanes(core, width):
    return pl.ds(pl.multiple_of(core * width, LANES), width)


def head_mask(shape, dim, which, head_dim, kind):
    place = lax.broadcasted_iota(jnp.int32, shape, dim)
    return ((place // head_dim) == which).astype(f32).astype(kind)


def attend_pairs(pairs, scale, head_dim, tables, bias, query, key, value, w_pos, probs, ctx_own, ctx_par, lhs, rhs):
    sin, cos, sin_t, cos_t, feats, feats_t = tables
    width = feats.shape[1]
    half = width // 2
    row_len = bias.shape[1]
    lhs[:, width : 2 * width] = feats[...]
    rhs[0:width, :] = feats_t[...]

    def one_pair(pair, carry):
        lanes = pl.ds(pl.multiple_of(pair * LANES, LANES), LANES)
        q_pair, k_pair, v_pair, w_pair = query[:, lanes], key[:, lanes], value[:, lanes], w_pos[:, lanes]
        rhs[2 * width : 2 * width + LANES, :] = k_pair.T
        mixed = [None, None]
        for which in (0, 1):
            lane_mask = head_mask((1, LANES), 1, which, head_dim, bf16)
            q_head = q_pair * lane_mask
            k_head = k_pair * lane_mask
            lhs[:, 2 * width :] = q_head
            for row in (0, 1):
                span = slice(row * row_len, (row + 1) * row_len)
                coeff = dot_nt(q_head[span], w_pair)
                along_sin, along_cos = coeff[:, :half], coeff[:, half:]
                sin_row, cos_row = sin[span, :], cos[span, :]
                lhs[span, 0:half] = (along_cos * sin_row - along_sin * cos_row).astype(bf16)
                lhs[span, half:width] = (along_sin * sin_row + along_cos * cos_row).astype(bf16)
                coeff = dot_nt(w_pair, k_head[span])
                along_sin, along_cos = coeff[:half], coeff[half:]
                sin_row, cos_row = sin_t[:, span], cos_t[:, span]
                rhs[width : width + half, span] = (along_cos * sin_row - along_sin * cos_row).astype(bf16)
                rhs[width + half : 2 * width, span] = (along_sin * sin_row + along_cos * cos_row).astype(bf16)
            for row in (0, 1):
                span = slice(row * row_len, (row + 1) * row_len)
                scores = dot(lhs[span, :], rhs[:, span]) * scale + bias[row]
                top = jnp.max(scores, axis=-1, keepdims=True)
                expo = jnp.exp(scores - top)
                prob = expo / jnp.sum(expo, axis=-1, keepdims=True)
                probs[pair - pairs[0], which * 2 + row] = prob
                piece = dot(prob.astype(bf16), v_pair[span] * lane_mask)
                mixed[row] = piece if mixed[row] is None else mixed[row] + piece
        ctx_own[:, lanes] = mixed[0].astype(bf16)
        ctx_par[:, lanes] = mixed[1].astype(bf16)
        return carry

    if pairs[1] - pairs[0] == 1:
        one_pair(pairs[0], 0)
    else:
        lax.fori_loop(pairs[0], pairs[1], one_pair, 0)


def project_kernel(rels, meta, own, par, *refs):
    pieces, (w_qk, w_v, w_pos, query, key, value, sems) = refs[: len(rels)], refs[len(rels) :]
    chip = meta[0]
    row_len, width = own.shape
    part = w_v.shape[1]
    rows = width // BLOCKS
    copies = []
    for piece, at, rel in slots_of(pieces, rels):
        source = piece.at[pl.ds(at * rows, rows), :]
        copies.append((source.at[:, pl.ds(0, 2 * part)], w_qk.at[block_rows(chip ^ rel, rows), :]))
        copies.append((source.at[:, pl.ds(2 * part, part)], w_v.at[block_rows(chip ^ rel, rows), :]))
        copies.append((source.at[:, pl.ds(3 * part, part)], w_pos.at[block_rows(pos_block(chip ^ rel), rows), :]))
    wait_all(run_copies(copies, sems))
    for row, tokens in enumerate((own, par)):
        span = slice(row * row_len, (row + 1) * row_len)
        query[span, :] = dot(tokens[...], w_qk[:, 0:part]).astype(bf16)
        key[span, :] = dot(tokens[...], w_qk[:, part:]).astype(bf16)
        value[span, :] = dot(tokens[...], w_v[...]).astype(bf16)


def attend_kernel(pairs, scale, head_dim, *refs):
    tables, bias, (query, key, value, w_pos), refs = refs[:6], refs[6], refs[7:11], refs[11:]
    before = pairs[0] * LANES
    if before:
        own_before, par_before = refs[:2]
        refs = refs[2:]
    probs, ctx_own, ctx_par, lhs, rhs = refs
    if before:
        ctx_own[:, 0:before] = own_before[:, 0:before]
        ctx_par[:, 0:before] = par_before[:, 0:before]
    attend_pairs(pairs, scale, head_dim, tables, bias, query, key, value, w_pos, probs, ctx_own, ctx_par, lhs, rhs)


def take_lists(refs, sizes):
    taken = []
    for size in sizes:
        taken.append(refs[:size])
        refs = refs[size:]
    return taken, refs


def vmem_spec():
    return pl.BlockSpec(memory_space=pltpu.VMEM)


def any_spec():
    return pl.BlockSpec(memory_space=pltpu.HBM)


def smem_spec():
    return pl.BlockSpec(memory_space=pltpu.SMEM)


def params(limit=VMEM_LIMIT):
    return pltpu.CompilerParams(vmem_limit_bytes=limit)


def shape(dims, kind):
    return jax.ShapeDtypeStruct(dims, kind)


def cost(flops, moved, scale=COST_SCALE):
    return pl.CostEstimate(flops=int(flops * scale), bytes_accessed=int(moved * scale), transcendentals=0)


def project(meta, own, par, pieces, rels):
    row_len, width = own.shape
    part = width // 2
    tokens = 2 * row_len
    copies = 3 * sum(map(len, rels))
    return pl.pallas_call(
        partial(project_kernel, rels),
        out_shape=[
            shape((width, 2 * part), bf16),
            shape((width, part), bf16),
            shape((width, part), bf16),
            shape((tokens, part), bf16),
            shape((tokens, part), bf16),
            shape((tokens, part), bf16),
        ],
        in_specs=[smem_spec()] + [vmem_spec()] * 2 + [any_spec()] * len(pieces),
        out_specs=[vmem_spec()] * 6,
        scratch_shapes=[pltpu.SemaphoreType.DMA((copies,))],
        compiler_params=params(),
        cost_estimate=cost(2 * 0.5e9, 6e6, ATTEND_SCALE),
        name="project",
    )(meta, own, par, *pieces)


def attend(tables, bias, query, key, value, w_pos, before, pairs, scale, head_dim):
    tokens, part = query.shape
    width = 2 * part
    row_len = tokens // 2
    return pl.pallas_call(
        partial(attend_kernel, pairs, scale, head_dim),
        out_shape=[
            shape((pairs[1] - pairs[0], 4, row_len, row_len), f32),
            shape((row_len, part), bf16),
            shape((row_len, part), bf16),
        ],
        in_specs=[vmem_spec()] * (11 + len(before)),
        out_specs=[vmem_spec()] * 3,
        scratch_shapes=[
            pltpu.VMEM((tokens, 2 * width + LANES), bf16),
            pltpu.VMEM((2 * width + LANES, tokens), bf16),
        ],
        compiler_params=params(),
        cost_estimate=cost(2 * 1.0e9, 12e6, ATTEND_SCALE),
        name="attend",
    )(*tables, bias, query, key, value, w_pos, *before)


def norm_values(values):
    centered = values - jnp.mean(values, axis=-1, keepdims=True)
    inv_std = lax.rsqrt(jnp.mean(centered * centered, axis=-1, keepdims=True) + epsilon)
    return centered * inv_std, inv_std


def norm_backward(grad, normed_vals, inv_std, gain):
    grad_normed = grad * gain
    centered_grad = grad_normed - jnp.mean(grad_normed, axis=-1, keepdims=True)
    return inv_std * (
        centered_grad - normed_vals * jnp.mean(grad_normed * normed_vals, axis=-1, keepdims=True)
    )


def column_copies(pieces, rels, chip, rows, start, size, target, lanes):
    place = pl.ds(pl.multiple_of(lanes, LANES), size)
    return [
        (piece.at[pl.ds(at * rows, rows), pl.ds(start, size)], target.at[block_rows(chip ^ rel, rows), place])
        for piece, at, rel in slots_of(pieces, rels)
    ]


def middle_kernel(wide_rels, rels, out_rels, cuts, tile, meta, ctx_mine, ctx_recv, tokens, cotangent, *refs):
    wide, refs = take_lists(refs, [len(wide_rels)] * 2)
    pieces, refs = take_lists(refs, [len(rels[0]), len(rels[1])] * 2)
    output, grad_resid, normed_low, low, grad_ctx_mine, grad_ctx_send, grad_gains, sums = refs[:8]
    grad_pre_to, grad_mine, grad_other = refs[8:11]
    w_out, w_up, w_down, act, act_grad, act_t, ordered, low_two, grad_buf, grad_pre = refs[11:21]
    out_sems, up_sems, down_sems, flush_sems, row_sems, *row_bufs = refs[21:]
    row_inputs = (ctx_mine, ctx_recv, tokens, cotangent)
    started_rows = run_copies(list(zip(row_inputs, row_bufs)), row_sems)
    ctx_mine, ctx_recv, tokens, cotangent = row_bufs
    chip, core = meta[0], meta[1]
    ff, width = w_down.shape
    half = width // 2
    rows = ff // BLOCKS // 2
    ff_half, piece_rows, side_width = ff // 2, width // BLOCKS, half + LANES
    copies_out, groups = [], []
    for side, halves in ((core, wide[0]), (1 - core, wide[1])):
        for start, size in ((0, UP_CHUNK), (UP_CHUNK, ff_half - UP_CHUNK)):
            lanes = side * ff_half + start
            groups.append((column_copies(halves, wide_rels, chip, piece_rows, start, size, w_up, lanes), lanes, size))
        copies_out += column_copies(halves, wide_rels, chip, piece_rows, ff_half, side_width, w_out, side * side_width)
    started_out = run_copies(copies_out, out_sems)
    started_up, base = [], 0
    for copies, lanes, size in groups:
        started_up.append((run_copies(copies, up_sems.at[pl.ds(base, len(copies))]), lanes, size))
        base += len(copies)
    copies = []
    for side, chunks in ((core, pieces[:2]), (1 - core, pieces[2:])):
        for i in (0, 1):
            for piece, at, rel in slots_of(chunks[i], rels[i]):
                copies.append(
                    (
                        piece.at[pl.ds(at * rows, rows), :],
                        w_down.at[block_rows((chip ^ rel) * 2 + side, rows), pl.ds(i * half, half)],
                    )
                )
    started_down = run_copies(copies, down_sems)

    wait_all(started_rows)
    wait_all(started_out)
    lanes_of = [slice(side * side_width, side * side_width + half) for side in (0, 1)]
    attn_out = jnp.concatenate(
        [
            dot(ctx_mine[...], w_out[block_rows(core, half), lanes])
            + dot(ctx_recv[...], w_out[block_rows(1 - core, half), lanes])
            for lanes in lanes_of
        ],
        axis=1,
    )
    gains_one, gains_two = [
        w_out[:, side * side_width + half : (side + 1) * side_width].astype(f32).T[0:8] for side in (0, 1)
    ]
    tokens_f = tokens[...].astype(f32)
    resid = tokens_f + attn_out
    vals_one, inv_one = norm_values(resid)
    normed_one = vals_one * gains_one[0:1, :] + gains_one[1:2, :]
    normed_low[...] = normed_one.astype(bf16)
    sums[0:1, :] = jnp.sum(tokens_f * tokens_f, axis=0, keepdims=True)
    sums[1:2, :] = jnp.sum(attn_out * attn_out, axis=0, keepdims=True)
    sums[2:3, :] = jnp.sum(resid * resid, axis=0, keepdims=True)
    sums[3:8, :] = jnp.zeros((5, width), f32)

    for copies, start, size in started_up:
        wait_all(copies)
        for at in range(0, size, tile):
            lanes = pl.ds(pl.multiple_of(start + at, tile), tile)
            pre = dot(normed_low[...], w_up[:, lanes])
            bell = 0.5 * (1.0 + lax.erf(pre * (0.5**0.5)))
            low_act = (pre * bell).astype(bf16)
            act[:, lanes] = low_act
            act_t[lanes, :] = low_act.T
            act_grad[:, lanes] = bell + pre * jnp.exp(pre * pre * -0.5) * (0.5 / math.pi) ** 0.5
    wait_all(started_down)
    vals, inv = norm_values(normed_one + dot(act[...], w_down[...]))
    gain, shift = gains_two[0:1, :], gains_two[1:2, :]
    output[...] = (vals * gain + shift).astype(bf16)
    grad = cotangent[...].astype(f32)
    grad_gains[2:3, :] = jnp.sum(grad * vals, axis=0, keepdims=True)
    grad_gains[3:4, :] = jnp.sum(grad, axis=0, keepdims=True)
    grad_gains[4:8, :] = jnp.zeros((4, width), f32)
    grad_two = norm_backward(grad, vals, inv, gain)
    low_two[...] = grad_two.astype(bf16)
    flushed = []
    for target, place in ((grad_other, 1 - core), (grad_mine, core)):
        for start, stop, order in zip(cuts, cuts[1:], out_rels):
            for slot, rel in enumerate(order):
                ordered[slot * rows : (slot + 1) * rows, :] = act_t[block_rows((chip ^ rel) * 2 + place, rows), :]
            buf = grad_buf.at[len(flushed) // (len(cuts) - 1), :, pl.ds(start, stop - start)]
            buf[...] = dot(ordered[...], low_two[:, start:stop]).astype(bf16)
            copy = pltpu.make_async_copy(buf, target.at[:, pl.ds(start, stop - start)], flush_sems.at[len(flushed)])
            copy.start()
            flushed.append(copy)

    grad = grad_two
    for at in range(0, ff, BACK_TILE):
        lanes = pl.ds(at, BACK_TILE)
        piece = (dot_nt(low_two[...], w_down[lanes, :]) * act_grad[:, lanes]).astype(bf16)
        grad_pre[:, lanes] = piece
        copy = pltpu.make_async_copy(grad_pre.at[:, lanes], grad_pre_to.at[:, lanes], flush_sems.at[len(flushed)])
        copy.start()
        flushed.append(copy)
        grad = grad + dot_nt(piece, w_up[:, lanes])
    back = norm_backward(grad, vals_one, inv_one, gains_one[0:1, :])
    grad_resid[...] = back
    low[...] = back.astype(bf16)
    for target, side in ((grad_ctx_mine, core), (grad_ctx_send, 1 - core)):
        parts = [dot_nt(low[:, i * half : (i + 1) * half], w_out[block_rows(side, half), lanes_of[i]]) for i in (0, 1)]
        target[...] = (parts[0] + parts[1]).astype(bf16)
    grad_gains[0:1, :] = jnp.sum(grad * vals_one, axis=0, keepdims=True)
    grad_gains[1:2, :] = jnp.sum(grad, axis=0, keepdims=True)
    wait_all(flushed)


def middle(meta, ctx_mine, ctx_recv, tokens, cotangent, wide, wide_rels, pieces, rels, out_rels, cuts, ff):
    count, width = tokens.shape
    half = width // 2
    tile = 512
    flat = [array for chunk in wide + pieces for array in chunk]
    slots_wide = 2 * sum(map(len, wide_rels))
    return pl.pallas_call(
        partial(middle_kernel, wide_rels, rels, out_rels, cuts, tile),
        out_shape=[
            shape((count, width), bf16),
            shape((count, width), f32),
            shape((count, width), bf16),
            shape((count, width), bf16),
            shape((count, half), bf16),
            shape((count, half), bf16),
            shape((8, width), f32),
            shape((8, width), f32),
            shape((count, ff), bf16),
        ]
        + [shape((ff // 2, width), bf16)] * 2,
        in_specs=[smem_spec()] + [any_spec()] * (4 + len(flat)),
        out_specs=[vmem_spec()] * 8 + [any_spec()] * 3,
        scratch_shapes=[
            pltpu.VMEM((width, width + 2 * LANES), bf16),
            pltpu.VMEM((width, ff), bf16),
            pltpu.VMEM((ff, width), bf16),
            pltpu.VMEM((count, ff), bf16),
            pltpu.VMEM((count, ff), f32),
            pltpu.VMEM((ff, count), bf16),
            pltpu.VMEM((ff // 2, count), bf16),
            pltpu.VMEM((count, width), bf16),
            pltpu.VMEM((2, ff // 2, width), bf16),
            pltpu.VMEM((count, ff), bf16),
            pltpu.SemaphoreType.DMA((slots_wide,)),
            pltpu.SemaphoreType.DMA((2 * slots_wide,)),
            pltpu.SemaphoreType.DMA((2 * sum(map(len, rels[0] + rels[1])),)),
            pltpu.SemaphoreType.DMA((2 * (len(cuts) - 1) + ff // BACK_TILE,)),
            pltpu.SemaphoreType.DMA((4,)),
            pltpu.VMEM((count, half), bf16),
            pltpu.VMEM((count, half), bf16),
            pltpu.VMEM((count, width), bf16),
            pltpu.VMEM((count, width), bf16),
        ],
        compiler_params=params(60 * 1024 * 1024),
        cost_estimate=cost(2 * 3.2e9, 30e6),
        name="middle",
    )(meta, ctx_mine, ctx_recv, tokens, cotangent, *flat)


def permute_rows(source, target, chip, out_rels):
    rows = source.shape[0] // BLOCKS
    for slot, rel in enumerate(out_rels):
        target[slot * rows : (slot + 1) * rows, :] = source[block_rows(chip ^ rel, rows), :]


def digit_scales(devices):
    base = 1 << ((256 // devices + 1).bit_length() - 1)
    if base < 8:
        return None
    exponents = np.full((2 * LANES, 1), 126.0)
    for half in (0, 1):
        for row in range(2, LANES):
            exponents[half * LANES + row, 0] = 123 - 3 * ((row - 2) % 42 + 42 * half)
    return np.exp2(exponents).astype(np.float32)


def digits_of(sums, places):
    row = lax.broadcasted_iota(jnp.int32, (LANES, 1), 0)
    totals = [jnp.sum(sums[i : i + 1, :], axis=1, keepdims=True) for i in range(3)]
    value = jnp.where(row < 44, totals[0], jnp.where(row < 86, totals[1], totals[2]))
    whole = jnp.floor(jnp.minimum(value / places, 2.0**30))
    return whole - 8.0 * jnp.floor(whole * 0.125)


def weight_grads_kernel(
    out_rels, cuts, meta, all_gains, sums, places, normed_in, mine_in, recv_in, low_in, grad_pre_in, *refs
):
    targets, grads, refs = refs[:2], refs[2:4], refs[4:]
    grad_pre, turned, ordered_one, ordered_two, gain_buf, in_sems, flush_sems, row_sems, *row_bufs = refs
    row_loads = run_copies(list(zip((normed_in, mine_in, recv_in, low_in), row_bufs)), row_sems)
    normed_low, ctx_mine, ctx_recv, low = row_bufs
    chip, core = meta[0], meta[1]
    width, ff = turned.shape[0], grad_pre.shape[1]
    half, ff_half = width // 2, ff // 2
    rows = width // BLOCKS
    stops = [min(cut, ff_half) for cut in cuts]
    tiles = [
        (side, place * ff_half, start, stop - start, ordered)
        for side, place in ((1, 1 - core), (0, core))
        for start, stop, ordered in zip(stops, stops[1:], (ordered_one, ordered_two))
    ]
    places_of = [pl.ds(pl.multiple_of(base + start, LANES), size) for _, base, start, size, _ in tiles]
    loads = run_copies([(grad_pre_in.at[:, lanes], grad_pre.at[:, lanes]) for lanes in places_of], in_sems)
    flushed = []

    def flush(side, start, size):
        lanes = pl.ds(start, size)
        copy = pltpu.make_async_copy(grads[side].at[:, lanes], targets[side].at[:, lanes], flush_sems.at[len(flushed)])
        copy.start()
        flushed.append(copy)

    row_loads[0].wait()
    turned[...] = normed_low[...].T
    permute_rows(turned, ordered_one, chip, out_rels[0])
    permute_rows(turned, ordered_two, chip, out_rels[1])
    for load, lanes, (side, _, start, size, ordered) in zip(loads, places_of, tiles):
        load.wait()
        grads[side][:, start : start + size] = dot(ordered[...], grad_pre[:, lanes]).astype(bf16)
        flush(side, start, size)
    wait_all(row_loads[1:])
    turned[block_rows(core, half), :] = ctx_mine[...].T
    turned[block_rows(1 - core, half), :] = ctx_recv[...].T
    permute_rows(turned, ordered_two, chip, out_rels[-1])
    first, second = all_gains[0:2, :], all_gains[2:4, :]
    at_first = (core == 0).astype(f32)
    pair = (first * at_first + second * (1.0 - at_first), first * (1.0 - at_first) + second * at_first)
    for side, place in ((1, 1 - core), (0, core)):
        grad = grads[side]
        grad[:, ff_half : ff_half + half] = dot(ordered_two[...], low[:, core_lanes(place, half)]).astype(bf16)
        digits = digits_of(sums[...], places[block_rows(place, LANES), :])[2:]
        padded = jnp.concatenate([pair[side], jnp.broadcast_to(digits, (LANES - 2, width))], axis=0)
        gain_buf[...] = padded.T.astype(bf16)
        for slot, rel in enumerate(out_rels[-1]):
            grad[slot * rows : (slot + 1) * rows, ff_half + half :] = gain_buf[block_rows(chip ^ rel, rows), :]
        flush(side, ff_half, half + LANES)
    wait_all(flushed)


def weight_grads(meta, grad_pre, normed_low, low, all_gains, ctx_mine, ctx_recv, sums, places, out_rels, cuts):
    count, ff = grad_pre.shape
    width = normed_low.shape[1]
    out = (width, ff // 2 + width // 2 + LANES)
    return pl.pallas_call(
        partial(weight_grads_kernel, out_rels, cuts),
        out_shape=[shape(out, bf16)] * 2,
        in_specs=[smem_spec()] + [vmem_spec()] * 3 + [any_spec()] * 5,
        out_specs=[any_spec()] * 2,
        scratch_shapes=[pltpu.VMEM(out, bf16)] * 2
        + [pltpu.VMEM((count, ff), bf16)]
        + [pltpu.VMEM((width, count), bf16)] * 3
        + [
            pltpu.VMEM((width, LANES), bf16),
            pltpu.SemaphoreType.DMA((4,)),
            pltpu.SemaphoreType.DMA((6,)),
            pltpu.SemaphoreType.DMA((4,)),
            pltpu.VMEM((count, width), bf16),
            pltpu.VMEM((count, width // 2), bf16),
            pltpu.VMEM((count, width // 2), bf16),
            pltpu.VMEM((count, width), bf16),
        ],
        compiler_params=params(60 * 1024 * 1024),
        cost_estimate=cost(2 * 0.8e9, 10e6),
        name="weight_grads",
    )(meta, all_gains, sums, places, normed_low, ctx_mine, ctx_recv, low, grad_pre)


def attend_backward_kernel(
    out_rels, split, scale, head_dim, meta, own_t, par_t, sin, cos, sin_t, cos_t, feats, feats_t, query, key, value, w_pos, probs,
    grad_own, grad_par, grad_qkv, *refs
):
    outs, refs = (refs[:2], refs[2:]) if split else (refs[:1], refs[1:])
    grad_ctx, coeff_q, coeff_k, x2_rel, pos_buf = refs
    chip = meta[0]
    tokens, width = feats.shape
    row_len = tokens // 2
    half = width // 2
    grad_ctx[0:row_len, :] = grad_own[...]
    grad_ctx[row_len:, :] = grad_par[...]
    q_pair, k_pair, v_pair, w_pair, g_pair = query[...], key[...], value[...], w_pos[...], grad_ctx[...]
    q_t, v_t, g_t, w_t = q_pair.T, v_pair.T, g_pair.T, w_pair.T
    grad_q = [None, None]
    grad_k = [None, None]
    grad_v = [None, None]

    def plus(total, term):
        return term if total is None else total + term

    grad_q_coeff = None
    grad_k_coeff = None
    pos_q = None
    pos_k = None
    for which in (0, 1):
        lane_mask = head_mask((1, LANES), 1, which, head_dim, bf16)
        row_mask = head_mask((LANES, 1), 0, which, head_dim, bf16)
        k_head, g_head, w_head = k_pair * lane_mask, g_pair * lane_mask, w_pair * lane_mask
        q_t_head, g_t_head, w_t_head = q_t * row_mask, g_t * row_mask, w_t * row_mask
        for row in (0, 1):
            span = slice(row * row_len, (row + 1) * row_len)
            prob = probs[0, which * 2 + row]
            grad_probs = dot(g_head[span], v_t[:, span])
            inner = jnp.sum(prob * grad_probs, axis=-1, keepdims=True)
            grad_scores = (prob * (grad_probs - inner) * scale).astype(bf16)
            grad_v[row] = plus(grad_v[row], dot(g_t_head[:, span], prob.astype(bf16)))
            grad_k[row] = plus(grad_k[row], dot(q_t_head[:, span], grad_scores))
            grad_q[row] = plus(grad_q[row], dot(grad_scores, k_head[span]))
            pos = dot(grad_scores, feats[span, :])
            first, second = pos[:, :half], pos[:, half:]
            sin_row, cos_row = sin[span, :], cos[span, :]
            coeff_q[span, 0:half] = (second * sin_row - first * cos_row).astype(bf16)
            coeff_q[span, half:] = (first * sin_row + second * cos_row).astype(bf16)
            pos = dot(feats_t[:, span], grad_scores)
            first, second = pos[:half], pos[half:]
            sin_row, cos_row = sin_t[:, span], cos_t[:, span]
            coeff_k[0:half, span] = (second * sin_row - first * cos_row).astype(bf16)
            coeff_k[half:, span] = (first * sin_row + second * cos_row).astype(bf16)
        grad_q_coeff = plus(grad_q_coeff, dot(coeff_q[...], w_head))
        grad_k_coeff = plus(grad_k_coeff, dot(w_t_head, coeff_k[...]))
        pos_q = plus(pos_q, dot(q_t_head, coeff_q[...]))
        pos_k = plus(pos_k, dot(coeff_k[...], k_head))
    d_q = (jnp.concatenate(grad_q, axis=0) + grad_q_coeff).astype(bf16)
    d_k = (jnp.concatenate(grad_k, axis=1) + grad_k_coeff).astype(bf16).T
    d_v = jnp.concatenate(grad_v, axis=1).astype(bf16).T
    grad_qkv[:, 0:LANES] = d_q
    grad_qkv[:, LANES : 2 * LANES] = d_k
    grad_qkv[:, 2 * LANES :] = d_v
    pos_buf[...] = (pos_k + pos_q.T).astype(bf16)
    rows = width // BLOCKS
    cuts = (0, 2 * LANES, 3 * LANES) if split else (0, 3 * LANES)
    for at, out in enumerate(outs):
        size = cuts[at + 1] - cuts[at]
        permute_rows(own_t, x2_rel.at[:, 0:row_len], chip, out_rels[at])
        permute_rows(par_t, x2_rel.at[:, row_len:], chip, out_rels[at])
        out[:, 0:size] = dot(x2_rel[...], grad_qkv[:, cuts[at] : cuts[at + 1]]).astype(bf16)
    for slot, rel in enumerate(out_rels[-1]):
        outs[-1][slot * rows : (slot + 1) * rows, size:] = pos_buf[block_rows(pos_block(chip ^ rel), rows), :]


def attend_backward(
    meta, pair, own_t, par_t, tables, query, key, value, w_pos, probs, place, grad_own, grad_par, out_rels, scale, head_dim
):
    width, row_len = own_t.shape
    tokens = 2 * row_len

    def whole(array):
        return pl.BlockSpec(array.shape, lambda i: (0,) * array.ndim)

    def columns(rows):
        return pl.BlockSpec((rows, LANES), lambda i: (0, pair))

    split = len(out_rels) > 1
    pieces = [shape((width, (2 if split else 4) * LANES), bf16)] * (2 if split else 1)
    return pl.pallas_call(
        partial(attend_backward_kernel, out_rels, split, scale, head_dim),
        grid=(1,),
        out_shape=[shape((tokens, 3 * LANES), bf16)] + pieces,
        in_specs=[smem_spec(), whole(own_t), whole(par_t)]
        + [whole(table) for table in tables]
        + [columns(tokens)] * 3
        + [columns(width), pl.BlockSpec((1, 4, row_len, row_len), lambda i: (place, 0, 0, 0))]
        + [columns(row_len)] * 2,
        out_specs=[pl.BlockSpec((tokens, 3 * LANES), lambda i: (0, 0))]
        + [pl.BlockSpec(piece.shape, lambda i: (0, 0)) for piece in pieces],
        scratch_shapes=[
            pltpu.VMEM((tokens, LANES), bf16),
            pltpu.VMEM((tokens, width), bf16),
            pltpu.VMEM((width, tokens), bf16),
            pltpu.VMEM((width, tokens), bf16),
            pltpu.VMEM((width, LANES), bf16),
        ],
        compiler_params=params(),
        cost_estimate=cost(2 * 1.3e9, 10e6, BACK_SCALES[pair]),
        name="attend_backward",
    )(meta, own_t, par_t, *tables, query, key, value, w_pos, probs, grad_own, grad_par)


def row_tables(boxes):
    rates = jnp.exp(jnp.arange(FREQS, dtype=f32) * (-math.log(10000.0) / FREQS))
    angles = boxes.astype(f32)[:, :, None] * rates[None, None, :]
    angles = jnp.transpose(angles, (1, 0, 2)).reshape(boxes.shape[1], 2 * FREQS)
    sin, cos = jnp.sin(angles), jnp.cos(angles)
    feats = jnp.concatenate([sin, cos], axis=1).astype(bf16)
    return sin, cos, sin.T, cos.T, feats, feats.T


def body(
    tokens_in, boxes, page_lengths, cotangent, w_qkv, w_out, w_pos, gain_attn, bias_attn, w_up, w_down, gain_ffn, bias_ffn
):
    row_len, width = tokens_in.shape
    ff = w_up.shape[1]
    half, ff_half = width // 2, ff // 2
    head_dim = width // HEADS
    scale = head_dim ** (-0.5)
    dp, rep = lax.axis_size("dp"), lax.axis_size("rep")
    chips = dp * rep // 2
    core = lax.axis_index("rep") % 2
    chip = lax.axis_index("dp") * (rep // 2) + lax.axis_index("rep") // 2
    fast = chips == BLOCKS
    meta = jnp.stack([chip if fast else 0 * chip, core]).astype(jnp.int32)
    x, y, z_wide, z = tree_stages()
    heads_orders = (z_wide + x + y, z_wide + y + x)
    deep_orders = (x + z + y, y + z + x)
    orders = (z + x + y, z + y + x)
    heads_rels, deep_rels, all_rels = [
        [slot_chips(order) for order in pair] for pair in (heads_orders, deep_orders, orders)
    ]

    def split_columns(stack, cut, *others):
        stack = hold(stack, others)
        return [[columns_of(stack, 0, cut)], [columns_of(stack, cut, stack[0].shape[1])]]

    def move(stacks, stages, *others):
        moved = []
        for stack, stage in zip(stacks, stages):
            stack = stack[:1] + hold(stack[1:], others if len(stack) > 1 else ())
            whole = stack[0] if len(stack) == 1 else jnp.concatenate(stack, axis=0)
            moved.append([whole] + [swap(whole, axis, mask) for axis, mask, _ in stage])
        return moved

    half_xy = 2 * (rep // 2)

    def heads_z_halves(stack):
        count = len(stack) // 2
        return [[piece[0] if len(piece) == 1 else jnp.concatenate(piece, axis=0)] for piece in (stack[:count], stack[count:])]

    def sent(stacks):
        return [stack[0] for stack in stacks]

    def came(stacks):
        return [piece for stack in stacks for piece in stack[1:]]

    def joined(stacks):
        return jnp.concatenate([jnp.concatenate(stack, axis=0) for stack in stacks], axis=1)

    def heads_half(side):
        parts = [w_qkv[:, at * width + side * half : at * width + (side + 1) * half] for at in range(3)]
        return jnp.concatenate(parts + [w_pos[:, side * half : (side + 1) * half]], axis=1)

    heads_block = pair_block(core, [heads_half(s) for s in (0, 1)])
    heads_z = gather_first(heads_block, z_wide)
    tokens_late, boxes, page_lengths, w_up, w_out, w_down, gain_attn, bias_attn, gain_ffn, bias_ffn = hold(
        [tokens_in, boxes, page_lengths, w_up, w_out, w_down, gain_attn, bias_attn, gain_ffn, bias_ffn], [heads_block]
    )
    deep = move([[w_down[:, :half]], [w_down[:, half:]]], (x[0], y[0]))
    gain_sets = ((gain_attn, bias_attn), (gain_ffn, bias_ffn))
    pad = jnp.zeros((w_up.shape[0], LANES - 2), bf16)
    wide_block = pair_block(
        core,
        [
            jnp.concatenate(
                [
                    w_up[:, s * ff_half : (s + 1) * ff_half],
                    w_out[:, s * half : (s + 1) * half],
                    jnp.stack(gain_sets[s], axis=1),
                    pad,
                ],
                axis=1,
            )
            for s in (0, 1)
        ],
    )

    tokens_par = swap_core(tokens_late)
    ends = jnp.cumsum(page_lengths, axis=1)
    places = jnp.arange(row_len, dtype=jnp.int32)
    segment = jnp.sum((places[None, :, None] >= ends[:, None, :]).astype(jnp.int32), axis=2)
    marks = jnp.concatenate([boxes, segment], axis=0)
    marks_other = swap_core(marks)
    segments = jnp.stack([marks[2], marks_other[2]])
    bias = jnp.where(segments[:, :, None] == segments[:, None, :], 0.0, masked_value).astype(f32)
    tables = row_tables(jnp.concatenate([marks[:2], marks_other[:2]], axis=1))

    def thin(stack, stage):
        return stack + [swap(piece, axis, mask) for axis, mask, _ in stage for piece in stack]

    wide_rels = half_slots(
        [slot_chips(z)[: chips // (2 * half_xy)], slot_chips(z)[chips // (2 * half_xy) :]], (x + y, y + x)
    )
    firsts = slot_chips(z_wide)
    heads_rels_in = half_slots([firsts[: len(firsts) // 2], firsts[len(firsts) // 2 :]], (x + y, y + x))
    heads = move(heads_z_halves(heads_z), (x[0], y[0]))
    wide_z = [after(wide_block, *heads_z[1:])]
    for stage in z[:-1]:
        wide_z = thin(wide_z, stage)
    heads = move(heads, (y[0], x[0]), *wide_z[1:])
    wide_z = thin([jnp.concatenate(wide_z[:1] + hold(wide_z[1:], sent(heads)), axis=0)], z[-1])
    deep_z = [joined([stack[:1] + hold(stack[1:], [wide_z[0]]) for stack in deep])]
    for stage in z[:-1]:
        deep_z = thin(deep_z, stage)
    wide = move([wide_z[:1], hold(wide_z[1:], came(heads))], (x[0], y[0]))

    def tabled(stacks, rels):
        done = [natural_pieces(stack, table, chip, fast) for stack, table in zip(stacks, rels * 2)]
        return [pieces for pieces, _ in done], [table for _, table in done[:2]]

    heads, table_heads = natural_halves(heads, heads_rels_in, chip, fast)
    w_qk, w_v, w_pos_half, query, key, value = project(
        meta, after(tokens_in, *sent(wide)), tokens_par, heads, table_heads
    )
    wide = move(wide, (y[0], x[0]), query)
    deep_z = thin([jnp.concatenate(deep_z[:1] + hold(deep_z[1:], sent(wide)), axis=0)], z[-1])
    probs, ctx_mine, ctx_send = attend(
        tables, bias, after(query, deep_z[0]), key, value, w_pos_half, [], (0, half // LANES), scale, head_dim
    )
    ctx_recv = swap_core(ctx_send)
    wide = [stack[:1] + hold(stack[1:], [ctx_mine]) for stack in wide]
    deep = move(split_columns(deep_z[:1] + hold(deep_z[1:], [ctx_mine]), half), (y[0], x[0]))
    wide_other, _ = natural_halves([[swap_core(piece) for piece in stack] for stack in wide], wide_rels, chip, fast)
    wide, table_wide = natural_halves(wide, wide_rels, chip, fast)
    wide = [wide, wide_other]
    deep, table_deep = tabled(deep + [[swap_core(piece) for piece in stack] for stack in deep], deep_rels)
    if not fast:
        plain, deep = deep, [None] * 4
        for i in (0, 1):
            mine, other = [stack[0].reshape(chips, 1, -1, half) for stack in (plain[i], plain[2 + i])]
            cut = by_core(core, mine, other, 1).reshape(BLOCKS, 2, -1, half)
            deep[i] = [jnp.where(core == 0, cut[:, 0], cut[:, 1]).reshape(-1, half)]
            deep[2 + i] = [jnp.where(core == 0, cut[:, 1], cut[:, 0]).reshape(-1, half)]

    natural = list(range(BLOCKS))
    order_three = y + x + z
    rels_three = slot_chips(order_three)
    deep_cuts = (0, 256, 512, 768) if DEEP_THREE else (0, half, width)
    wide_cuts = (0, ff_half // 2, ff_half, ff_half + half + LANES) if WIDE_THREE else (0, UP_CHUNK, ff_half + half + LANES)
    sum_orders, sum_rels = orders + (order_three,), all_rels + [rels_three]
    pair_rels, out_rels = [tuple(rels) if fast else (natural,) * len(rels) for rels in (all_rels, sum_rels)]
    deep_out, wide_out = out_rels[: len(deep_cuts) - 1], out_rels[: len(wide_cuts) - 1]
    output, grad_resid_one, normed_low, grad_low, grad_ctx_mine, grad_ctx_send, all_gains, sums, grad_pre, deep_mine, deep_other = middle(
        meta, ctx_mine, ctx_recv, tokens_in, cotangent, wide, table_wide, deep, table_deep, deep_out, deep_cuts, ff
    )
    if not fast:
        mine, other = [grads.reshape(BLOCKS, 1, -1, width) for grads in (deep_mine, deep_other)]
        cut = by_core(core, mine, other, 1).reshape(chips, 2, -1, width)
        deep_mine = jnp.where(core == 0, cut[:, 0], cut[:, 1]).reshape(-1, width)
        deep_other = jnp.where(core == 0, cut[:, 1], cut[:, 0]).reshape(-1, width)

    def sums_of(terms, cuts):
        parts = [
            [in_slots(term[:, start:stop], rels, chip, fast) for term in terms]
            for start, stop, rels in zip(cuts, cuts[1:], sum_rels)
        ]
        third = Scatter(parts[2:], sum_orders[2:]) if len(parts) > 2 else None
        return Scatter(parts[:2], sum_orders[:2]), third

    def whole_sum(first, third, token):
        total = first.finish(*token)
        return total if third is None else jnp.concatenate([total, third.finish(*token)], axis=1)

    def more(scatter, token):
        return token if scatter is None else scatter.step(*token)

    places = digit_scales(dp * rep)
    deep_core = swap_core(deep_other)
    wide_mine, wide_other = weight_grads(
        meta, grad_pre, normed_low, grad_low, all_gains, ctx_mine, ctx_recv, sums,
        jnp.ones((2 * LANES, 1), f32) if places is None else jnp.asarray(places), wide_out, wide_cuts
    )
    grad_ctx_recv = swap_core(grad_ctx_send)
    s_deep, s_deep_z = sums_of([deep_mine, after(deep_core, wide_mine)], deep_cuts)
    token = s_deep.step() + more(s_deep_z, [])
    wide_core = swap_core(wide_other)
    own_t, par_t = tokens_in.T, tokens_par.T

    def back_pair(pair, rels, *others):
        return attend_backward(
            meta, pair, own_t, par_t, tables, query, key, value, w_pos_half, probs, pair, after(grad_ctx_mine, *others),
            grad_ctx_recv, rels, scale, head_dim
        )

    pair_grads = [None] * 3
    pair_grads[0], pair_zero = back_pair(0, pair_rels[:1], *token)
    s_wide, s_wide_z = sums_of([wide_mine, after(wide_core, pair_zero)], wide_cuts)
    token = s_wide.step() + more(s_wide_z, [])
    pair_grads[1], pair_one, pair_two = back_pair(1, pair_rels, *token)
    pair_grads[2], pair_three = back_pair(2, pair_rels[1:], pair_one)
    s_pair = Scatter(
        [
            [in_slots(jnp.concatenate(pieces, axis=1), rels, chip, fast)]
            for pieces, rels in zip(((pair_zero, pair_one), (pair_two, pair_three)), all_rels)
        ],
        orders,
    )
    token = s_deep.step(pair_three)
    token = more(s_deep_z, token)
    token = more(s_wide_z, token)
    token = s_wide.step(*token)
    token = s_pair.step(*token)
    grad_q, grad_k, grad_v = [
        jnp.concatenate([grads[:, i * LANES : (i + 1) * LANES] for grads in pair_grads], axis=1) for i in range(3)
    ]
    grad_x2 = dot_nt(after(jnp.concatenate([grad_q, grad_k], axis=1), *token), w_qk) + dot_nt(grad_v, w_v)
    grad_tokens = grad_resid_one + grad_x2[:row_len] + swap_core(grad_x2[row_len:])
    token = s_deep.step(*token)
    token = more(s_deep_z, token)
    token = s_wide.step(*token)
    token = more(s_wide_z, token)
    token = s_deep.step(*token)
    token = s_pair.step(*token)
    token = more(s_deep_z, token)
    token = s_wide.step(*token)
    token = s_pair.step(*token)
    deep_sum = whole_sum(s_deep, s_deep_z, token)
    wide_sum = whole_sum(s_wide, s_wide_z, token)
    pair_sum = s_pair.finish()

    def own_rows(values):
        rows = values.shape[0] // 2
        mine = jnp.where(core == 0, values[:rows], values[rows:])
        send = jnp.where(core == 0, values[rows:], values[:rows])
        return mine, swap_core(send)

    def sides(pieces, start, size):
        return by_core(core, pieces[0][:, start : start + size], pieces[1][:, start : start + size], 1)

    wide_rows = own_rows(wide_sum)
    pair_rows = own_rows(pair_sum)

    starts = [[0, 1, 2, 3], [4, 5, 6, 7], [8, 9, 10, 11]]

    def pair_columns(which):
        picked = [
            jnp.concatenate([rows[:, at[which] * LANES : (at[which] + 1) * LANES] for at in starts], axis=1)
            for rows in pair_rows
        ]
        return by_core(core, picked[0], picked[1], 1)

    gain_rows = sides(wide_rows, ff_half + half, LANES)
    if places is None:
        totals = after(jnp.sum(sums[:3], axis=1), pair_sum)
        for axis, size in (("rep", rep), ("dp", dp)):
            for bit in range(size.bit_length() - 1):
                totals = totals + swap(totals, axis, 1 << bit)
    else:
        parts = gain_rows[0].reshape(2, LANES) * jnp.asarray(places).reshape(2, LANES)
        totals = jnp.sum(jnp.transpose(parts[:, 2:].reshape(2, 3, 42), (1, 0, 2)).reshape(3, 84), axis=1)
    rms = jnp.sqrt(totals / (row_len * width * dp * rep))
    return (
        output,
        grad_tokens,
        rms,
        jnp.concatenate([pair_columns(0), pair_columns(1), pair_columns(2)], axis=1),
        sides(wide_rows, ff_half, half),
        pair_columns(3),
        gain_rows[:, 0],
        gain_rows[:, 1],
        sides(wide_rows, 0, ff_half),
        deep_sum,
        gain_rows[:, LANES],
        gain_rows[:, LANES + 1],
    )


def solution(mesh):
    rows = P(("dp", "rep"), None)
    line = P(("dp", "rep"))
    in_specs = (rows, P(None, ("dp", "rep")), rows, rows, rows, rows, rows, line, line, rows, rows, line, line)
    out_specs = (rows, rows, P(), rows, rows, rows, line, line, rows, rows, line, line)
    return jax.shard_map(body, mesh=mesh, in_specs=in_specs, out_specs=out_specs, check_vma=False)
```
